32 devices in a mesh: grp: 4 (over x, core), seq: 8 (over z, y).
Axes of the slice: x: 2, y: 2, z: 4, core: 2. Of those that a mesh axis runs over, the one named last changes fastest.
Arguments:
- tokens: bfloat16 [4096, 2048], P(('grp', 'seq')), may hold values from -6 to 6
- doc_lengths: int32 [4, 8], P('grp'), may hold values from 1 to 897, 1024 in all within a row
- cotangent: bfloat16 [4096, 2048], P(('grp', 'seq')), may hold values from -6 to 6
- attn_gain: bfloat16 [2048], P(('grp', 'seq')), may hold values from 0.5 to 1.5
- query_weight: bfloat16 [2048, 1024], P(('grp', 'seq')), may hold values from -0.125 to 0.125
- key_weight: bfloat16 [2048, 1024], P(('grp', 'seq')), may hold values from -0.125 to 0.125
- value_weight: bfloat16 [2048, 2048], P(('grp', 'seq')), may hold values from -0.125 to 0.125
- gate_weight: bfloat16 [2048, 2048], P(('grp', 'seq')), may hold values from -0.125 to 0.125
- rank_in: bfloat16 [2048, 16], P(('grp', 'seq')), may hold values from -0.125 to 0.125
- rank_out: bfloat16 [1024, 16], P(('grp', 'seq')), may hold values from -3 to 3
- decay_bias: bfloat16 [1024], P(('grp', 'seq')), may hold values from -1 to 12, as said below
- head_gain: bfloat16 [512], P(('grp', 'seq')), may hold values from 0.5 to 1.5
- out_weight: bfloat16 [2048, 2048], P(('grp', 'seq')), may hold values from -0.25 to 0.25
- mlp_gain: bfloat16 [2048], P(('grp', 'seq')), may hold values from 0.5 to 1.5
- mlp_gate_weight: bfloat16 [2048, 5632], P(('grp', 'seq')), may hold values from -0.125 to 0.125
- mlp_up_weight: bfloat16 [2048, 5632], P(('grp', 'seq')), may hold values from -0.125 to 0.125
- down_weight: bfloat16 [2048, 5632], P(('grp', 'seq')), may hold values from -0.109375 to 0.109375
Outputs:
- layer_out: float32 [4096, 2048], P(('grp', 'seq'))
- tokens_grad: float32 [4096, 2048], P(('grp', 'seq'))
- attn_gain_grad: float32 [2048], P(('grp', 'seq'))
- query_grad: float32 [2048, 1024], P(('grp', 'seq'))
- key_grad: float32 [2048, 1024], P(('grp', 'seq'))
- value_grad: float32 [2048, 2048], P(('grp', 'seq'))
- gate_grad: float32 [2048, 2048], P(('grp', 'seq'))
- rank_in_grad: float32 [2048, 16], P(('grp', 'seq'))
- rank_out_grad: float32 [1024, 16], P(('grp', 'seq'))
- decay_bias_grad: float32 [1024], P(('grp', 'seq'))
- head_gain_grad: float32 [512], P(('grp', 'seq'))
- out_weight_grad: float32 [2048, 2048], P(('grp', 'seq'))
- mlp_gain_grad: float32 [2048], P(('grp', 'seq'))
- mlp_gate_grad: float32 [2048, 5632], P(('grp', 'seq'))
- mlp_up_grad: float32 [2048, 5632], P(('grp', 'seq'))
- down_grad: float32 [2048, 5632], P(('grp', 'seq'))
The draws below stay inside these ranges and needn't reach their ends.
Inputs may be any that keep to these rules, and one draw needn't show every extreme that they name: `doc_lengths`: row s lists the lengths of the 8 documents packed, in order, into sequence s; they sum to 1024, and one of them is 897. `decay_bias`: one bias a key channel.
All inputs are finite; a program needn't handle non-finite values.
Results may differ from the reference program's by a relative error of at most 0.035.
Values may be sent and summed in bfloat16 or wider, within the bound.
A program may use at most 576 MiB of HBM per device.

```python
import math
from functools import partial
import jax
import jax.numpy as jnp
import numpy as np
from jax import lax

D = 2048
H = 4
DK = 256
DV = 512
R = 16
FF = 5632
CH = 64
DOCS = 8
TOK_DEV = 128
LEN = 1024
SEQS = 4
TOKENS = 4096


def draw_decay_bias(key, part):
    key = jax.random.fold_in(key, 7)
    return jax.random.uniform(key, (H * DK,), jnp.float32, -1.0, 12.0).astype(jnp.bfloat16)


def raised(array, own_key, source, target, blocks, factor):
    def block_of(dim):
        return (jnp.arange(array.shape[dim]) // (array.shape[dim] // blocks)).reshape((-1,) + (1,) * (array.ndim - 1 - dim))

    near = jax.random.permutation(own_key, blocks)[block_of(target)]
    second = (block_of(target) + blocks // 2) % blocks
    return jnp.where((block_of(source) == near) | (block_of(source) == second), factor * array, array)


def shard_levels(rng, shape, shards, smallest, top_value):
    factor_of = 1.0
    for position, blocks in shards:
        heights = jax.random.uniform(jax.random.fold_in(jax.random.fold_in(rng, 6), position), (blocks,), jnp.float32, smallest / len(shards), top_value / len(shards))
        factor_of = factor_of * jnp.repeat(jnp.exp(heights), shape[position] // blocks).reshape((-1,) + (1,) * (len(shape) - 1 - position))
    return factor_of


def split_up(amount, total, bound, lean):
    weights = [(1 << 20) // math.isqrt(standing ** lean) + 1 for standing in range(2, amount + 1)]
    spare, counts = total - bound - (amount - 1), [1] * (amount - 1)
    while spare > 0:
        movable = [i for i in range(amount - 1) if counts[i] < bound]
        mass, budget = sum([weights[i] for i in movable]), spare
        for i in movable:
            more = min(bound - counts[i], max(1, budget * weights[i] // mass), spare)
            counts[i] = counts[i] + more
            spare = spare - more
    return np.array([bound] + counts)


def uneven_parts(key, amount, total, bound, skew):
    if amount == 2:
        one = jax.random.randint(key, (), max(1, total - bound), min(bound, total - 1) + 1)
        return jnp.stack([one, total - one])
    tallies = jnp.asarray(split_up(amount, total, bound, skew), jnp.int32)
    pairs = (amount - 1) // 2
    source_of, taker = tallies[1:1 + 2 * pairs:2], tallies[2:2 + 2 * pairs:2]
    margin = jnp.minimum(source_of - 1, bound - taker)
    shifted = jax.random.randint(jax.random.fold_in(key, 1), (pairs,), 0, 1 << 20) % (margin + 1)
    tallies = tallies.at[1:1 + 2 * pairs:2].set(source_of - shifted).at[2:2 + 2 * pairs:2].set(taker + shifted)
    return tallies[jax.random.permutation(jax.random.fold_in(key, 2), amount)]


def scatter_about(own_key, extent, scale, bound, pieces=(), held_as=jnp.bfloat16):
    gain = shard_levels(own_key, extent, pieces, -0.22, 0.18) if pieces else 1.0
    drawn = jax.random.normal(own_key, extent, jnp.float32) * scale * gain
    return jnp.minimum(jnp.maximum(drawn, -bound), bound).astype(held_as)


def noise_with(key, dims, scale, bound, shards, heavy, held_as=jnp.bfloat16):
    drawn = scale * jax.random.normal(key, dims, jnp.float32)
    if shards:
        drawn = drawn * shard_levels(key, dims, shards, -0.22, 0.18)
    return jnp.clip(raised(drawn, jax.random.fold_in(key, 3), *heavy), -bound, bound).astype(held_as)


def setup_inputs(seed: int = 0) -> dict:
    key_list = jax.random.split(jax.random.key(seed), 18)
    return {
        "tokens": scatter_about(key_list[0], (TOKENS, D), 1.0, 6.0, ((0, 32),)),
        "doc_lengths": jax.vmap(lambda own: uneven_parts(own, DOCS, LEN, LEN - TOK_DEV + 1, 2))(jax.random.split(key_list[1], SEQS)).reshape((SEQS, DOCS)).astype(jnp.int32),
        "cotangent": noise_with(key_list[2], (TOKENS, D), 1.0, 6.0, ((0, 32),), (0, 1, 32, 2.75)),
        "attn_gain": jnp.clip(1.0 + 0.1 * jax.random.normal(key_list[3], (D,), jnp.float32), 0.5, 1.5).astype(jnp.bfloat16),
        "query_weight": scatter_about(key_list[4], (D, H * DK), D ** -0.5, 0.125, ((0, 32),)),
        "key_weight": scatter_about(key_list[5], (D, H * DK), D ** -0.5, 0.125, ((0, 32),)),
        "value_weight": scatter_about(key_list[6], (D, H * DV), D ** -0.5, 0.125, ((0, 32),)),
        "gate_weight": scatter_about(key_list[7], (D, H * DV), D ** -0.5, 0.125, ((0, 32),)),
        "rank_in": scatter_about(key_list[8], (D, R), D ** -0.5, 0.125, ((0, 32),)),
        "rank_out": scatter_about(key_list[9], (H * DK, R), (2.0 / R ** 0.5), 3.0, ((0, 32),)),
        "decay_bias": draw_decay_bias(jax.random.fold_in(key_list[17], 71), 0),
        "head_gain": jnp.clip(1.0 + 0.1 * jax.random.normal(key_list[11], (DV,), jnp.float32), 0.5, 1.5).astype(jnp.bfloat16),
        "out_weight": scatter_about(key_list[12], (D, H * DV), (H * DV // 4) ** -0.5, 0.25, ((0, 32),)),
        "mlp_gain": jnp.clip(1.0 + 0.1 * jax.random.normal(key_list[13], (D,), jnp.float32), 0.5, 1.5).astype(jnp.bfloat16),
        "mlp_gate_weight": scatter_about(key_list[14], (D, FF), D ** -0.5, 0.125, ((0, 32),)),
        "mlp_up_weight": scatter_about(key_list[15], (D, FF), D ** -0.5, 0.125, ((0, 32),)),
        "down_weight": scatter_about(key_list[16], (D, FF), (FF // 2) ** -0.5, 0.109375, ((0, 32),)),
    }


HIGHEST = lax.Precision.HIGHEST
norm_eps = 1e-06
head_eps = 0.25
decay_norm = 16.0

@jax.custom_vjp
def low(v):
    return lax.optimization_barrier(v.astype(jnp.bfloat16)).astype(jnp.float32)

@jax.custom_vjp
def low_back(v):
    return v

def low_keep(v):
    return (low(v), None)

def low_pass(kept, grad):
    return (grad,)

def back_keep(v):
    return (v, None)

def back_low(kept, grad):
    return (low(grad),)
low.defvjp(low_keep, low_pass)
low_back.defvjp(back_keep, back_low)

def exact_dot(left, right):
    return jnp.dot(left, right, precision=HIGHEST, preferred_element_type=jnp.float32)

def rms_scale(row_values):
    return row_values * lax.rsqrt(lax.optimization_barrier(jnp.mean(row_values * row_values, axis=-1, keepdims=True)) + norm_eps)

def head_gate(mixed_rows, out_gate, head_scale):
    normed = mixed_rows * lax.rsqrt(lax.optimization_barrier(jnp.mean(mixed_rows * mixed_rows, axis=-1, keepdims=True)) + head_eps) * head_scale
    return (normed * jax.nn.silu(out_gate.reshape(mixed_rows.shape))).reshape(out_gate.shape)

def block_step(carried, inputs):
    state_rows, segment_before = carried
    query_block, key_block, value_block, decay_block, segment_block = inputs
    positions = lax.iota(jnp.int32, query_block.shape[0])
    cumulative = jnp.cumsum(decay_block, axis=0)
    final_sum = cumulative[-1]
    query_scaled = query_block * query_block.shape[-1] ** (-0.5)
    query_decay = query_scaled * jnp.exp(cumulative)
    key_end = key_block * jnp.exp(final_sum[None] - cumulative)
    allowed_bool = (positions[:, None] >= positions[None, :]) & (segment_block[:, None] == segment_block[None, :])
    allowed = allowed_bool.astype(query_block.dtype)
    spread = cumulative[:, None] - cumulative[None, :]
    inside = allowed_bool[:, :, None, None]
    relative = jnp.where(inside, jnp.exp(jnp.where(inside, spread, 0.0)), 0.0)
    scores = jnp.einsum('thc,shc,tshc->hts', query_scaled, key_block, relative, precision=HIGHEST) * allowed[None]
    outputs = jnp.einsum('hts,shv->thv', scores, value_block, precision=HIGHEST)
    entry_rows = (segment_block == segment_before).astype(query_block.dtype)
    outputs = outputs + entry_rows[:, None, None] * jnp.einsum('thc,hcv->thv', query_decay, state_rows, precision=HIGHEST)
    seg_last = segment_block[-1]
    tail_mask = (segment_block == seg_last).astype(query_block.dtype)
    passes = (seg_last == segment_before).astype(query_block.dtype)
    state_rows = passes * jnp.exp(final_sum)[:, :, None] * state_rows + jnp.einsum('shc,shv->hcv', key_end * tail_mask[:, None, None], value_block, precision=HIGHEST)
    return ((state_rows, seg_last), outputs)

def mixer_sequence(packed):
    query_heads, key_heads, value_heads, decay_heads, segments = packed
    row_count = query_heads.shape[0]
    blocks = row_count // CH

    def to_blocks(array_rows):
        return array_rows.reshape((blocks, CH) + array_rows.shape[1:])
    initial = (jnp.zeros((H, DK, DV), jnp.float32), jnp.int32(-1))
    final_carry, outputs = lax.scan(jax.checkpoint(block_step), initial, (to_blocks(query_heads), to_blocks(key_heads), to_blocks(value_heads), to_blocks(decay_heads), to_blocks(segments)))
    return outputs.reshape(row_count, H, DV)

def layer_forward(segments, token_rows, attn_gain, query_weight, key_weight, value_weight, gate_weight, rank_in, rank_out, decay_bias, head_gain, out_weight, mlp_gain, mlp_gate_weight, mlp_up_weight, down_weight):
    row_count = token_rows.shape[0]
    normed_in = low(rms_scale(token_rows) * attn_gain)
    query_rows = low_back(low(exact_dot(normed_in, query_weight)))
    key_rows = low_back(low(exact_dot(normed_in, key_weight)))
    value_rows = low_back(low(exact_dot(normed_in, value_weight)))
    out_gate = low_back(exact_dot(normed_in, gate_weight))
    rank_low = low_back(low(exact_dot(normed_in, rank_in)))
    decay_logit = low_back(exact_dot(rank_low, rank_out.T) + decay_bias)
    log_decay = jax.nn.log_sigmoid(decay_logit) / decay_norm
    mixed_rows = lax.map(mixer_sequence, (query_rows.reshape(SEQS, LEN, H, DK), key_rows.reshape(SEQS, LEN, H, DK), value_rows.reshape(SEQS, LEN, H, DV), log_decay.reshape(SEQS, LEN, H, DK), segments))
    mixed_rows = mixed_rows.reshape(row_count, H, DV)
    gated_rows = low(head_gate(mixed_rows, out_gate, head_gain))
    residual = token_rows + low_back(exact_dot(gated_rows, out_weight.T))
    normed_mlp = low(rms_scale(residual) * mlp_gain)
    gate_pre = low_back(exact_dot(normed_mlp, mlp_gate_weight))
    up_pre = low_back(exact_dot(normed_mlp, mlp_up_weight))
    hidden = low(jax.nn.silu(gate_pre) * up_pre)
    return residual + low_back(exact_dot(hidden, down_weight.T))

def reference(tokens, doc_lengths, cotangent, attn_gain, query_weight, key_weight, value_weight, gate_weight, rank_in, rank_out, decay_bias, head_gain, out_weight, mlp_gain, mlp_gate_weight, mlp_up_weight, down_weight):
    doc_ends = jnp.cumsum(doc_lengths, axis=1).astype(jnp.int32)
    positions = lax.iota(jnp.int32, LEN)
    segments = lax.optimization_barrier(jnp.sum((doc_ends[:, None, :] <= positions[None, :, None]).astype(jnp.int32), axis=2)).astype(jnp.int32)
    weight_values = [piece.astype(jnp.float32) for piece in (attn_gain, query_weight, key_weight, value_weight, gate_weight, rank_in, rank_out, decay_bias, head_gain, out_weight, mlp_gain, mlp_gate_weight, mlp_up_weight, down_weight)]
    layer_out, pullback = jax.vjp(partial(layer_forward, segments), tokens.astype(jnp.float32), *weight_values)
    gradients = pullback(cotangent.astype(jnp.float32))
    return (layer_out, gradients[0], gradients[1], gradients[2], gradients[3], gradients[4], gradients[5], gradients[6], gradients[7], gradients[8], gradients[9], gradients[10], gradients[11], gradients[12], gradients[13], gradients[14])
```

```python
import functools

import jax
import jax.numpy as jnp
import numpy as np
from jax import lax
from jax.experimental import pallas as pl
from jax.experimental.pallas import tpu as pltpu
from jax.sharding import Mesh
from jax.sharding import PartitionSpec as P

H = 4
DK = 256
DV = 512
R = 16
CHUNK = 128
LEVELS = 7
SMALL = 128
WAIT_FLOPS = 30_000_000_000
norm_eps = 1e-06
head_eps = 0.25
decay_norm = 16.0
BF = jnp.bfloat16
F32 = jnp.float32
REST = ("x", "c", "y")
OWN = ("x", "c", "z", "y")


def dot_plain(left, right):
    return jnp.dot(left, right, preferred_element_type=F32)


def dot_rows(left, right):
    return lax.dot_general(left, right, (((1,), (1,)), ((), ())), preferred_element_type=F32)


def dot_cols(left, right):
    return lax.dot_general(left, right, (((0,), (0,)), ((), ())), preferred_element_type=F32)


def split_two(value):
    high = value.astype(BF)
    return jnp.concatenate([high, (value - high.astype(F32)).astype(BF)], axis=1)


def sum_two(value):
    half = value.shape[1] // 2
    return value[:, :half] + value[:, half:]


def chunk_tables():
    t = np.arange(CHUNK)[:, None]
    j = np.arange(CHUNK)[None, :]
    parts = []
    level = np.full((CHUNK, CHUNK), -1, np.int32)
    for number in range(LEVELS):
        half = CHUNK >> (number + 1)
        middle = t // (2 * half) * (2 * half) + half - 1
        upper = t % (2 * half) >= half
        parts.append(np.where(upper, (j > middle) & (j <= t), (j > t) & (j <= middle)))
        pair = (t // (2 * half) == j // (2 * half)) & upper & (j % (2 * half) < half)
        level[pair] = number
    level[np.arange(CHUNK), np.arange(CHUNK)] = LEVELS
    parts.append(j <= t)
    parts.append(j > t)
    return np.concatenate(parts, axis=0).astype(np.float32), level


def upper_rows(number):
    half = CHUNK >> (number + 1)
    rows = lax.broadcasted_iota(jnp.int32, (CHUNK, 1), 0)
    return lax.rem(rows, 2 * half) >= half


def factors(ld_ref, sums_ref):
    exponents = sum_two(dot_plain(sums_ref[...], split_two(ld_ref[...])))
    return jnp.exp(exponents)


def rows_of(value, number):
    return value[number * CHUNK : (number + 1) * CHUNK]


def mix_forward_body(
    q_ref, k_ref, v_ref, ld_ref, aux_ref, seg_ref, sums_ref, level_ref,
    out_ref, enter_ref, score_ref, state,
):
    @pl.when(pl.program_id(0) == 0)
    def _():
        state[...] = jnp.zeros_like(state)

    factor = factors(ld_ref, sums_ref)
    query = q_ref[...].astype(F32) * DK ** (-0.5)
    key = k_ref[...].astype(F32)
    level = level_ref[...]
    aux = aux_ref[...]
    scores = jnp.where(level == LEVELS, dot_rows(query.astype(BF), k_ref[...]), 0.0)
    for number in range(LEVELS):
        part = rows_of(factor, number)
        pairs = dot_rows((query * part).astype(BF), (key * part).astype(BF))
        scores = jnp.where(level == number, pairs, scores)
    scores = jnp.where(aux[:, 2:3] == seg_ref[0], scores, 0.0).astype(BF)
    score_ref[0] = scores
    cumulative = rows_of(factor, LEVELS)
    enter = state[...].astype(BF)
    enter_ref[0] = enter
    lifted = (query * cumulative * aux[:, 0:1]).astype(BF)
    ending = (key * rows_of(factor, LEVELS + 1) * aux[:, 1:2]).astype(BF)
    out = dot_plain(scores, v_ref[...]) + dot_rows(lifted, enter)
    out_ref[...] = out.astype(out_ref.dtype)
    through = cumulative[CHUNK - 1 :] * aux[0:1, 3:4]
    state[...] = state[...] * through + dot_cols(v_ref[...], ending)


def mix_backward_body(
    q_ref, k_ref, v_ref, ld_ref, aux_ref, seg_ref, sums_ref, sums_t_ref, level_ref, level_t_ref,
    enter_ref, score_ref, do_ref,
    dq_ref, dk_ref, dv_ref, dld_ref, state,
):
    @pl.when(pl.program_id(0) == 0)
    def _():
        state[...] = jnp.zeros_like(state)

    factor = factors(ld_ref, sums_ref)
    scale = DK ** (-0.5)
    query = q_ref[...].astype(F32) * scale
    key = k_ref[...].astype(F32)
    value = v_ref[...]
    grad = do_ref[...]
    level = level_ref[...]
    level_t = level_t_ref[...]
    aux = aux_ref[...]
    same = aux[:, 2:3] == seg_ref[0]
    weight = jnp.where(same, dot_rows(grad, value), 0.0)
    weight_t = jnp.where(same, dot_rows(value, grad), 0.0)
    diagonal = jnp.sum(jnp.where(level == LEVELS, weight, 0.0), axis=1, keepdims=True)
    dq = diagonal * key
    dk = diagonal * query
    moved = []
    for number in range(LEVELS):
        part = rows_of(factor, number)
        left = jnp.concatenate(
            [
                jnp.where(level == number, weight, 0.0).astype(BF),
                jnp.where(level_t == number, weight_t, 0.0).astype(BF),
            ],
            axis=1,
        )
        right = jnp.concatenate([(key * part).astype(BF), (query * part).astype(BF)], axis=0)
        both = dot_plain(left, right) * part
        upper = upper_rows(number)
        dq = dq + jnp.where(upper, both, 0.0)
        dk = dk + jnp.where(upper, 0.0, both)
        moved.append(both * jnp.where(upper, query, key))
    cumulative = rows_of(factor, LEVELS)
    enter = enter_ref[0]
    after = state[...]
    after_low = after.astype(BF)
    lift = cumulative * aux[:, 0:1]
    finish = rows_of(factor, LEVELS + 1) * aux[:, 1:2]
    lifted = query * lift
    ending = key * finish
    from_enter = dot_plain(grad, enter)
    from_after = dot_plain(value, after_low)
    moved.append(lifted * from_enter)
    moved.append(ending * from_after)
    dq_ref[...] = ((dq + lift * from_enter) * scale).astype(dq_ref.dtype)
    dk_ref[...] = (dk + finish * from_after).astype(dk_ref.dtype)
    dv = dot_cols(score_ref[0], grad) + dot_rows(ending.astype(BF), after_low)
    dv_ref[...] = dv.astype(dv_ref.dtype)
    through = cumulative[CHUNK - 1 :] * aux[0:1, 3:4]
    passing = jnp.sum(after * enter.astype(F32), axis=0, keepdims=True) * through
    spread = sum_two(dot_plain(sums_t_ref[...], split_two(jnp.concatenate(moved, axis=0))))
    dld_ref[...] = spread + passing
    state[...] = after * through + dot_cols(grad, lifted.astype(BF))


def mix_specs(count, width, backward):
    def at(i):
        return count - 1 - i if backward else i

    def tokens(columns):
        return pl.BlockSpec((CHUNK, columns), lambda i: (at(i), 0))

    def chunks(rows, columns):
        return pl.BlockSpec((1, rows, columns), lambda i: (at(i), 0, 0))

    def whole(rows, columns):
        return pl.BlockSpec((rows, columns), lambda i: (0, 0))

    return tokens, chunks, whole


def mix_forward(query, key, value, log_decay, aux, seg_rows):
    total, width = value.shape
    count = total // CHUNK
    sums, level = chunk_tables()
    tokens, chunks, whole = mix_specs(count, width, False)
    return pl.pallas_call(
        mix_forward_body,
        grid=(count,),
        in_specs=[
            tokens(DK), tokens(DK), tokens(width), tokens(DK), tokens(aux.shape[1]),
            chunks(1, CHUNK), whole(*sums.shape), whole(CHUNK, CHUNK),
        ],
        out_specs=[tokens(width), chunks(width, DK), chunks(CHUNK, CHUNK)],
        out_shape=[
            jax.ShapeDtypeStruct((total, width), BF),
            jax.ShapeDtypeStruct((count, width, DK), BF),
            jax.ShapeDtypeStruct((count, CHUNK, CHUNK), BF),
        ],
        scratch_shapes=[pltpu.VMEM((width, DK), F32)],
        compiler_params=pltpu.CompilerParams(
            dimension_semantics=("arbitrary",), vmem_limit_bytes=32 * 1024 * 1024
        ),
        cost_estimate=pl.CostEstimate(
            flops=total * 2 * (8 * CHUNK * DK + 2 * width * DK + CHUNK * width + 18 * CHUNK * DK),
            bytes_accessed=total * 4096, transcendentals=total * 9 * DK,
        ),
        name="mix_forward",
    )(query, key, value, log_decay, aux, seg_rows, jnp.asarray(sums, BF), jnp.asarray(level))


def mix_backward(query, key, value, log_decay, aux, seg_rows, enter, scores, grad):
    total, width = value.shape
    count = total // CHUNK
    sums, level = chunk_tables()
    tokens, chunks, whole = mix_specs(count, width, True)
    return pl.pallas_call(
        mix_backward_body,
        grid=(count,),
        in_specs=[
            tokens(DK), tokens(DK), tokens(width), tokens(DK), tokens(aux.shape[1]),
            chunks(1, CHUNK), whole(*sums.shape), whole(*sums.shape[::-1]),
            whole(CHUNK, CHUNK), whole(CHUNK, CHUNK),
            chunks(width, DK), chunks(CHUNK, CHUNK), tokens(width),
        ],
        out_specs=[tokens(DK), tokens(DK), tokens(width), tokens(DK)],
        out_shape=[
            jax.ShapeDtypeStruct((total, DK), BF),
            jax.ShapeDtypeStruct((total, DK), BF),
            jax.ShapeDtypeStruct((total, width), BF),
            jax.ShapeDtypeStruct((total, DK), F32),
        ],
        scratch_shapes=[pltpu.VMEM((width, DK), F32)],
        compiler_params=pltpu.CompilerParams(
            dimension_semantics=("arbitrary",), vmem_limit_bytes=48 * 1024 * 1024
        ),
        cost_estimate=pl.CostEstimate(
            flops=total * 2 * (14 * CHUNK * DK + 4 * width * DK + CHUNK * width + 36 * CHUNK * DK),
            bytes_accessed=total * 6144, transcendentals=total * 9 * DK,
        ),
        name="mix_backward",
    )(
        query, key, value, log_decay, aux, seg_rows, jnp.asarray(sums, BF),
        jnp.asarray(np.ascontiguousarray(sums.T), BF), jnp.asarray(level),
        jnp.asarray(np.ascontiguousarray(level.T)), enter, scores, grad,
    )


def remote(source, target, send, arrive, axis, place):
    return pltpu.make_async_remote_copy(
        src_ref=source, dst_ref=target, send_sem=send, recv_sem=arrive,
        device_id={axis: place}, device_id_type=pl.DeviceIdType.MESH,
    )


def greet_line(axis, count):
    me = lax.axis_index(axis)
    barrier = pltpu.get_barrier_semaphore()

    @pl.when(me > 0)
    def _():
        pl.semaphore_signal(
            barrier, inc=1, device_id={axis: me - 1}, device_id_type=pl.DeviceIdType.MESH
        )

    @pl.when(me < count - 1)
    def _():
        pl.semaphore_signal(
            barrier, inc=1, device_id={axis: me + 1}, device_id_type=pl.DeviceIdType.MESH
        )

    pl.semaphore_wait(barrier, jnp.where((me > 0) & (me < count - 1), 2, 1))


def gather_body(axis, count, x_ref, out_ref, send, arrive, local_sem):
    me = lax.axis_index(axis)
    own = x_ref.shape[0]
    greet_line(axis, count)

    def block(index):
        return out_ref.at[pl.ds(pl.multiple_of(index * own, own), own)]

    def hop(direction, step):
        index = me - step if direction == 0 else me + step
        source = x_ref if step == 0 else block(index)
        return remote(
            source, block(index), send.at[direction, step], arrive.at[direction, step],
            axis, me + 1 if direction == 0 else me - 1,
        )

    def landed(direction, step):
        index = me - 1 - step if direction == 0 else me + 1 + step
        return remote(
            block(index), block(index), send.at[direction, step], arrive.at[direction, step],
            axis, me + 1 if direction == 0 else me - 1,
        )

    mine = pltpu.make_async_copy(x_ref, block(me), local_sem)
    mine.start()
    for step in range(count):
        if step > 0:

            @pl.when(me - step >= 0)
            def _():
                landed(0, step - 1).wait_recv()

        if step < count - 1:

            @pl.when((me - step >= 0) & (me < count - 1))
            def _():
                hop(0, step).start()

        if step > 0:

            @pl.when(me + step <= count - 1)
            def _():
                landed(1, step - 1).wait_recv()

        if step < count - 1:

            @pl.when((me + step <= count - 1) & (me > 0))
            def _():
                hop(1, step).start()

    for step in range(count - 1):

        @pl.when((me - step >= 0) & (me < count - 1))
        def _():
            hop(0, step).wait_send()

        @pl.when((me + step <= count - 1) & (me > 0))
        def _():
            hop(1, step).wait_send()

    mine.wait()


def gather_line(block, axis, number):
    count = lax.axis_size(axis)
    rows, columns = block.shape
    return pl.pallas_call(
        functools.partial(gather_body, axis, count),
        in_specs=[pl.BlockSpec(memory_space=pl.ANY)],
        out_specs=pl.BlockSpec(memory_space=pl.ANY),
        out_shape=jax.ShapeDtypeStruct((count * rows, columns), block.dtype),
        scratch_shapes=[
            pltpu.SemaphoreType.DMA((2, count - 1)),
            pltpu.SemaphoreType.DMA((2, count - 1)),
            pltpu.SemaphoreType.DMA,
        ],
        compiler_params=pltpu.CompilerParams(collective_id=number, has_side_effects=True),
        cost_estimate=pl.CostEstimate(
            flops=WAIT_FLOPS, bytes_accessed=count * rows * columns * 4, transcendentals=0
        ),
        name="gather_line",
    )(block)


def scatter_body(axis, count, x_ref, out_ref, up, down, send, arrive):
    me = lax.axis_index(axis)
    own = out_ref.shape[0]
    greet_line(axis, count)

    def part(index):
        return x_ref.at[pl.ds(pl.multiple_of(index * own, own), own)]

    def hop(direction, number, source):
        held = (up, down)[direction].at[number]
        return remote(
            source, held, send.at[direction, number], arrive.at[direction, number],
            axis, me + 1 if direction == 0 else me - 1,
        )

    def stage(direction, number):
        target = count - 1 - number if direction == 0 else number
        first = me == 0 if direction == 0 else me == count - 1
        passed = me < target if direction == 0 else me > target
        held = (up, down)[direction].at[number]

        @pl.when(first)
        def _():
            hop(direction, number, part(target)).start()

        @pl.when(jnp.logical_not(first) & (passed | (me == target)))
        def _():
            hop(direction, number, held).wait_recv()

        @pl.when(jnp.logical_not(first) & passed)
        def _():
            held[...] = (held[...].astype(F32) + part(target)[...].astype(F32)).astype(BF)
            hop(direction, number, held).start()

    for order in (0, 1):

        @pl.when((me >= count // 2) == (order == 1))
        def _():
            for number in range(count - 1):
                stage(order, number)
                stage(1 - order, number)

    out_ref[...] = part(me)[...].astype(F32)
    for number in range(count - 1):

        @pl.when(me == count - 1 - number)
        def _():
            out_ref[...] += up[number].astype(F32)

        @pl.when(me == number)
        def _():
            out_ref[...] += down[number].astype(F32)

    for number in range(count - 1):

        @pl.when(me < count - 1 - number)
        def _():
            hop(0, number, up.at[number]).wait_send()

        @pl.when(me > number)
        def _():
            hop(1, number, down.at[number]).wait_send()


def scatter_line(partial, axis, number):
    count = lax.axis_size(axis)
    rows, columns = partial.shape
    own = rows // count
    return pl.pallas_call(
        functools.partial(scatter_body, axis, count),
        in_specs=[pl.BlockSpec(memory_space=pltpu.VMEM)],
        out_specs=pl.BlockSpec(memory_space=pltpu.VMEM),
        out_shape=jax.ShapeDtypeStruct((own, columns), F32),
        scratch_shapes=[
            pltpu.VMEM((count - 1, own, columns), BF),
            pltpu.VMEM((count - 1, own, columns), BF),
            pltpu.SemaphoreType.DMA((2, count - 1)),
            pltpu.SemaphoreType.DMA((2, count - 1)),
        ],
        compiler_params=pltpu.CompilerParams(
            collective_id=number, has_side_effects=True, vmem_limit_bytes=32 * 1024 * 1024
        ),
        cost_estimate=pl.CostEstimate(
            flops=WAIT_FLOPS, bytes_accessed=rows * columns * 4, transcendentals=0
        ),
        name="scatter_line",
    )(partial)


def swap_body(axis, count, x_ref, out_ref, send, arrive, local_sem):
    me = lax.axis_index(axis)
    barrier = pltpu.get_barrier_semaphore()
    for away in range(1, count):
        pl.semaphore_signal(
            barrier, inc=1, device_id={axis: lax.rem(me + away, count)},
            device_id_type=pl.DeviceIdType.MESH,
        )
    pl.semaphore_wait(barrier, count - 1)
    mine = pltpu.make_async_copy(x_ref.at[me], out_ref.at[me], local_sem)
    mine.start()

    def hop(away):
        peer = lax.rem(me + away, count)
        return remote(
            x_ref.at[peer], out_ref.at[me], send.at[away - 1], arrive.at[away - 1], axis, peer
        )

    def landed(away):
        peer = lax.rem(me + count - away, count)
        return remote(
            x_ref.at[peer], out_ref.at[peer], send.at[away - 1], arrive.at[away - 1], axis, peer
        )

    for away in range(1, count):
        hop(away).start()
    for away in range(1, count):
        landed(away).wait_recv()
    for away in range(1, count):
        hop(away).wait_send()
    mine.wait()


def swap_blocks(value, axis, number):
    count = lax.axis_size(axis)
    return pl.pallas_call(
        functools.partial(swap_body, axis, count),
        in_specs=[pl.BlockSpec(memory_space=pl.ANY)],
        out_specs=pl.BlockSpec(memory_space=pl.ANY),
        out_shape=jax.ShapeDtypeStruct(value.shape, value.dtype),
        scratch_shapes=[
            pltpu.SemaphoreType.DMA((count - 1,)),
            pltpu.SemaphoreType.DMA((count - 1,)),
            pltpu.SemaphoreType.DMA,
        ],
        compiler_params=pltpu.CompilerParams(collective_id=number, has_side_effects=True),
        cost_estimate=pl.CostEstimate(
            flops=WAIT_FLOPS // 2, bytes_accessed=value.size * 4, transcendentals=0
        ),
        name="swap_blocks",
    )(value)


def local(
    tokens, doc_lengths, cotangent, attn_gain, query_weight, key_weight, value_weight, gate_weight,
    rank_in, rank_out, decay_bias, head_gain, out_weight, mlp_gain, mlp_gate_weight,
    mlp_up_weight, down_weight,
):
    own, width = tokens.shape
    rows = query_weight.shape[0]
    X, C, Z, Y = (lax.axis_size(name) for name in OWN)
    z = lax.axis_index("z")
    group = own * Z
    total = group * Y
    ff = down_weight.shape[1] // Z
    dvp = DV // Y

    def blocked(value):
        lead = value.shape[:-1]
        cut = value.reshape(lead + (X, C, Z, Y, rows))
        return jnp.swapaxes(cut, -3, -2).reshape(lead + (width,))

    def unblocked(value):
        lead = value.shape[:-1]
        cut = value.reshape(lead + (X, C, Y, Z, rows))
        return jnp.swapaxes(cut, -3, -2).reshape(lead + (width,))

    def cut_columns(weight):
        return jnp.swapaxes(weight.reshape(rows, Z, weight.shape[1] // Z), 0, 1)

    def pad_rows(value):
        flat = value.reshape(value.shape[0], -1)
        return jnp.pad(flat, ((0, rows - flat.shape[0]), (0, 0)))

    numbers = iter(range(32))

    def swap_z(value):
        return swap_blocks(value, "z", next(numbers))

    def swap_y(value):
        return swap_blocks(value, "y", next(numbers))

    def gather_z(value):
        return gather_line(value, "z", next(numbers))

    def scatter_z(value):
        return scatter_line(value.astype(BF), "z", next(numbers))

    def to_sequence(value):
        cut = value.reshape(Y, Z, own, value.shape[-1])
        return jnp.swapaxes(cut, 0, 1).reshape(total, value.shape[-1])

    def from_sequence(value):
        cut = value.reshape(Z, Y, own, value.shape[-1])
        return jnp.swapaxes(cut, 0, 1).reshape(Y, group, value.shape[-1])

    def gather_rest(value):
        return lax.all_gather(value, REST, axis=0, tiled=True)

    small = jnp.concatenate(
        [
            rank_in, pad_rows(attn_gain), pad_rows(mlp_gain), pad_rows(rank_out),
            pad_rows(decay_bias), pad_rows(head_gain),
        ],
        axis=1,
    )
    small = jnp.pad(small, ((0, 0), (0, SMALL - small.shape[1])))
    first = jnp.concatenate(
        [cut_columns(w) for w in (query_weight, key_weight, value_weight, gate_weight)]
        + [jnp.broadcast_to(small[None], (Z,) + small.shape)],
        axis=2,
    )
    input_weights = gather_rest(swap_z(first).reshape(Z * rows, -1))
    second = swap_z(
        jnp.concatenate(
            [cut_columns(w) for w in (out_weight, mlp_gate_weight, mlp_up_weight, down_weight)],
            axis=2,
        )
    ).reshape(Z * rows, -1)
    out_piece = gather_rest(second[:, :DV])
    mlp_piece = gather_rest(second[:, DV : DV + 2 * ff])
    down_piece = gather_rest(second[:, DV + 2 * ff :])

    own_tokens = blocked(tokens)
    group_tokens = gather_z(own_tokens)
    group_cotangent = gather_z(blocked(cotangent))

    projected = 2 * DK + 2 * DV
    small_all = input_weights[:, projected:].astype(F32)

    def device_rows(value, count):
        cut = value.reshape(X, C, Y, Z, rows, -1)[:, :, :, :, : rows // count]
        return jnp.swapaxes(cut, 2, 3).reshape(width // count, -1)

    attn_gain_all = small_all[:, R]
    mlp_gain_all = small_all[:, R + 1]
    rank_out_all = device_rows(small_all[:, R + 2 : 2 * R + 2], width // (H * DK))
    bias_all = device_rows(small_all[:, 2 * R + 2 : 2 * R + 3], width // (H * DK))
    head_gain_all = device_rows(small_all[:, 2 * R + 3 : 2 * R + 4], width // DV)[:, 0]
    rank_out_z = lax.dynamic_slice_in_dim(rank_out_all, z * DK, DK).astype(BF)
    bias_z = lax.dynamic_slice_in_dim(bias_all, z * DK, DK)[:, 0]

    rows_in = group_tokens.astype(F32)
    scale_in = lax.rsqrt(jnp.mean(rows_in * rows_in, axis=1, keepdims=True) + norm_eps)
    normed_in = (rows_in * scale_in * attn_gain_all).astype(BF)
    heads = dot_plain(normed_in, input_weights)
    out_gate = heads[:, 2 * DK + DV : projected]
    low = heads.astype(BF)
    shared = jnp.concatenate([low[:, : 2 * DK], low[:, projected:]], axis=1)
    values = jnp.swapaxes(low[:, 2 * DK : 2 * DK + DV].reshape(group, Y, dvp), 0, 1)
    sent = jnp.concatenate([jnp.broadcast_to(shared[None], (Y,) + shared.shape), values], axis=2)
    sequence = to_sequence(swap_y(sent))
    queries = sequence[:, :DK]
    keys = sequence[:, DK : 2 * DK]
    rank_low = sequence[:, 2 * DK : 2 * DK + R]
    value_part = sequence[:, 2 * DK + SMALL :]
    decay_logit = dot_rows(rank_low, rank_out_z) + bias_z
    log_decay = jax.nn.log_sigmoid(decay_logit) / decay_norm

    doc_ends = jnp.cumsum(doc_lengths[0])
    positions = lax.iota(jnp.int32, total)
    segments = jnp.sum((doc_ends[None, :] <= positions[:, None]).astype(jnp.int32), axis=1)
    cut = segments.reshape(-1, CHUNK)
    last = cut[:, CHUNK - 1 :]
    before = jnp.concatenate([jnp.full((1, 1), -1, jnp.int32), last[:-1]], axis=0)
    aux = jnp.stack(
        [cut == before, cut == last, cut, jnp.broadcast_to(last == before, cut.shape)], axis=-1
    )
    aux = aux.reshape(total, 4).astype(F32)
    seg_rows = cut.astype(F32)[:, None, :]

    mixed_part, enter, scores = mix_forward(queries, keys, value_part, log_decay, aux, seg_rows)
    mixed = jnp.swapaxes(swap_y(from_sequence(mixed_part)), 0, 1).reshape(group, DV).astype(F32)

    head_scale = lax.rsqrt(jnp.mean(mixed * mixed, axis=1, keepdims=True) + head_eps)
    head_hat = mixed * head_scale
    head_out = head_hat * head_gain_all
    sig_out = jax.nn.sigmoid(out_gate)
    silu_out = out_gate * sig_out
    gated = (head_out * silu_out).astype(BF)
    residual = own_tokens.astype(F32) + scatter_z(dot_rows(gated, out_piece))
    scale_mid = lax.rsqrt(jnp.mean(residual * residual, axis=1, keepdims=True) + norm_eps)
    hat_mid = residual * scale_mid
    normed_mlp = gather_z((hat_mid * mlp_gain_all).astype(BF))

    both_pre = dot_plain(normed_mlp, mlp_piece)
    gate_pre = both_pre[:, :ff]
    up_pre = both_pre[:, ff:]
    sig_gate = jax.nn.sigmoid(gate_pre)
    silu_gate = gate_pre * sig_gate
    hidden = (silu_gate * up_pre).astype(BF)
    grad_hidden = dot_plain(group_cotangent, down_piece)
    grad_gate = (grad_hidden * up_pre * sig_gate * (1.0 + gate_pre * (1.0 - sig_gate))).astype(BF)
    grad_up = (grad_hidden * silu_gate).astype(BF)
    grad_both = jnp.concatenate([grad_gate, grad_up], axis=1)
    grad_normed_mlp = scatter_z(dot_rows(grad_both, mlp_piece))
    layer_out = residual + scatter_z(dot_rows(hidden, down_piece))

    mlp_sums = lax.psum_scatter(
        jnp.concatenate(
            [dot_cols(normed_mlp, grad_both), dot_cols(group_cotangent, hidden)], axis=1
        ).astype(BF),
        REST, scatter_dimension=0, tiled=True,
    )
    mlp_rows = swap_z(mlp_sums.reshape(Z, rows, 3 * ff)).astype(F32)

    mlp_gain_part = jnp.sum(grad_normed_mlp * hat_mid, axis=0)
    scaled = grad_normed_mlp * mlp_gain_all
    grad_residual = blocked(cotangent).astype(F32) + scale_mid * (
        scaled - hat_mid * jnp.mean(scaled * hat_mid, axis=1, keepdims=True)
    )
    grad_branch = gather_z(grad_residual.astype(BF))
    grad_gated = dot_plain(grad_branch, out_piece)
    grad_head = grad_gated * silu_out
    head_gain_part = jnp.sum(grad_head * head_hat, axis=0)
    from_head = grad_head * head_gain_all
    grad_mixed = head_scale * (
        from_head - head_hat * jnp.mean(from_head * head_hat, axis=1, keepdims=True)
    )
    grad_out_gate = (grad_gated * head_out * sig_out * (1.0 + out_gate * (1.0 - sig_out))).astype(BF)
    grad_part = to_sequence(
        swap_y(jnp.swapaxes(grad_mixed.astype(BF).reshape(group, Y, dvp), 0, 1))
    )
    dq, dk, dv, dld = mix_backward(
        queries, keys, value_part, log_decay, aux, seg_rows, enter, scores, grad_part
    )
    dlogit = (dld * jax.nn.sigmoid(-decay_logit) / decay_norm).astype(BF)
    back = swap_y(from_sequence(jnp.concatenate([dq, dk, dlogit, dv], axis=1)))
    summed = jnp.sum(back[:, :, : 3 * DK].astype(F32), axis=0).astype(BF)
    grad_value = jnp.swapaxes(back[:, :, 3 * DK :], 0, 1).reshape(group, DV)
    grad_logit = summed[:, 2 * DK :]
    bias_part = jnp.sum(grad_logit.astype(F32), axis=0)
    rank_low_group = low[:, projected : projected + R]
    rank_out_part = dot_cols(grad_logit, rank_low_group)
    grad_rank = dot_plain(grad_logit, rank_out_z).astype(BF)
    grad_heads = jnp.concatenate(
        [
            summed[:, : 2 * DK], grad_value, grad_out_gate,
            jnp.pad(grad_rank, ((0, 0), (0, SMALL - R))),
        ],
        axis=1,
    )
    grad_normed_in = scatter_z(dot_rows(grad_heads, input_weights))
    rows_own = own_tokens.astype(F32)
    scale_own = lax.rsqrt(jnp.mean(rows_own * rows_own, axis=1, keepdims=True) + norm_eps)
    hat_own = rows_own * scale_own
    attn_gain_part = jnp.sum(grad_normed_in * hat_own, axis=0)
    scaled_in = grad_normed_in * attn_gain_all
    tokens_grad = grad_residual + scale_own * (
        scaled_in - hat_own * jnp.mean(scaled_in * hat_own, axis=1, keepdims=True)
    )

    def to_device_rows(value, count):
        cut = value.reshape(X, C, Z, Y, rows // count, -1)
        cut = jnp.swapaxes(cut, 2, 3)
        cut = jnp.pad(cut, ((0, 0),) * 4 + ((0, rows - rows // count), (0, 0)))
        return cut.reshape(width, -1)

    def at_head(value):
        return lax.dynamic_update_slice_in_dim(
            jnp.zeros((H * DK, value.shape[1]), F32), value, z * DK, 0
        )

    weight_part = dot_cols(normed_in, grad_heads)
    small_part = jnp.concatenate(
        [
            weight_part[:, projected : projected + R],
            attn_gain_part[:, None],
            mlp_gain_part[:, None],
            to_device_rows(at_head(rank_out_part), width // (H * DK)),
            to_device_rows(at_head(bias_part[:, None]), width // (H * DK)),
            to_device_rows(head_gain_part[:, None], width // DV),
        ],
        axis=1,
    )
    small_part = jnp.pad(small_part, ((0, 0), (0, SMALL - small_part.shape[1])))
    attn_sums = lax.psum_scatter(
        jnp.concatenate(
            [weight_part[:, :projected], dot_cols(grad_branch, gated), small_part], axis=1
        ).astype(BF),
        REST, scatter_dimension=0, tiled=True,
    )
    attn_rows = swap_z(attn_sums.reshape(Z, rows, -1)).astype(F32)

    def joined(value):
        return jnp.swapaxes(value, 0, 1).reshape(rows, -1)

    small_rows = jnp.sum(attn_rows[:, :, projected + DV :], axis=0)
    return (
        unblocked(layer_out),
        unblocked(tokens_grad),
        small_rows[:, R],
        joined(attn_rows[:, :, :DK]),
        joined(attn_rows[:, :, DK : 2 * DK]),
        joined(attn_rows[:, :, 2 * DK : 2 * DK + DV]),
        joined(attn_rows[:, :, 2 * DK + DV : projected]),
        small_rows[:, :R],
        small_rows[: rows * H * DK // width, R + 2 : 2 * R + 2],
        small_rows[: rows * H * DK // width, 2 * R + 2],
        small_rows[: rows * DV // width, 2 * R + 3],
        joined(attn_rows[:, :, projected : projected + DV]),
        small_rows[:, R + 1],
        joined(mlp_rows[:, :, :ff]),
        joined(mlp_rows[:, :, ff : 2 * ff]),
        joined(mlp_rows[:, :, 2 * ff :]),
    )


def solution(mesh):
    groups, places = mesh.shape["grp"], mesh.shape["seq"]
    wide = Mesh(mesh.devices.reshape(groups // 2, 2, H, places // H), OWN)
    split = P(OWN, None)
    line = P(OWN)
    by_sequence = P(("x", "c"), None)
    placed = (
        split, by_sequence, split, line, split, split, split, split, split, split,
        line, line, split, line, split, split, split,
    )
    return jax.shard_map(
        local,
        mesh=wide,
        in_specs=placed,
        out_specs=(
            split, split, line, split, split, split, split, split, split, line, line, split,
            line, split, split, split,
        ),
        check_vma=False,
    )
```

```python
import functools

import jax
import jax.numpy as jnp
import numpy as np
from jax import lax
from jax.experimental import pallas as pl
from jax.experimental.pallas import tpu as pltpu
from jax.sharding import Mesh
from jax.sharding import PartitionSpec as P

H = 4
DK = 256
DV = 512
R = 16
CHUNK = 128
LEVELS = 7
SMALL = 128
WAIT_FLOPS = 100_000_000
PIECES = 2
norm_eps = 1e-06
head_eps = 0.25
decay_norm = 16.0
BF = jnp.bfloat16
F32 = jnp.float32
REST = ("x", "c", "y")
OWN = ("x", "c", "z", "y")


def dot_plain(left, right):
    return jnp.dot(left, right, preferred_element_type=F32)


def dot_rows(left, right):
    return lax.dot_general(left, right, (((1,), (1,)), ((), ())), preferred_element_type=F32)


def dot_cols(left, right):
    return lax.dot_general(left, right, (((0,), (0,)), ((), ())), preferred_element_type=F32)


def split_two(value):
    high = value.astype(BF)
    return jnp.concatenate([high, (value - high.astype(F32)).astype(BF)], axis=1)


def sum_two(value):
    half = value.shape[1] // 2
    return value[:, :half] + value[:, half:]


def chunk_tables():
    t = np.arange(CHUNK)[:, None]
    j = np.arange(CHUNK)[None, :]
    parts = []
    level = np.full((CHUNK, CHUNK), -1, np.int32)
    for number in range(LEVELS):
        half = CHUNK >> (number + 1)
        middle = t // (2 * half) * (2 * half) + half - 1
        upper = t % (2 * half) >= half
        parts.append(np.where(upper, (j > middle) & (j <= t), (j > t) & (j <= middle)))
        pair = (t // (2 * half) == j // (2 * half)) & upper & (j % (2 * half) < half)
        level[pair] = number
    level[np.arange(CHUNK), np.arange(CHUNK)] = LEVELS
    parts.append(j <= t)
    parts.append(j > t)
    return np.concatenate(parts, axis=0).astype(np.float32), level


def upper_rows(number):
    half = CHUNK >> (number + 1)
    rows = lax.broadcasted_iota(jnp.int32, (CHUNK, 1), 0)
    return lax.rem(rows, 2 * half) >= half


def factors(ld_ref, sums_ref):
    exponents = sum_two(dot_plain(sums_ref[...], split_two(ld_ref[...])))
    return jnp.exp(exponents)


def rows_of(value, number):
    return value[number * CHUNK : (number + 1) * CHUNK]


def mix_forward_body(
    q_ref, k_ref, v_ref, ld_ref, aux_ref, seg_ref, sums_ref, level_ref,
    out_ref, enter_ref, score_ref, state,
):
    @pl.when(pl.program_id(0) == 0)
    def _():
        state[...] = jnp.zeros_like(state)

    factor = factors(ld_ref, sums_ref)
    query = q_ref[...].astype(F32) * DK ** (-0.5)
    key = k_ref[...].astype(F32)
    level = level_ref[...]
    aux = aux_ref[...]
    scores = jnp.where(level == LEVELS, dot_rows(query.astype(BF), k_ref[...]), 0.0)
    for number in range(LEVELS):
        part = rows_of(factor, number)
        pairs = dot_rows((query * part).astype(BF), (key * part).astype(BF))
        scores = jnp.where(level == number, pairs, scores)
    scores = jnp.where(aux[:, 2:3] == seg_ref[0], scores, 0.0).astype(BF)
    score_ref[0] = scores
    cumulative = rows_of(factor, LEVELS)
    enter = state[...].astype(BF)
    enter_ref[0] = enter
    lifted = (query * cumulative * aux[:, 0:1]).astype(BF)
    ending = (key * rows_of(factor, LEVELS + 1) * aux[:, 1:2]).astype(BF)
    out = dot_plain(scores, v_ref[...]) + dot_rows(lifted, enter)
    out_ref[...] = out.astype(out_ref.dtype)
    through = cumulative[CHUNK - 1 :] * aux[0:1, 3:4]
    state[...] = state[...] * through + dot_cols(v_ref[...], ending)


def mix_backward_body(
    q_ref, k_ref, v_ref, ld_ref, aux_ref, seg_ref, sums_ref, sums_t_ref, level_ref, level_t_ref,
    enter_ref, score_ref, do_ref,
    dq_ref, dk_ref, dv_ref, dld_ref, state,
):
    @pl.when(pl.program_id(0) == 0)
    def _():
        state[...] = jnp.zeros_like(state)

    factor = factors(ld_ref, sums_ref)
    scale = DK ** (-0.5)
    query = q_ref[...].astype(F32) * scale
    key = k_ref[...].astype(F32)
    value = v_ref[...]
    grad = do_ref[...]
    level = level_ref[...]
    level_t = level_t_ref[...]
    aux = aux_ref[...]
    same = aux[:, 2:3] == seg_ref[0]
    weight = jnp.where(same, dot_rows(grad, value), 0.0)
    weight_t = jnp.where(same, dot_rows(value, grad), 0.0)
    diagonal = jnp.sum(jnp.where(level == LEVELS, weight, 0.0), axis=1, keepdims=True)
    dq = diagonal * key
    dk = diagonal * query
    moved = []
    for number in range(LEVELS):
        part = rows_of(factor, number)
        left = jnp.concatenate(
            [
                jnp.where(level == number, weight, 0.0).astype(BF),
                jnp.where(level_t == number, weight_t, 0.0).astype(BF),
            ],
            axis=1,
        )
        right = jnp.concatenate([(key * part).astype(BF), (query * part).astype(BF)], axis=0)
        both = dot_plain(left, right) * part
        upper = upper_rows(number)
        dq = dq + jnp.where(upper, both, 0.0)
        dk = dk + jnp.where(upper, 0.0, both)
        moved.append(both * jnp.where(upper, query, key))
    cumulative = rows_of(factor, LEVELS)
    enter = enter_ref[0]
    after = state[...]
    after_low = after.astype(BF)
    lift = cumulative * aux[:, 0:1]
    finish = rows_of(factor, LEVELS + 1) * aux[:, 1:2]
    lifted = query * lift
    ending = key * finish
    from_enter = dot_plain(grad, enter)
    from_after = dot_plain(value, after_low)
    moved.append(lifted * from_enter)
    moved.append(ending * from_after)
    dq_ref[...] = ((dq + lift * from_enter) * scale).astype(dq_ref.dtype)
    dk_ref[...] = (dk + finish * from_after).astype(dk_ref.dtype)
    dv = dot_cols(score_ref[0], grad) + dot_rows(ending.astype(BF), after_low)
    dv_ref[...] = dv.astype(dv_ref.dtype)
    through = cumulative[CHUNK - 1 :] * aux[0:1, 3:4]
    passing = jnp.sum(after * enter.astype(F32), axis=0, keepdims=True) * through
    spread = sum_two(dot_plain(sums_t_ref[...], split_two(jnp.concatenate(moved, axis=0))))
    dld_ref[...] = spread + passing
    state[...] = after * through + dot_cols(grad, lifted.astype(BF))


def mix_specs(count, width, backward):
    def at(i):
        return count - 1 - i if backward else i

    def tokens(columns):
        return pl.BlockSpec((CHUNK, columns), lambda i: (at(i), 0))

    def chunks(rows, columns):
        return pl.BlockSpec((1, rows, columns), lambda i: (at(i), 0, 0))

    def whole(rows, columns):
        return pl.BlockSpec((rows, columns), lambda i: (0, 0))

    return tokens, chunks, whole


def mix_forward(query, key, value, log_decay, aux, seg_rows):
    total, width = value.shape
    count = total // CHUNK
    sums, level = chunk_tables()
    tokens, chunks, whole = mix_specs(count, width, False)
    return pl.pallas_call(
        mix_forward_body,
        grid=(count,),
        in_specs=[
            tokens(DK), tokens(DK), tokens(width), tokens(DK), tokens(aux.shape[1]),
            chunks(1, CHUNK), whole(*sums.shape), whole(CHUNK, CHUNK),
        ],
        out_specs=[tokens(width), chunks(width, DK), chunks(CHUNK, CHUNK)],
        out_shape=[
            jax.ShapeDtypeStruct((total, width), BF),
            jax.ShapeDtypeStruct((count, width, DK), BF),
            jax.ShapeDtypeStruct((count, CHUNK, CHUNK), BF),
        ],
        scratch_shapes=[pltpu.VMEM((width, DK), F32)],
        compiler_params=pltpu.CompilerParams(
            dimension_semantics=("arbitrary",), vmem_limit_bytes=32 * 1024 * 1024
        ),
        cost_estimate=pl.CostEstimate(
            flops=total * 2 * (8 * CHUNK * DK + 2 * width * DK + CHUNK * width + 18 * CHUNK * DK),
            bytes_accessed=total * 4096, transcendentals=total * 9 * DK,
        ),
        name="mix_forward",
    )(query, key, value, log_decay, aux, seg_rows, jnp.asarray(sums, BF), jnp.asarray(level))


def mix_backward(query, key, value, log_decay, aux, seg_rows, enter, scores, grad):
    total, width = value.shape
    count = total // CHUNK
    sums, level = chunk_tables()
    tokens, chunks, whole = mix_specs(count, width, True)
    return pl.pallas_call(
        mix_backward_body,
        grid=(count,),
        in_specs=[
            tokens(DK), tokens(DK), tokens(width), tokens(DK), tokens(aux.shape[1]),
            chunks(1, CHUNK), whole(*sums.shape), whole(*sums.shape[::-1]),
            whole(CHUNK, CHUNK), whole(CHUNK, CHUNK),
            chunks(width, DK), chunks(CHUNK, CHUNK), tokens(width),
        ],
        out_specs=[tokens(DK), tokens(DK), tokens(width), tokens(DK)],
        out_shape=[
            jax.ShapeDtypeStruct((total, DK), BF),
            jax.ShapeDtypeStruct((total, DK), BF),
            jax.ShapeDtypeStruct((total, width), BF),
            jax.ShapeDtypeStruct((total, DK), F32),
        ],
        scratch_shapes=[pltpu.VMEM((width, DK), F32)],
        compiler_params=pltpu.CompilerParams(
            dimension_semantics=("arbitrary",), vmem_limit_bytes=48 * 1024 * 1024
        ),
        cost_estimate=pl.CostEstimate(
            flops=total * 2 * (14 * CHUNK * DK + 4 * width * DK + CHUNK * width + 36 * CHUNK * DK),
            bytes_accessed=total * 6144, transcendentals=total * 9 * DK,
        ),
        name="mix_backward",
    )(
        query, key, value, log_decay, aux, seg_rows, jnp.asarray(sums, BF),
        jnp.asarray(np.ascontiguousarray(sums.T), BF), jnp.asarray(level),
        jnp.asarray(np.ascontiguousarray(level.T)), enter, scores, grad,
    )


def remote(source, target, send, arrive, axis, place):
    return pltpu.make_async_remote_copy(
        src_ref=source, dst_ref=target, send_sem=send, recv_sem=arrive,
        device_id={axis: place}, device_id_type=pl.DeviceIdType.MESH,
    )


def greet(peers):
    barrier = pltpu.get_barrier_semaphore()
    number = 0
    for present, peer in peers:
        if present is True:
            pl.semaphore_signal(
                barrier, inc=1, device_id=peer, device_id_type=pl.DeviceIdType.MESH
            )
            number = number + 1
        else:

            @pl.when(present)
            def _():
                pl.semaphore_signal(
                    barrier, inc=1, device_id=peer, device_id_type=pl.DeviceIdType.MESH
                )

            number = number + jnp.where(present, 1, 0)
    pl.semaphore_wait(barrier, number)


def line_peers(axis, count):
    me = lax.axis_index(axis)
    return [(me > 0, {axis: me - 1}), (me < count - 1, {axis: me + 1})]


def all_peers(axis, count):
    me = lax.axis_index(axis)
    return [(True, {axis: lax.rem(me + away, count)}) for away in range(1, count)]


class Gather:
    def __init__(self, axis, count, x_ref, out_ref, send, arrive, local_sem):
        self.axis, self.count, self.x_ref, self.out_ref = axis, count, x_ref, out_ref
        self.send, self.arrive = send, arrive
        self.me = lax.axis_index(axis)
        self.mine = pltpu.make_async_copy(x_ref, self.block(self.me), local_sem)

    def block(self, index):
        own = self.x_ref.shape[0]
        return self.out_ref.at[pl.ds(pl.multiple_of(index * own, own), own)]

    def copy(self, direction, step, index, source):
        return remote(
            source, self.block(index), self.send.at[direction, step],
            self.arrive.at[direction, step], self.axis,
            self.me + 1 if direction == 0 else self.me - 1,
        )

    def hop(self, direction, step):
        index = self.me - step if direction == 0 else self.me + step
        return self.copy(direction, step, index, self.x_ref if step == 0 else self.block(index))

    def landed(self, direction, step):
        index = self.me - 1 - step if direction == 0 else self.me + 1 + step
        return self.copy(direction, step, index, self.block(index))

    def holds(self, direction, step):
        return self.me - step >= 0 if direction == 0 else self.me + step <= self.count - 1

    def hands_on(self, direction, step):
        inner = self.me < self.count - 1 if direction == 0 else self.me > 0
        return self.holds(direction, step) & inner

    def start(self):
        self.mine.start()
        self.run(0)

    def run(self, first, last=None):
        for step in range(first, first + 1 if last is None else last):
            for direction in (0, 1):
                if step > 0:

                    @pl.when(self.holds(direction, step))
                    def _():
                        self.landed(direction, step - 1).wait_recv()

                if step < self.count - 1:

                    @pl.when(self.hands_on(direction, step))
                    def _():
                        self.hop(direction, step).start()

    def finish(self):
        for step in range(self.count - 1):
            for direction in (0, 1):

                @pl.when(self.hands_on(direction, step))
                def _():
                    self.hop(direction, step).wait_send()

        self.mine.wait()

    @staticmethod
    def scratch(count):
        return [
            pltpu.SemaphoreType.DMA((2, count - 1)),
            pltpu.SemaphoreType.DMA((2, count - 1)),
            pltpu.SemaphoreType.DMA,
        ]


class Swap:
    def __init__(self, axis, count, x_ref, out_ref, send, arrive, local_sem):
        self.axis, self.count, self.x_ref, self.out_ref = axis, count, x_ref, out_ref
        self.send, self.arrive = send, arrive
        self.me = lax.axis_index(axis)
        self.mine = pltpu.make_async_copy(x_ref.at[self.me], out_ref.at[self.me], local_sem)

    def hop(self, away):
        peer = lax.rem(self.me + away, self.count)
        return remote(
            self.x_ref.at[peer], self.out_ref.at[self.me], self.send.at[away - 1],
            self.arrive.at[away - 1], self.axis, peer,
        )

    def landed(self, away):
        peer = lax.rem(self.me + self.count - away, self.count)
        return remote(
            self.x_ref.at[peer], self.out_ref.at[peer], self.send.at[away - 1],
            self.arrive.at[away - 1], self.axis, peer,
        )

    def start(self):
        self.mine.start()
        for away in range(1, self.count):
            self.hop(away).start()

    def finish(self):
        for away in range(1, self.count):
            self.landed(away).wait_recv()
        for away in range(1, self.count):
            self.hop(away).wait_send()
        self.mine.wait()

    @staticmethod
    def scratch(count):
        return [
            pltpu.SemaphoreType.DMA((count - 1,)),
            pltpu.SemaphoreType.DMA((count - 1,)),
            pltpu.SemaphoreType.DMA,
        ]


class Scatter:
    def __init__(self, axis, count, pieces, x_ref, out_ref, up, down, send, arrive):
        self.axis, self.count, self.pieces = axis, count, pieces
        self.x_ref, self.out_ref, self.held_refs = x_ref, out_ref, (up, down)
        self.send, self.arrive = send, arrive
        self.me = lax.axis_index(axis)
        self.own = out_ref.shape[0]
        self.size = self.own // pieces

    def part(self, index, piece):
        start = pl.multiple_of(index * self.own + piece * self.size, self.size)
        return self.x_ref.at[pl.ds(start, self.size)]

    def held(self, direction, number, piece):
        return self.held_refs[direction].at[number, pl.ds(piece * self.size, self.size)]

    def hop(self, direction, number, piece, source=None):
        held = self.held(direction, number, piece)
        return remote(
            held if source is None else source, held, self.send.at[direction, number, piece],
            self.arrive.at[direction, number, piece], self.axis,
            self.me + 1 if direction == 0 else self.me - 1,
        )

    def target(self, direction, number):
        return self.count - 1 - number if direction == 0 else number

    def start(self):
        for direction in (0, 1):

            @pl.when(self.me == (0 if direction == 0 else self.count - 1))
            def _():
                for number in range(self.count - 1):
                    target = self.target(direction, number)
                    for piece in range(self.pieces):
                        self.hop(direction, number, piece, self.part(target, piece)).start()

    def stage(self, direction, number, piece):
        me, target = self.me, self.target(direction, number)
        inner = me > 0 if direction == 0 else me < self.count - 1
        passed = me < target if direction == 0 else me > target
        held = self.held(direction, number, piece)

        @pl.when(inner & (passed | (me == target)))
        def _():
            self.hop(direction, number, piece).wait_recv()

        @pl.when(inner & passed)
        def _():
            mine = self.part(target, piece)[...].astype(F32)
            held[...] = (held[...].astype(F32) + mine).astype(BF)
            self.hop(direction, number, piece).start()

    def run(self, number, far):
        for order in (0, 1):

            @pl.when((self.me >= self.count // 2) == (order == 1))
            def _():
                for piece in range(self.pieces):
                    self.stage(1 - order if far else order, number, piece)

    def finish(self):
        me, count, out_ref = self.me, self.count, self.out_ref
        for piece in range(self.pieces):
            rows = pl.ds(piece * self.size, self.size)
            out_ref[rows] = self.part(me, piece)[...].astype(F32)
            for direction in (0, 1):
                for number in range(count - 1):
                    inner = me > 0 if direction == 0 else me < count - 1

                    @pl.when((me == self.target(direction, number)) & inner)
                    def _():
                        out_ref[rows] += self.held(direction, number, piece)[...].astype(F32)

        for direction in (0, 1):
            for number in range(count - 1):
                target = self.target(direction, number)

                @pl.when(me < target if direction == 0 else me > target)
                def _():
                    for piece in range(self.pieces):
                        self.hop(direction, number, piece).wait_send()

    @staticmethod
    def scratch(count, own, columns, pieces):
        return [
            pltpu.VMEM((count - 1, own, columns), BF),
            pltpu.VMEM((count - 1, own, columns), BF),
            pltpu.SemaphoreType.DMA((2, count - 1, pieces)),
            pltpu.SemaphoreType.DMA((2, count - 1, pieces)),
        ]


class Spread:
    def __init__(self, sizes, x_ref, out_ref, send, arrive, far_send, far_arrive, near_send,
                 near_arrive, local_sem):
        self.X, self.C, self.Z, self.Y = sizes
        self.x_ref, self.out_ref = x_ref, out_ref
        self.send, self.arrive = send, arrive
        self.far_send, self.far_arrive = far_send, far_arrive
        self.near_send, self.near_arrive = near_send, near_arrive
        self.x, self.c, self.z, self.y = (lax.axis_index(name) for name in OWN)
        self.others = self.X * self.Y - 1
        self.mine = pltpu.make_async_copy(
            x_ref.at[self.z], self.place(0, self.c, 0), local_sem
        )

    def across(self, offset, sign):
        down, right = offset // self.Y, offset % self.Y
        if sign < 0:
            down, right = self.X - down, self.Y - right
        return lax.rem(self.x + down, self.X), lax.rem(self.y + right, self.Y)

    def place(self, offset, c, slot):
        x, y = self.across(offset, -1)
        z = lax.rem(self.z + self.Z - slot, self.Z)
        return self.out_ref.at[((x * self.C + c) * self.Y + y) * self.Z + z]

    def along(self, away):
        return remote(
            self.x_ref.at[lax.rem(self.z + away, self.Z)], self.place(0, self.c, 0),
            self.send.at[away - 1], self.arrive.at[away - 1], "z",
            lax.rem(self.z + away, self.Z),
        )

    def along_landed(self, away):
        held = self.place(0, self.c, away)
        return remote(
            held, held, self.send.at[away - 1], self.arrive.at[away - 1], "z",
            lax.rem(self.z + away, self.Z),
        )

    def far(self, offset, slot, landed=False):
        x, y = self.across(offset, 1)
        held = self.place(offset if landed else 0, self.c, slot)
        source = self.x_ref.at[self.z] if slot == 0 and not landed else held
        return pltpu.make_async_remote_copy(
            src_ref=source, dst_ref=held, send_sem=self.far_send.at[offset - 1, slot],
            recv_sem=self.far_arrive.at[offset - 1, slot], device_id={"x": x, "y": y},
            device_id_type=pl.DeviceIdType.MESH,
        )

    def near(self, offset, slot, landed=False):
        held = self.place(offset, 1 - self.c if landed else self.c, slot)
        direct = offset == 0 and slot == 0 and not landed
        return remote(
            self.x_ref.at[self.z] if direct else held, held, self.near_send.at[offset, slot],
            self.near_arrive.at[offset, slot], "c", 1 - self.c,
        )

    def peers(self):
        found = all_peers("z", self.Z) + [(True, {"c": 1 - self.c})]
        for offset in range(1, self.others + 1):
            x, y = self.across(offset, 1)
            found.append((True, {"x": x, "y": y}))
        return found

    def start(self):
        self.mine.start()
        for away in range(1, self.Z):
            self.along(away).start()
        self.hand_on(0)

    def hand_on(self, slot):
        if slot > 0:
            self.along_landed(slot).wait_recv()
        for offset in range(1, self.others + 1):
            self.far(offset, slot).start()
        self.near(0, slot).start()

    def collect(self, slot):
        for offset in range(1, self.others + 1):
            self.far(offset, slot, True).wait_recv()
            self.near(offset, slot).start()

    def finish(self):
        for slot in range(self.Z):
            for offset in range(self.others + 1):
                self.near(offset, slot, True).wait_recv()
        for slot in range(self.Z):
            for offset in range(self.others + 1):
                self.near(offset, slot).wait_send()
                if offset > 0:
                    self.far(offset, slot).wait_send()
        for away in range(1, self.Z):
            self.along(away).wait_send()
        self.mine.wait()

    @staticmethod
    def scratch(sizes):
        X, C, Z, Y = sizes
        far = pltpu.SemaphoreType.DMA((max(X * Y - 1, 1), Z))
        near = pltpu.SemaphoreType.DMA((X * Y, Z))
        line = pltpu.SemaphoreType.DMA((Z - 1,))
        return [line, line, far, far, near, near, pltpu.SemaphoreType.DMA]


def spread_and_gather(value, block, other, sizes, number):
    X, C, Z, Y = sizes

    def body(v_ref, x_ref, o_ref, spread_ref, out_ref, swapped_ref, *sems):
        spread = Spread(sizes, v_ref, spread_ref, *sems[:7])
        gather = Gather("z", Z, x_ref, out_ref, *sems[7:10])
        swap = Swap("z", Z, o_ref, swapped_ref, *sems[10:])
        greet(spread.peers())
        spread.start()
        gather.start()
        for slot in range(1, Z):
            spread.hand_on(slot)
        for step in range(1, Z):
            gather.run(step)
            if step == Z - 2:
                swap.start()
            spread.collect(step - 1)
        spread.collect(Z - 1)
        spread.finish()
        gather.finish()
        swap.finish()

    anywhere = pl.BlockSpec(memory_space=pl.ANY)
    return pl.pallas_call(
        body,
        in_specs=[anywhere] * 3,
        out_specs=[anywhere] * 3,
        out_shape=[
            jax.ShapeDtypeStruct((X * C * Y * Z,) + value.shape[1:], value.dtype),
            jax.ShapeDtypeStruct((Z * block.shape[0],) + block.shape[1:], block.dtype),
            jax.ShapeDtypeStruct(other.shape, other.dtype),
        ],
        scratch_shapes=Spread.scratch(sizes) + Gather.scratch(Z) + Swap.scratch(Z),
        compiler_params=pltpu.CompilerParams(collective_id=number, has_side_effects=True),
        cost_estimate=pl.CostEstimate(
            flops=WAIT_FLOPS, bytes_accessed=value.size * X * C * Y * 2, transcendentals=0
        ),
        name="spread_and_gather",
    )(value, block, other)


def move(number, scatter=None, swaps=(), gathers=(), extras=(), post=None):
    in_vmem, anywhere = pl.BlockSpec(memory_space=pltpu.VMEM), pl.BlockSpec(memory_space=pl.ANY)
    values, in_specs, shapes, out_specs, scratch = [], [], [], [], []
    flags = {}

    def scale(axis):
        return lax.axis_size(axis)

    if scatter is not None:
        partial, axis = scatter
        own = partial.shape[0] // scale(axis)
        values += [partial, *extras]
        in_specs += [in_vmem] * (1 + len(extras))
        shapes.append(jax.ShapeDtypeStruct((own, partial.shape[1]), F32))
        out_specs.append(in_vmem)
        scratch += Scatter.scratch(scale(axis), own, partial.shape[1], PIECES)
        flags = dict(vmem_limit_bytes=40 * 1024 * 1024)
    for value, axis in swaps:
        values.append(value)
        in_specs.append(anywhere)
        shapes.append(jax.ShapeDtypeStruct(value.shape, value.dtype))
        out_specs.append(anywhere)
        scratch += Swap.scratch(scale(axis))
    for block, axis in gathers:
        values.append(block)
        in_specs.append(anywhere)
        shapes.append(
            jax.ShapeDtypeStruct((scale(axis) * block.shape[0], block.shape[1]), block.dtype)
        )
        out_specs.append(anywhere)
        scratch += Gather.scratch(scale(axis))

    def body(*refs):
        ins = list(refs[: len(values)])
        outs = list(refs[len(values) : len(values) + len(shapes)])
        sems = list(refs[len(values) + len(shapes) :])
        peers = {}
        adding, extra_refs, swapping, gathering = None, (), [], []
        if scatter is not None:
            axis = scatter[1]
            adding = Scatter(axis, scale(axis), PIECES, ins.pop(0), outs.pop(0), *sems[:4])
            extra_refs, ins, sems = ins[: len(extras)], ins[len(extras) :], sems[4:]
            peers[axis] = line_peers(axis, scale(axis))
        for _, axis in gathers:
            peers[axis] = line_peers(axis, scale(axis))
        for _, axis in swaps:
            peers[axis] = all_peers(axis, scale(axis))
            swapping.append(Swap(axis, scale(axis), ins.pop(0), outs.pop(0), *sems[:3]))
            sems = sems[3:]
        for _, axis in gathers:
            gathering.append(Gather(axis, scale(axis), ins.pop(0), outs.pop(0), *sems[:3]))
            sems = sems[3:]
        greet([peer for found in peers.values() for peer in found])
        for part in gathering + ([adding] if adding else []) + swapping:
            part.start()
        steps = max([part.count for part in gathering + ([adding] if adding else [])] + [0])
        for part in gathering:
            part.run(1)
        for step in range(1, steps):
            if adding:
                adding.run(step - 1, False)
            for part in gathering:
                if step + 1 < part.count:
                    part.run(step + 1)
            if adding:
                adding.run(step - 1, True)
        if adding:
            adding.finish()
            if post is not None:
                adding.out_ref[...] = post(adding.out_ref[...], *[r[...] for r in extra_refs])
        for part in swapping + gathering:
            part.finish()

    size = sum(v.size for v in values)
    return pl.pallas_call(
        body,
        in_specs=in_specs,
        out_specs=out_specs,
        out_shape=shapes,
        scratch_shapes=scratch,
        compiler_params=pltpu.CompilerParams(
            collective_id=number, has_side_effects=True, **flags
        ),
        cost_estimate=pl.CostEstimate(
            flops=WAIT_FLOPS, bytes_accessed=size * 4, transcendentals=0
        ),
        name="move",
    )(*values)


def local(
    tokens, doc_lengths, cotangent, attn_gain, query_weight, key_weight, value_weight, gate_weight,
    rank_in, rank_out, decay_bias, head_gain, out_weight, mlp_gain, mlp_gate_weight,
    mlp_up_weight, down_weight,
):
    own, width = tokens.shape
    rows = query_weight.shape[0]
    X, C, Z, Y = (lax.axis_size(name) for name in OWN)
    z = lax.axis_index("z")
    group = own * Z
    total = group * Y
    ff = down_weight.shape[1] // Z
    dvp = DV // Y

    def blocked(value):
        lead = value.shape[:-1]
        cut = value.reshape(lead + (X, C, Z, Y, rows))
        return jnp.swapaxes(cut, -3, -2).reshape(lead + (width,))

    def straight(value):
        found = []
        for start in range(0, width, Z * Y * rows):
            for at_z in range(Z):
                for at_y in range(Y):
                    first_lane = start + (at_y * Z + at_z) * rows
                    found.append(value[:, first_lane : first_lane + rows])
        return jnp.concatenate(found, axis=1)

    def cut_columns(weight):
        return jnp.swapaxes(weight.reshape(rows, Z, weight.shape[1] // Z), 0, 1)

    def pad_rows(value):
        flat = value.reshape(value.shape[0], -1)
        return jnp.pad(flat, ((0, rows - flat.shape[0]), (0, 0)))

    numbers = iter(range(32))

    def swap_y(value):
        return move(next(numbers), swaps=[(value, "y")])[0]

    def gather_z(value):
        return move(next(numbers), gathers=[(value, "z")])[0]

    def after(value, *others):
        return lax.optimization_barrier((value,) + others)[0]

    def to_sequence(value):
        cut = value.reshape(Y, Z, own, value.shape[-1])
        return jnp.swapaxes(cut, 0, 1).reshape(total, value.shape[-1])

    def from_sequence(value):
        cut = value.reshape(Z, Y, own, value.shape[-1])
        return jnp.swapaxes(cut, 0, 1).reshape(Y, group, value.shape[-1])

    def scatter_rest(value):
        sums = lax.psum_scatter(value, REST, scatter_dimension=0, tiled=True)
        return sums.reshape(Z, rows, -1)

    def gather_rest(value):
        return lax.all_gather(value.reshape(Z * rows, -1), REST, axis=0, tiled=True)

    small = jnp.concatenate(
        [
            rank_in, pad_rows(attn_gain), pad_rows(mlp_gain), pad_rows(rank_out),
            pad_rows(decay_bias), pad_rows(head_gain),
        ],
        axis=1,
    )
    small = jnp.pad(small, ((0, 0), (0, SMALL - small.shape[1])))
    first = jnp.concatenate(
        [cut_columns(w) for w in (query_weight, key_weight, value_weight, gate_weight)]
        + [jnp.broadcast_to(small[None], (Z,) + small.shape)],
        axis=2,
    )
    own_tokens = blocked(tokens)
    input_weights, group_tokens, out_weights = spread_and_gather(
        first, own_tokens, cut_columns(out_weight), (X, C, Z, Y), next(numbers)
    )
    input_weights = input_weights.reshape(width, -1)
    mlp_weights = jnp.concatenate(
        [cut_columns(mlp_gate_weight), cut_columns(mlp_up_weight)], axis=2
    )
    down_weights = cut_columns(down_weight)

    projected = 2 * DK + 2 * DV
    near = 2 * DK + DV
    small_all = input_weights[:, projected:].astype(F32)

    def device_rows(value, count):
        cut = value.reshape(X, C, Y, Z, rows, -1)[:, :, :, :, : rows // count]
        return jnp.swapaxes(cut, 2, 3).reshape(width // count, -1)

    attn_gain_all = small_all[:, R]
    mlp_gain_all = small_all[:, R + 1]
    rank_out_all = device_rows(small_all[:, R + 2 : 2 * R + 2], width // (H * DK))
    bias_all = device_rows(small_all[:, 2 * R + 2 : 2 * R + 3], width // (H * DK))
    head_gain_all = device_rows(small_all[:, 2 * R + 3 : 2 * R + 4], width // DV)[:, 0]
    rank_out_z = lax.dynamic_slice_in_dim(rank_out_all, z * DK, DK).astype(BF)
    bias_z = lax.dynamic_slice_in_dim(bias_all, z * DK, DK)[:, 0]

    rows_in = group_tokens.astype(F32)
    scale_in = lax.rsqrt(jnp.mean(rows_in * rows_in, axis=1, keepdims=True) + norm_eps)
    normed_in = (rows_in * scale_in * attn_gain_all).astype(BF)
    heads = dot_plain(normed_in, input_weights)
    out_gate = heads[:, 2 * DK + DV : projected]
    low = heads.astype(BF)
    shared = jnp.concatenate([low[:, : 2 * DK], low[:, projected:]], axis=1)
    values = jnp.swapaxes(low[:, 2 * DK : 2 * DK + DV].reshape(group, Y, dvp), 0, 1)
    sent = jnp.concatenate([jnp.broadcast_to(shared[None], (Y,) + shared.shape), values], axis=2)
    sent, mlp_weights = move(next(numbers), swaps=[(sent, "y"), (mlp_weights, "z")])
    out_piece = gather_rest(out_weights)
    mlp_piece = gather_rest(mlp_weights)
    sequence = to_sequence(sent)
    queries = sequence[:, :DK]
    keys = sequence[:, DK : 2 * DK]
    rank_low = sequence[:, 2 * DK : 2 * DK + R]
    value_part = sequence[:, 2 * DK + SMALL :]
    decay_logit = dot_rows(rank_low, rank_out_z) + bias_z
    log_decay = jax.nn.log_sigmoid(decay_logit) / decay_norm

    doc_ends = jnp.cumsum(doc_lengths[0])
    positions = lax.iota(jnp.int32, total)
    segments = jnp.sum((doc_ends[None, :] <= positions[:, None]).astype(jnp.int32), axis=1)
    cut = segments.reshape(-1, CHUNK)
    last = cut[:, CHUNK - 1 :]
    before = jnp.concatenate([jnp.full((1, 1), -1, jnp.int32), last[:-1]], axis=0)
    aux = jnp.stack(
        [cut == before, cut == last, cut, jnp.broadcast_to(last == before, cut.shape)], axis=-1
    )
    aux = aux.reshape(total, 4).astype(F32)
    seg_rows = cut.astype(F32)[:, None, :]

    mixed_part, enter, scores = mix_forward(queries, keys, value_part, log_decay, aux, seg_rows)
    mixed_part, down_weights = move(
        next(numbers), swaps=[(from_sequence(mixed_part), "y"), (down_weights, "z")]
    )
    down_piece = gather_rest(down_weights)
    mixed = jnp.swapaxes(mixed_part, 0, 1).reshape(group, DV).astype(F32)

    head_scale = lax.rsqrt(jnp.mean(mixed * mixed, axis=1, keepdims=True) + head_eps)
    head_hat = mixed * head_scale
    head_out = head_hat * head_gain_all
    sig_out = jax.nn.sigmoid(out_gate)
    silu_out = out_gate * sig_out
    gated = (head_out * silu_out).astype(BF)
    own_cotangent = blocked(cotangent)
    residual, group_cotangent = move(
        next(numbers), scatter=(dot_rows(gated, out_piece).astype(BF), "z"),
        gathers=[(own_cotangent, "z")], extras=[own_tokens],
        post=lambda total_sum, x: total_sum + x.astype(F32),
    )
    scale_mid = lax.rsqrt(jnp.mean(residual * residual, axis=1, keepdims=True) + norm_eps)
    hat_mid = residual * scale_mid
    normed_mlp = gather_z((hat_mid * mlp_gain_all).astype(BF))

    both_pre = dot_plain(normed_mlp, mlp_piece)
    gate_pre = both_pre[:, :ff]
    up_pre = both_pre[:, ff:]
    sig_gate = jax.nn.sigmoid(gate_pre)
    silu_gate = gate_pre * sig_gate
    hidden = (silu_gate * up_pre).astype(BF)
    grad_hidden = dot_plain(group_cotangent, down_piece)
    grad_gate = (grad_hidden * up_pre * sig_gate * (1.0 + gate_pre * (1.0 - sig_gate))).astype(BF)
    grad_up = (grad_hidden * silu_gate).astype(BF)
    grad_both = jnp.concatenate([grad_gate, grad_up], axis=1)
    out_partial = dot_rows(hidden, down_piece).astype(BF)
    mlp_back, down_partial = lax.optimization_barrier(
        (
            dot_rows(grad_both, mlp_piece).astype(BF),
            dot_cols(group_cotangent, hidden).astype(BF),
        )
    )
    down_sums = scatter_rest(down_partial)
    grad_normed_mlp = move(next(numbers), scatter=(mlp_back, "z"))[0]
    mlp_partial = dot_cols(normed_mlp, grad_both).astype(BF)

    mlp_gain_part = jnp.sum(grad_normed_mlp * hat_mid, axis=0)
    scaled = grad_normed_mlp * mlp_gain_all
    grad_residual = own_cotangent.astype(F32) + scale_mid * (
        scaled - hat_mid * jnp.mean(scaled * hat_mid, axis=1, keepdims=True)
    )
    branch_own, mlp_partial = lax.optimization_barrier((grad_residual.astype(BF), mlp_partial))
    mlp_sums = scatter_rest(after(mlp_partial, down_sums))
    layer_out, grad_branch = move(
        next(numbers), scatter=(out_partial, "z"), gathers=[(branch_own, "z")],
        extras=[residual], post=lambda total_sum, rest: straight(total_sum + rest),
    )
    grad_gated = dot_plain(grad_branch, out_piece)
    grad_head = grad_gated * silu_out
    head_gain_part = jnp.sum(grad_head * head_hat, axis=0)
    from_head = grad_head * head_gain_all
    grad_mixed = head_scale * (
        from_head - head_hat * jnp.mean(from_head * head_hat, axis=1, keepdims=True)
    )
    grad_out_gate = (grad_gated * head_out * sig_out * (1.0 + out_gate * (1.0 - sig_out))).astype(BF)
    grad_part = to_sequence(
        swap_y(jnp.swapaxes(grad_mixed.astype(BF).reshape(group, Y, dvp), 0, 1))
    )
    dq, dk, dv, dld = mix_backward(
        queries, keys, value_part, log_decay, aux, seg_rows, enter, scores, grad_part
    )
    dlogit = (dld * jax.nn.sigmoid(-decay_logit) / decay_norm).astype(BF)
    back = from_sequence(jnp.concatenate([dq, dk, dlogit, dv], axis=1))
    side_partial = jnp.concatenate(
        [dot_cols(normed_in, grad_out_gate), dot_cols(grad_branch, gated)], axis=1
    ).astype(BF)
    back, side_partial = lax.optimization_barrier((back, side_partial))
    side_sums = scatter_rest(after(side_partial, mlp_sums))
    back, down_rows, mlp_rows = move(
        next(numbers), swaps=[(back, "y"), (down_sums, "z"), (mlp_sums, "z")]
    )
    summed = jnp.sum(back[:, :, : 3 * DK].astype(F32), axis=0).astype(BF)
    grad_value = jnp.swapaxes(back[:, :, 3 * DK :], 0, 1).reshape(group, DV)
    grad_logit = summed[:, 2 * DK :]
    bias_part = jnp.sum(grad_logit.astype(F32), axis=0)
    rank_low_group = low[:, projected : projected + R]
    rank_out_part = dot_cols(grad_logit, rank_low_group)
    grad_rank = dot_plain(grad_logit, rank_out_z).astype(BF)
    grad_heads = jnp.concatenate(
        [
            summed[:, : 2 * DK], grad_value, grad_out_gate,
            jnp.pad(grad_rank, ((0, 0), (0, SMALL - R))),
        ],
        axis=1,
    )
    normed_in_partial = dot_rows(grad_heads, input_weights)
    attn_gain_part = jnp.sum(normed_in_partial * (rows_in * scale_in), axis=0)
    def to_device_rows(value, count):
        cut = value.reshape(X, C, Z, Y, rows // count, -1)
        cut = jnp.swapaxes(cut, 2, 3)
        cut = jnp.pad(cut, ((0, 0),) * 4 + ((0, rows - rows // count), (0, 0)))
        return cut.reshape(width, -1)

    def at_head(value):
        return lax.dynamic_update_slice_in_dim(
            jnp.zeros((H * DK, value.shape[1]), F32), value, z * DK, 0
        )

    near_part = dot_cols(
        normed_in, jnp.concatenate([grad_heads[:, :near], grad_heads[:, projected:]], axis=1)
    )
    small_part = jnp.concatenate(
        [
            near_part[:, near : near + R],
            attn_gain_part[:, None],
            mlp_gain_part[:, None],
            to_device_rows(at_head(rank_out_part), width // (H * DK)),
            to_device_rows(at_head(bias_part[:, None]), width // (H * DK)),
            to_device_rows(head_gain_part[:, None], width // DV),
        ],
        axis=1,
    )
    small_part = jnp.pad(small_part, ((0, 0), (0, SMALL - small_part.shape[1])))
    near_partial = jnp.concatenate([near_part[:, :near], small_part], axis=1).astype(BF)
    partial, near_partial = lax.optimization_barrier(
        (normed_in_partial.astype(BF), near_partial)
    )
    near_sums = scatter_rest(after(near_partial, side_sums))

    def finish_tokens(back_sum, x, grad_res, gain):
        held = x.astype(F32)
        scale = lax.rsqrt(jnp.mean(held * held, axis=1, keepdims=True) + norm_eps)
        hat = held * scale
        scaled = back_sum * gain
        mean = jnp.mean(scaled * hat, axis=1, keepdims=True)
        return straight(grad_res + scale * (scaled - hat * mean))

    tokens_grad, side_rows = move(
        next(numbers), scatter=(partial, "z"), swaps=[(side_sums, "z")],
        extras=[own_tokens, grad_residual, attn_gain_all[None]], post=finish_tokens,
    )
    near_rows = move(next(numbers), swaps=[(after(near_sums, tokens_grad), "z")])[0]

    def joined(value):
        return jnp.swapaxes(value, 0, 1).reshape(rows, -1).astype(F32)

    small_rows = jnp.sum(near_rows[:, :, near : near + SMALL].astype(F32), axis=0)
    return (
        layer_out,
        tokens_grad,
        small_rows[:, R],
        joined(near_rows[:, :, :DK]),
        joined(near_rows[:, :, DK : 2 * DK]),
        joined(near_rows[:, :, 2 * DK : near]),
        joined(side_rows[:, :, :DV]),
        small_rows[:, :R],
        small_rows[: rows * H * DK // width, R + 2 : 2 * R + 2],
        small_rows[: rows * H * DK // width, 2 * R + 2],
        small_rows[: rows * DV // width, 2 * R + 3],
        joined(side_rows[:, :, DV:]),
        small_rows[:, R + 1],
        joined(mlp_rows[:, :, :ff]),
        joined(mlp_rows[:, :, ff:]),
        joined(down_rows),
    )


def solution(mesh):
    groups, places = mesh.shape["grp"], mesh.shape["seq"]
    wide = Mesh(mesh.devices.reshape(groups // 2, 2, H, places // H), OWN)
    split = P(OWN, None)
    line = P(OWN)
    by_sequence = P(("x", "c"), None)
    placed = (
        split, by_sequence, split, line, split, split, split, split, split, split,
        line, line, split, line, split, split, split,
    )
    return jax.shard_map(
        local,
        mesh=wide,
        in_specs=placed,
        out_specs=(
            split, split, line, split, split, split, split, split, split, line, line, split,
            line, split, split, split,
        ),
        check_vma=False,
    )
```

```python
import functools

import jax
import jax.numpy as jnp
import numpy as np
from jax import lax
from jax.experimental import pallas as pl
from jax.experimental.pallas import tpu as pltpu
from jax.sharding import Mesh
from jax.sharding import PartitionSpec as P

H = 4
DK = 256
DV = 512
R = 16
CHUNK = 128
LEVELS = 7
SMALL = 128
WAIT_FLOPS = 100_000_000
PIECES = 2
norm_eps = 1e-06
head_eps = 0.25
decay_norm = 16.0
BF = jnp.bfloat16
F32 = jnp.float32
REST = ("x", "c", "y")
OWN = ("x", "c", "z", "y")


def dot_plain(left, right):
    return jnp.dot(left, right, preferred_element_type=F32)


def dot_rows(left, right):
    return lax.dot_general(left, right, (((1,), (1,)), ((), ())), preferred_element_type=F32)


def dot_cols(left, right):
    return lax.dot_general(left, right, (((0,), (0,)), ((), ())), preferred_element_type=F32)


def split_two(value):
    high = value.astype(BF)
    return jnp.concatenate([high, (value - high.astype(F32)).astype(BF)], axis=1)


def sum_two(value):
    half = value.shape[1] // 2
    return value[:, :half] + value[:, half:]


def chunk_tables():
    t = np.arange(CHUNK)[:, None]
    j = np.arange(CHUNK)[None, :]
    parts = []
    level = np.full((CHUNK, CHUNK), -1, np.int32)
    for number in range(LEVELS):
        half = CHUNK >> (number + 1)
        middle = t // (2 * half) * (2 * half) + half - 1
        upper = t % (2 * half) >= half
        parts.append(np.where(upper, (j > middle) & (j <= t), (j > t) & (j <= middle)))
        pair = (t // (2 * half) == j // (2 * half)) & upper & (j % (2 * half) < half)
        level[pair] = number
    level[np.arange(CHUNK), np.arange(CHUNK)] = LEVELS
    parts.append(j <= t)
    parts.append(j > t)
    return np.concatenate(parts, axis=0).astype(np.float32), level


def upper_rows(number):
    half = CHUNK >> (number + 1)
    rows = lax.broadcasted_iota(jnp.int32, (CHUNK, 1), 0)
    return lax.rem(rows, 2 * half) >= half


def factors(ld_ref, sums_ref):
    exponents = sum_two(dot_plain(sums_ref[...], split_two(ld_ref[...])))
    return jnp.exp(exponents)


def rows_of(value, number):
    return value[number * CHUNK : (number + 1) * CHUNK]


def mix_forward_body(
    q_ref, k_ref, v_ref, ld_ref, aux_ref, seg_ref, sums_ref, level_ref,
    out_ref, enter_ref, score_ref, state,
):
    @pl.when(pl.program_id(0) == 0)
    def _():
        state[...] = jnp.zeros_like(state)

    factor = factors(ld_ref, sums_ref)
    query = q_ref[...].astype(F32) * DK ** (-0.5)
    key = k_ref[...].astype(F32)
    level = level_ref[...]
    aux = aux_ref[...]
    scores = jnp.where(level == LEVELS, dot_rows(query.astype(BF), k_ref[...]), 0.0)
    for number in range(LEVELS):
        part = rows_of(factor, number)
        pairs = dot_rows((query * part).astype(BF), (key * part).astype(BF))
        scores = jnp.where(level == number, pairs, scores)
    scores = jnp.where(aux[:, 2:3] == seg_ref[0], scores, 0.0).astype(BF)
    score_ref[0] = scores
    cumulative = rows_of(factor, LEVELS)
    enter = state[...].astype(BF)
    enter_ref[0] = enter
    lifted = (query * cumulative * aux[:, 0:1]).astype(BF)
    ending = (key * rows_of(factor, LEVELS + 1) * aux[:, 1:2]).astype(BF)
    out = dot_plain(scores, v_ref[...]) + dot_rows(lifted, enter)
    out_ref[...] = out.astype(out_ref.dtype)
    through = cumulative[CHUNK - 1 :] * aux[0:1, 3:4]
    state[...] = state[...] * through + dot_cols(v_ref[...], ending)


def mix_backward_body(
    q_ref, k_ref, v_ref, ld_ref, aux_ref, seg_ref, sums_ref, sums_t_ref, level_ref, level_t_ref,
    enter_ref, score_ref, do_ref,
    dq_ref, dk_ref, dv_ref, dld_ref, state,
):
    @pl.when(pl.program_id(0) == 0)
    def _():
        state[...] = jnp.zeros_like(state)

    factor = factors(ld_ref, sums_ref)
    scale = DK ** (-0.5)
    query = q_ref[...].astype(F32) * scale
    key = k_ref[...].astype(F32)
    value = v_ref[...]
    grad = do_ref[...]
    level = level_ref[...]
    level_t = level_t_ref[...]
    aux = aux_ref[...]
    same = aux[:, 2:3] == seg_ref[0]
    weight = jnp.where(same, dot_rows(grad, value), 0.0)
    weight_t = jnp.where(same, dot_rows(value, grad), 0.0)
    diagonal = jnp.sum(jnp.where(level == LEVELS, weight, 0.0), axis=1, keepdims=True)
    dq = diagonal * key
    dk = diagonal * query
    moved = []
    for number in range(LEVELS):
        part = rows_of(factor, number)
        left = jnp.concatenate(
            [
                jnp.where(level == number, weight, 0.0).astype(BF),
                jnp.where(level_t == number, weight_t, 0.0).astype(BF),
            ],
            axis=1,
        )
        right = jnp.concatenate([(key * part).astype(BF), (query * part).astype(BF)], axis=0)
        both = dot_plain(left, right) * part
        upper = upper_rows(number)
        dq = dq + jnp.where(upper, both, 0.0)
        dk = dk + jnp.where(upper, 0.0, both)
        moved.append(both * jnp.where(upper, query, key))
    cumulative = rows_of(factor, LEVELS)
    enter = enter_ref[0]
    after = state[...]
    after_low = after.astype(BF)
    lift = cumulative * aux[:, 0:1]
    finish = rows_of(factor, LEVELS + 1) * aux[:, 1:2]
    lifted = query * lift
    ending = key * finish
    from_enter = dot_plain(grad, enter)
    from_after = dot_plain(value, after_low)
    moved.append(lifted * from_enter)
    moved.append(ending * from_after)
    dq_ref[...] = ((dq + lift * from_enter) * scale).astype(dq_ref.dtype)
    dk_ref[...] = (dk + finish * from_after).astype(dk_ref.dtype)
    dv = dot_cols(score_ref[0], grad) + dot_rows(ending.astype(BF), after_low)
    dv_ref[...] = dv.astype(dv_ref.dtype)
    through = cumulative[CHUNK - 1 :] * aux[0:1, 3:4]
    passing = jnp.sum(after * enter.astype(F32), axis=0, keepdims=True) * through
    spread = sum_two(dot_plain(sums_t_ref[...], split_two(jnp.concatenate(moved, axis=0))))
    dld_ref[...] = spread + passing
    state[...] = after * through + dot_cols(grad, lifted.astype(BF))


def mix_specs(count, width, backward):
    def at(i):
        return count - 1 - i if backward else i

    def tokens(columns):
        return pl.BlockSpec((CHUNK, columns), lambda i: (at(i), 0))

    def chunks(rows, columns):
        return pl.BlockSpec((1, rows, columns), lambda i: (at(i), 0, 0))

    def whole(rows, columns):
        return pl.BlockSpec((rows, columns), lambda i: (0, 0))

    return tokens, chunks, whole


def mix_forward(query, key, value, log_decay, aux, seg_rows):
    total, width = value.shape
    count = total // CHUNK
    sums, level = chunk_tables()
    tokens, chunks, whole = mix_specs(count, width, False)
    return pl.pallas_call(
        mix_forward_body,
        grid=(count,),
        in_specs=[
            tokens(DK), tokens(DK), tokens(width), tokens(DK), tokens(aux.shape[1]),
            chunks(1, CHUNK), whole(*sums.shape), whole(CHUNK, CHUNK),
        ],
        out_specs=[tokens(width), chunks(width, DK), chunks(CHUNK, CHUNK)],
        out_shape=[
            jax.ShapeDtypeStruct((total, width), BF),
            jax.ShapeDtypeStruct((count, width, DK), BF),
            jax.ShapeDtypeStruct((count, CHUNK, CHUNK), BF),
        ],
        scratch_shapes=[pltpu.VMEM((width, DK), F32)],
        compiler_params=pltpu.CompilerParams(
            dimension_semantics=("arbitrary",), vmem_limit_bytes=32 * 1024 * 1024
        ),
        cost_estimate=pl.CostEstimate(
            flops=total * 2 * (8 * CHUNK * DK + 2 * width * DK + CHUNK * width + 18 * CHUNK * DK),
            bytes_accessed=total * 4096, transcendentals=total * 9 * DK,
        ),
        name="mix_forward",
    )(query, key, value, log_decay, aux, seg_rows, jnp.asarray(sums, BF), jnp.asarray(level))


def mix_backward(query, key, value, log_decay, aux, seg_rows, enter, scores, grad):
    total, width = value.shape
    count = total // CHUNK
    sums, level = chunk_tables()
    tokens, chunks, whole = mix_specs(count, width, True)
    return pl.pallas_call(
        mix_backward_body,
        grid=(count,),
        in_specs=[
            tokens(DK), tokens(DK), tokens(width), tokens(DK), tokens(aux.shape[1]),
            chunks(1, CHUNK), whole(*sums.shape), whole(*sums.shape[::-1]),
            whole(CHUNK, CHUNK), whole(CHUNK, CHUNK),
            chunks(width, DK), chunks(CHUNK, CHUNK), tokens(width),
        ],
        out_specs=[tokens(DK), tokens(DK), tokens(width), tokens(DK)],
        out_shape=[
            jax.ShapeDtypeStruct((total, DK), BF),
            jax.ShapeDtypeStruct((total, DK), BF),
            jax.ShapeDtypeStruct((total, width), BF),
            jax.ShapeDtypeStruct((total, DK), F32),
        ],
        scratch_shapes=[pltpu.VMEM((width, DK), F32)],
        compiler_params=pltpu.CompilerParams(
            dimension_semantics=("arbitrary",), vmem_limit_bytes=48 * 1024 * 1024
        ),
        cost_estimate=pl.CostEstimate(
            flops=total * 2 * (14 * CHUNK * DK + 4 * width * DK + CHUNK * width + 36 * CHUNK * DK),
            bytes_accessed=total * 6144, transcendentals=total * 9 * DK,
        ),
        name="mix_backward",
    )(
        query, key, value, log_decay, aux, seg_rows, jnp.asarray(sums, BF),
        jnp.asarray(np.ascontiguousarray(sums.T), BF), jnp.asarray(level),
        jnp.asarray(np.ascontiguousarray(level.T)), enter, scores, grad,
    )


def remote(source, target, send, arrive, axis, place):
    return pltpu.make_async_remote_copy(
        src_ref=source, dst_ref=target, send_sem=send, recv_sem=arrive,
        device_id={axis: place}, device_id_type=pl.DeviceIdType.MESH,
    )


def greet(peers):
    barrier = pltpu.get_barrier_semaphore()
    number = 0
    for present, peer in peers:
        if present is True:
            pl.semaphore_signal(
                barrier, inc=1, device_id=peer, device_id_type=pl.DeviceIdType.MESH
            )
            number = number + 1
        else:

            @pl.when(present)
            def _():
                pl.semaphore_signal(
                    barrier, inc=1, device_id=peer, device_id_type=pl.DeviceIdType.MESH
                )

            number = number + jnp.where(present, 1, 0)
    pl.semaphore_wait(barrier, number)


def line_peers(axis, count):
    me = lax.axis_index(axis)
    return [(me > 0, {axis: me - 1}), (me < count - 1, {axis: me + 1})]


def all_peers(axis, count):
    me = lax.axis_index(axis)
    return [(True, {axis: lax.rem(me + away, count)}) for away in range(1, count)]


class Gather:
    def __init__(self, axis, count, x_ref, out_ref, send, arrive, local_sem):
        self.axis, self.count, self.x_ref, self.out_ref = axis, count, x_ref, out_ref
        self.send, self.arrive = send, arrive
        self.me = lax.axis_index(axis)
        self.mine = pltpu.make_async_copy(x_ref, self.block(self.me), local_sem)

    def block(self, index):
        own = self.x_ref.shape[0]
        return self.out_ref.at[pl.ds(pl.multiple_of(index * own, own), own)]

    def copy(self, direction, step, index, source):
        return remote(
            source, self.block(index), self.send.at[direction, step],
            self.arrive.at[direction, step], self.axis,
            self.me + 1 if direction == 0 else self.me - 1,
        )

    def hop(self, direction, step):
        index = self.me - step if direction == 0 else self.me + step
        return self.copy(direction, step, index, self.x_ref if step == 0 else self.block(index))

    def landed(self, direction, step):
        index = self.me - 1 - step if direction == 0 else self.me + 1 + step
        return self.copy(direction, step, index, self.block(index))

    def holds(self, direction, step):
        return self.me - step >= 0 if direction == 0 else self.me + step <= self.count - 1

    def hands_on(self, direction, step):
        inner = self.me < self.count - 1 if direction == 0 else self.me > 0
        return self.holds(direction, step) & inner

    def start(self):
        self.mine.start()
        self.run(0)

    def run(self, first, last=None):
        for step in range(first, first + 1 if last is None else last):
            for direction in (0, 1):
                if step > 0:

                    @pl.when(self.holds(direction, step))
                    def _():
                        self.landed(direction, step - 1).wait_recv()

                if step < self.count - 1:

                    @pl.when(self.hands_on(direction, step))
                    def _():
                        self.hop(direction, step).start()

    def finish(self):
        self.finish_sends()
        self.mine.wait()

    def finish_sends(self):
        for step in range(self.count - 1):
            for direction in (0, 1):

                @pl.when(self.hands_on(direction, step))
                def _():
                    self.hop(direction, step).wait_send()

    @staticmethod
    def scratch(count):
        return [
            pltpu.SemaphoreType.DMA((2, count - 1)),
            pltpu.SemaphoreType.DMA((2, count - 1)),
            pltpu.SemaphoreType.DMA,
        ]


class Swap:
    def __init__(self, axis, count, x_ref, out_ref, send, arrive, local_sem):
        self.axis, self.count, self.x_ref, self.out_ref = axis, count, x_ref, out_ref
        self.send, self.arrive = send, arrive
        self.me = lax.axis_index(axis)
        self.mine = pltpu.make_async_copy(x_ref.at[self.me], out_ref.at[self.me], local_sem)

    def hop(self, away):
        peer = lax.rem(self.me + away, self.count)
        return remote(
            self.x_ref.at[peer], self.out_ref.at[self.me], self.send.at[away - 1],
            self.arrive.at[away - 1], self.axis, peer,
        )

    def landed(self, away):
        peer = lax.rem(self.me + self.count - away, self.count)
        return remote(
            self.x_ref.at[peer], self.out_ref.at[peer], self.send.at[away - 1],
            self.arrive.at[away - 1], self.axis, peer,
        )

    def start(self):
        self.mine.start()
        for away in range(1, self.count):
            self.hop(away).start()

    def finish(self):
        for away in range(1, self.count):
            self.landed(away).wait_recv()
        for away in range(1, self.count):
            self.hop(away).wait_send()
        self.mine.wait()

    @staticmethod
    def scratch(count):
        return [
            pltpu.SemaphoreType.DMA((count - 1,)),
            pltpu.SemaphoreType.DMA((count - 1,)),
            pltpu.SemaphoreType.DMA,
        ]


class Scatter:
    def __init__(self, axis, count, pieces, x_ref, out_ref, up, down, send, arrive):
        self.axis, self.count, self.pieces = axis, count, pieces
        self.x_ref, self.out_ref, self.held_refs = x_ref, out_ref, (up, down)
        self.send, self.arrive = send, arrive
        self.me = lax.axis_index(axis)
        self.own = out_ref.shape[0]
        self.size = self.own // pieces

    def part(self, index, piece):
        start = pl.multiple_of(index * self.own + piece * self.size, self.size)
        return self.x_ref.at[pl.ds(start, self.size)]

    def held(self, direction, number, piece):
        return self.held_refs[direction].at[number, pl.ds(piece * self.size, self.size)]

    def hop(self, direction, number, piece, source=None):
        held = self.held(direction, number, piece)
        return remote(
            held if source is None else source, held, self.send.at[direction, number, piece],
            self.arrive.at[direction, number, piece], self.axis,
            self.me + 1 if direction == 0 else self.me - 1,
        )

    def target(self, direction, number):
        return self.count - 1 - number if direction == 0 else number

    def start(self, numbers=None):
        for direction in (0, 1):

            @pl.when(self.me == (0 if direction == 0 else self.count - 1))
            def _():
                for number in range(self.count - 1) if numbers is None else numbers:
                    target = self.target(direction, number)
                    for piece in range(self.pieces):
                        self.hop(direction, number, piece, self.part(target, piece)).start()

    def stage(self, direction, number, piece):
        me, target = self.me, self.target(direction, number)
        inner = me > 0 if direction == 0 else me < self.count - 1
        passed = me < target if direction == 0 else me > target
        held = self.held(direction, number, piece)

        @pl.when(inner & (passed | (me == target)))
        def _():
            self.hop(direction, number, piece).wait_recv()

        @pl.when(inner & passed)
        def _():
            mine = self.part(target, piece)[...].astype(F32)
            held[...] = (held[...].astype(F32) + mine).astype(BF)
            self.hop(direction, number, piece).start()

    def run(self, number, far):
        for order in (0, 1):

            @pl.when((self.me >= self.count // 2) == (order == 1))
            def _():
                for piece in range(self.pieces):
                    self.stage(1 - order if far else order, number, piece)

    def finish(self):
        me, count, out_ref = self.me, self.count, self.out_ref
        for piece in range(self.pieces):
            rows = pl.ds(piece * self.size, self.size)
            out_ref[rows] = self.part(me, piece)[...].astype(F32)
            for direction in (0, 1):
                for number in range(count - 1):
                    inner = me > 0 if direction == 0 else me < count - 1

                    @pl.when((me == self.target(direction, number)) & inner)
                    def _():
                        out_ref[rows] += self.held(direction, number, piece)[...].astype(F32)

        for direction in (0, 1):
            for number in range(count - 1):
                target = self.target(direction, number)

                @pl.when(me < target if direction == 0 else me > target)
                def _():
                    for piece in range(self.pieces):
                        self.hop(direction, number, piece).wait_send()

    @staticmethod
    def scratch(count, own, columns, pieces):
        return [
            pltpu.VMEM((count - 1, own, columns), BF),
            pltpu.VMEM((count - 1, own, columns), BF),
            pltpu.SemaphoreType.DMA((2, count - 1, pieces)),
            pltpu.SemaphoreType.DMA((2, count - 1, pieces)),
        ]


class Spread:
    def __init__(self, sizes, x_ref, out_ref, send, arrive, far_send, far_arrive, near_send,
                 near_arrive, local_sem):
        self.X, self.C, self.Z, self.Y = sizes
        self.x_ref, self.out_ref = x_ref, out_ref
        self.send, self.arrive = send, arrive
        self.far_send, self.far_arrive = far_send, far_arrive
        self.near_send, self.near_arrive = near_send, near_arrive
        self.x, self.c, self.z, self.y = (lax.axis_index(name) for name in OWN)
        self.others = self.X * self.Y - 1
        self.mine = pltpu.make_async_copy(
            x_ref.at[self.z], self.place(0, self.c, 0), local_sem
        )

    def across(self, offset, sign):
        down, right = offset // self.Y, offset % self.Y
        if sign < 0:
            down, right = self.X - down, self.Y - right
        return lax.rem(self.x + down, self.X), lax.rem(self.y + right, self.Y)

    def place(self, offset, c, slot):
        x, y = self.across(offset, -1)
        z = lax.rem(self.z + self.Z - slot, self.Z)
        return self.out_ref.at[((x * self.C + c) * self.Y + y) * self.Z + z]

    def along(self, away):
        return remote(
            self.x_ref.at[lax.rem(self.z + away, self.Z)], self.place(0, self.c, 0),
            self.send.at[away - 1], self.arrive.at[away - 1], "z",
            lax.rem(self.z + away, self.Z),
        )

    def along_landed(self, away):
        held = self.place(0, self.c, away)
        return remote(
            held, held, self.send.at[away - 1], self.arrive.at[away - 1], "z",
            lax.rem(self.z + away, self.Z),
        )

    def far(self, offset, slot, landed=False):
        x, y = self.across(offset, 1)
        held = self.place(offset if landed else 0, self.c, slot)
        source = self.x_ref.at[self.z] if slot == 0 and not landed else held
        return pltpu.make_async_remote_copy(
            src_ref=source, dst_ref=held, send_sem=self.far_send.at[offset - 1, slot],
            recv_sem=self.far_arrive.at[offset - 1, slot], device_id={"x": x, "y": y},
            device_id_type=pl.DeviceIdType.MESH,
        )

    def near(self, offset, slot, landed=False):
        held = self.place(offset, 1 - self.c if landed else self.c, slot)
        direct = offset == 0 and slot == 0 and not landed
        return remote(
            self.x_ref.at[self.z] if direct else held, held, self.near_send.at[offset, slot],
            self.near_arrive.at[offset, slot], "c", 1 - self.c,
        )

    def peers(self):
        found = all_peers("z", self.Z) + [(True, {"c": 1 - self.c})]
        for offset in range(1, self.others + 1):
            x, y = self.across(offset, 1)
            found.append((True, {"x": x, "y": y}))
        return found

    def start(self):
        self.mine.start()
        for away in range(1, self.Z):
            self.along(away).start()
        self.hand_on(0)

    def hand_on(self, slot):
        if slot > 0:
            self.along_landed(slot).wait_recv()
        for offset in range(1, self.others + 1):
            self.far(offset, slot).start()
        self.near(0, slot).start()

    def collect(self, slot):
        for offset in range(1, self.others + 1):
            self.far(offset, slot, True).wait_recv()
            self.near(offset, slot).start()

    def finish(self):
        for slot in range(self.Z):
            for offset in range(self.others + 1):
                self.near(offset, slot, True).wait_recv()
        for slot in range(self.Z):
            for offset in range(self.others + 1):
                self.near(offset, slot).wait_send()
                if offset > 0:
                    self.far(offset, slot).wait_send()
        for away in range(1, self.Z):
            self.along(away).wait_send()
        self.mine.wait()

    @staticmethod
    def scratch(sizes):
        X, C, Z, Y = sizes
        far = pltpu.SemaphoreType.DMA((max(X * Y - 1, 1), Z))
        near = pltpu.SemaphoreType.DMA((X * Y, Z))
        line = pltpu.SemaphoreType.DMA((Z - 1,))
        return [line, line, far, far, near, near, pltpu.SemaphoreType.DMA]


def spread_and_gather(value, block, other, sizes, number):
    X, C, Z, Y = sizes

    def body(v_ref, x_ref, o_ref, spread_ref, out_ref, swapped_ref, *sems):
        spread = Spread(sizes, v_ref, spread_ref, *sems[:7])
        gather = Gather("z", Z, x_ref, out_ref, *sems[7:10])
        swap = Swap("z", Z, o_ref, swapped_ref, *sems[10:])
        greet(spread.peers())
        spread.start()
        gather.start()
        for slot in range(1, Z):
            spread.hand_on(slot)
        for step in range(1, Z):
            gather.run(step)
            if step == Z - 2:
                swap.start()
            spread.collect(step - 1)
        spread.collect(Z - 1)
        spread.finish()
        gather.finish()
        swap.finish()

    anywhere = pl.BlockSpec(memory_space=pl.ANY)
    return pl.pallas_call(
        body,
        in_specs=[anywhere] * 3,
        out_specs=[anywhere] * 3,
        out_shape=[
            jax.ShapeDtypeStruct((X * C * Y * Z,) + value.shape[1:], value.dtype),
            jax.ShapeDtypeStruct((Z * block.shape[0],) + block.shape[1:], block.dtype),
            jax.ShapeDtypeStruct(other.shape, other.dtype),
        ],
        scratch_shapes=Spread.scratch(sizes) + Gather.scratch(Z) + Swap.scratch(Z),
        compiler_params=pltpu.CompilerParams(collective_id=number, has_side_effects=True),
        cost_estimate=pl.CostEstimate(
            flops=WAIT_FLOPS, bytes_accessed=value.size * X * C * Y * 2, transcendentals=0
        ),
        name="spread_and_gather",
    )(value, block, other)


def move(number, scatter=None, swaps=(), gathers=(), extras=(), post=None):
    in_vmem, anywhere = pl.BlockSpec(memory_space=pltpu.VMEM), pl.BlockSpec(memory_space=pl.ANY)
    values, in_specs, shapes, out_specs, scratch = [], [], [], [], []
    flags = {}

    def scale(axis):
        return lax.axis_size(axis)

    if scatter is not None:
        partial, axis = scatter
        own = partial.shape[0] // scale(axis)
        values += [partial, *extras]
        in_specs += [in_vmem] * (1 + len(extras))
        shapes.append(jax.ShapeDtypeStruct((own, partial.shape[1]), F32))
        out_specs.append(in_vmem)
        scratch += Scatter.scratch(scale(axis), own, partial.shape[1], PIECES)
        flags = dict(vmem_limit_bytes=40 * 1024 * 1024)
    for value, axis in swaps:
        values.append(value)
        in_specs.append(anywhere)
        shapes.append(jax.ShapeDtypeStruct(value.shape, value.dtype))
        out_specs.append(anywhere)
        scratch += Swap.scratch(scale(axis))
    for block, axis in gathers:
        values.append(block)
        in_specs.append(anywhere)
        shapes.append(
            jax.ShapeDtypeStruct((scale(axis) * block.shape[0], block.shape[1]), block.dtype)
        )
        out_specs.append(anywhere)
        scratch += Gather.scratch(scale(axis))

    def body(*refs):
        ins = list(refs[: len(values)])
        outs = list(refs[len(values) : len(values) + len(shapes)])
        sems = list(refs[len(values) + len(shapes) :])
        peers = {}
        adding, extra_refs, swapping, gathering = None, (), [], []
        if scatter is not None:
            axis = scatter[1]
            adding = Scatter(axis, scale(axis), PIECES, ins.pop(0), outs.pop(0), *sems[:4])
            extra_refs, ins, sems = ins[: len(extras)], ins[len(extras) :], sems[4:]
            peers[axis] = line_peers(axis, scale(axis))
        for _, axis in gathers:
            peers[axis] = line_peers(axis, scale(axis))
        for _, axis in swaps:
            peers[axis] = all_peers(axis, scale(axis))
            swapping.append(Swap(axis, scale(axis), ins.pop(0), outs.pop(0), *sems[:3]))
            sems = sems[3:]
        for _, axis in gathers:
            gathering.append(Gather(axis, scale(axis), ins.pop(0), outs.pop(0), *sems[:3]))
            sems = sems[3:]
        greet([peer for found in peers.values() for peer in found])
        for part in gathering + ([adding] if adding else []) + swapping:
            part.start()
        steps = max([part.count for part in gathering + ([adding] if adding else [])] + [0])
        for part in gathering:
            part.run(1)
        for step in range(1, steps):
            if adding:
                adding.run(step - 1, False)
            for part in gathering:
                if step + 1 < part.count:
                    part.run(step + 1)
            if adding:
                adding.run(step - 1, True)
        if adding:
            adding.finish()
            if post is not None:
                adding.out_ref[...] = post(adding.out_ref[...], *[r[...] for r in extra_refs])
        for part in swapping + gathering:
            part.finish()

    size = sum(v.size for v in values)
    return pl.pallas_call(
        body,
        in_specs=in_specs,
        out_specs=out_specs,
        out_shape=shapes,
        scratch_shapes=scratch,
        compiler_params=pltpu.CompilerParams(
            collective_id=number, has_side_effects=True, **flags
        ),
        cost_estimate=pl.CostEstimate(
            flops=WAIT_FLOPS, bytes_accessed=size * 4, transcendentals=0
        ),
        name="move",
    )(*values)


LANES = 128
TILE = 256


def feed_forward(normed_own, mlp_piece, cotangent, number):
    count = lax.axis_size("z")
    own, width = normed_own.shape
    group, ff = own * count, mlp_piece.shape[1] // 3
    half = group // 2
    columns = ff // LANES
    block = width // (2 * lax.axis_size("x"))
    per = block // TILE

    def body(x_ref, w_hbm, c_hbm, sum_ref, down_ref, grad_hbm,
             w_ref, d_ref, c_ref, normed, hidden_grad, hidden, grads, partial, stage, received,
             load_sem, store_sem, pair_send, pair_arrive, gather_send, gather_arrive, local_sem, up, down, send, arrive):
        me, core = lax.axis_index("z"), lax.axis_index("c")
        loads = [
            pltpu.make_async_copy(source, target, load_sem.at[i])
            for i, (source, target) in enumerate(
                [
                    (c_hbm, c_ref),
                    (w_hbm.at[:, pl.ds(2 * ff, ff)], d_ref),
                    (w_hbm.at[:, pl.ds(0, 2 * ff)], w_ref),
                ]
            )
        ]
        for load in loads:
            load.start()
        gather = Gather("z", count, x_ref, normed, gather_send, gather_arrive, local_sem)
        scatter = Scatter("z", count, PIECES, partial, sum_ref, up, down, send, arrive)
        greet(line_peers("z", count) + [(True, {"c": 1 - core})])
        gather.start()
        loads[0].wait()
        loads[1].wait()

        def tile_of(index, size):
            return pl.ds(pl.multiple_of(index * size, size), size)

        def spans(total):
            return [pl.ds(at, min(TILE, total - at)) for at in range(0, total, TILE)]

        for at in spans(ff):
            hidden_grad[:, at] = dot_plain(c_ref[...], d_ref[:, at])
        loads[2].wait()
        lower = me < count // 2
        nearer = me // (count // 2)

        def forward(rows):
            for j in range(columns):
                both_at, at = pl.ds(j * 2 * LANES, 2 * LANES), pl.ds(j * LANES, LANES)
                both = dot_plain(normed[rows], w_ref[:, both_at])
                gate, upper = both[:, :LANES], both[:, LANES:]
                grad = hidden_grad[rows, at]
                sig = jax.nn.sigmoid(gate)
                silu = gate * sig
                hidden[rows, at] = (silu * upper).astype(BF)
                grad_gate = grad * upper * sig * (1.0 + gate * (1.0 - sig))
                grads[rows, both_at] = jnp.concatenate(
                    [grad_gate.astype(BF), (grad * silu).astype(BF)], axis=1
                )

        def backward(rows):
            for at in spans(width):
                partial[rows, at] = dot_rows(grads[rows], w_ref[at]).astype(BF)

        kept = width // 2 // TILE

        def rows_kept(number, by):
            start = (number // per * 2 + by) * block + number % per * TILE
            return pl.ds(pl.multiple_of(start, TILE), TILE)

        def store(number):
            return pltpu.make_async_copy(
                stage.at[number % 2], grad_hbm.at[pl.ds(number * TILE, TILE)],
                store_sem.at[number % 2],
            )

        def pass_over(number):
            return remote(
                stage.at[number % 2], received.at[number], pair_send.at[number % 2],
                pair_arrive.at[number], "c", 1 - core,
            )

        def weight_rows(i):
            ours, number = i >= kept, i % kept
            if i >= 2:
                if i - 2 >= kept:
                    store(i - 2 - kept).wait()
                else:
                    pass_over(i - 2).wait_send()
            at = rows_kept(number, core if ours else 1 - core)
            slot = i % 2
            top = dot_cols(normed[:, at], grads[...])
            low = dot_cols(c_ref[:, at], hidden[...])
            if ours:
                pass_over(number).wait_recv()
                top = top + received[number, :, : 2 * ff].astype(F32)
                low = low + received[number, :, 2 * ff :].astype(F32)
            stage[slot, :, : 2 * ff] = top.astype(BF)
            stage[slot, :, 2 * ff :] = low.astype(BF)
            if ours:
                store(number).start()
            else:
                pass_over(number).start()
            at = pl.ds(i * TILE, TILE)
            down_ref[:, at] = dot_rows(hidden[...], d_ref[at]).astype(BF)

        def away(near):
            block = jnp.where(lower, count // 2, count // 2 - 1)
            end = jnp.where(lower, count - 1, 0)
            return tile_of(block if near else end, own)

        gather.run(1)
        gather.mine.wait()
        forward(tile_of(nearer, half))
        gather.run(2)
        forward(away(True))
        gather.run(3)
        forward(away(False))
        backward(away(False))
        scatter.start([0])
        backward(away(True))
        scatter.start([1])
        backward(tile_of(nearer, half))
        scatter.start([2])
        units = list(range(width // TILE))
        stages = [(step, far) for step in range(count - 1) for far in (False, True)]
        spare = len(units) - len(stages)
        for i in units[: max(spare, 0)]:
            weight_rows(i)
        rest = units[max(spare, 0) :]
        for step, far in stages:
            scatter.run(step, far)
            if rest:
                weight_rows(rest.pop(0))
        scatter.finish()
        gather.finish_sends()
        for number in range(kept - 2, kept):
            store(number).wait()

    in_vmem, anywhere = pl.BlockSpec(memory_space=pltpu.VMEM), pl.BlockSpec(memory_space=pl.ANY)
    return pl.pallas_call(
        body,
        in_specs=[in_vmem, anywhere, anywhere],
        out_specs=[in_vmem, in_vmem, anywhere],
        out_shape=[
            jax.ShapeDtypeStruct((own, width), F32),
            jax.ShapeDtypeStruct((group, width), BF),
            jax.ShapeDtypeStruct((width // 2, 3 * ff), BF),
        ],
        scratch_shapes=[
            pltpu.VMEM((width, 2 * ff), BF),
            pltpu.VMEM((width, ff), BF),
            pltpu.VMEM((group, width), BF),
            pltpu.VMEM((group, width), BF),
            pltpu.VMEM((group, ff), F32),
            pltpu.VMEM((group, ff), BF),
            pltpu.VMEM((group, 2 * ff), BF),
            pltpu.VMEM((group, width), BF),
            pltpu.VMEM((2, TILE, 3 * ff), BF),
            pltpu.VMEM((width // 2 // TILE, TILE, 3 * ff), BF),
            pltpu.SemaphoreType.DMA((3,)),
            pltpu.SemaphoreType.DMA((2,)),
            pltpu.SemaphoreType.DMA((2,)),
            pltpu.SemaphoreType.DMA((width // 2 // TILE,)),
        ]
        + Gather.scratch(count)
        + Scatter.scratch(count, own, width, PIECES),
        compiler_params=pltpu.CompilerParams(
            collective_id=number, has_side_effects=True, vmem_limit_bytes=60 * 1024 * 1024
        ),
        cost_estimate=pl.CostEstimate(
            flops=WAIT_FLOPS, bytes_accessed=width * ff * 12, transcendentals=0
        ),
        name="feed_forward",
    )(normed_own, mlp_piece, cotangent)


def join(values, parts):
    Z, rows = values[0].shape[:2]

    def body(*refs):
        ins, outs = refs[: len(values)], refs[len(values) :]
        for out_ref, (index, start, size, turns, turn) in zip(outs, parts):
            held = ins[index]
            if turns == 1:
                out_ref[...] = held[0, :, start : start + size].astype(F32)
            else:
                for j in range(size // LANES):
                    at = start + (j * turns + turn) * LANES
                    out_ref[:, j * LANES : (j + 1) * LANES] = held[0, :, at : at + LANES].astype(F32)

    return pl.pallas_call(
        body,
        grid=(Z,),
        in_specs=[pl.BlockSpec((1,) + v.shape[1:], lambda i: (i, 0, 0)) for v in values],
        out_specs=[pl.BlockSpec((rows, part[2]), lambda i: (0, i)) for part in parts],
        out_shape=[jax.ShapeDtypeStruct((rows, Z * part[2]), F32) for part in parts],
        compiler_params=pltpu.CompilerParams(dimension_semantics=("arbitrary",)),
        name="join",
    )(*values)


def local(
    tokens, doc_lengths, cotangent, attn_gain, query_weight, key_weight, value_weight, gate_weight,
    rank_in, rank_out, decay_bias, head_gain, out_weight, mlp_gain, mlp_gate_weight,
    mlp_up_weight, down_weight,
):
    own, width = tokens.shape
    rows = query_weight.shape[0]
    X, C, Z, Y = (lax.axis_size(name) for name in OWN)
    z = lax.axis_index("z")
    group = own * Z
    total = group * Y
    ff = down_weight.shape[1] // Z
    dvp = DV // Y

    def blocked(value):
        lead = value.shape[:-1]
        cut = value.reshape(lead + (X, C, Z, Y, rows))
        return jnp.swapaxes(cut, -3, -2).reshape(lead + (width,))

    def straight(value):
        found = []
        for start in range(0, width, Z * Y * rows):
            for at_z in range(Z):
                for at_y in range(Y):
                    first_lane = start + (at_y * Z + at_z) * rows
                    found.append(value[:, first_lane : first_lane + rows])
        return jnp.concatenate(found, axis=1)

    def cut_columns(weight):
        return jnp.swapaxes(weight.reshape(rows, Z, weight.shape[1] // Z), 0, 1)

    def pad_rows(value):
        flat = value.reshape(value.shape[0], -1)
        return jnp.pad(flat, ((0, rows - flat.shape[0]), (0, 0)))

    numbers = iter(range(32))

    def swap_y(value):
        return move(next(numbers), swaps=[(value, "y")])[0]

    def after(value, *others):
        return lax.optimization_barrier((value,) + others)[0]

    def to_sequence(value):
        cut = value.reshape(Y, Z, own, value.shape[-1])
        return jnp.swapaxes(cut, 0, 1).reshape(total, value.shape[-1])

    def from_sequence(value):
        cut = value.reshape(Z, Y, own, value.shape[-1])
        return jnp.swapaxes(cut, 0, 1).reshape(Y, group, value.shape[-1])

    def scatter_rest(value, axes=REST):
        sums = lax.psum_scatter(value, axes, scatter_dimension=0, tiled=True)
        return sums.reshape(Z, rows, -1)

    def gather_rest(value):
        return lax.all_gather(value.reshape(Z * rows, -1), REST, axis=0, tiled=True)

    small = jnp.concatenate(
        [
            rank_in, pad_rows(attn_gain), pad_rows(mlp_gain), pad_rows(rank_out),
            pad_rows(decay_bias), pad_rows(head_gain),
        ],
        axis=1,
    )
    small = jnp.pad(small, ((0, 0), (0, SMALL - small.shape[1])))
    first = jnp.concatenate(
        [cut_columns(w) for w in (query_weight, key_weight, value_weight, gate_weight)]
        + [jnp.broadcast_to(small[None], (Z,) + small.shape)],
        axis=2,
    )
    own_tokens = blocked(tokens)
    input_weights, group_tokens, out_weights = spread_and_gather(
        first, own_tokens, cut_columns(out_weight), (X, C, Z, Y), next(numbers)
    )
    input_weights = input_weights.reshape(width, -1)
    mlp_weights = jnp.stack(
        [
            cut_columns(w).reshape(Z, rows, ff // LANES, LANES)
            for w in (mlp_gate_weight, mlp_up_weight)
        ],
        axis=3,
    ).reshape(Z, rows, 2 * ff)
    mlp_weights = jnp.concatenate([mlp_weights, cut_columns(down_weight)], axis=2)

    projected = 2 * DK + 2 * DV
    near = 2 * DK + DV
    small_all = input_weights[:, projected:].astype(F32)

    def device_rows(value, count):
        cut = value.reshape(X, C, Y, Z, rows, -1)[:, :, :, :, : rows // count]
        return jnp.swapaxes(cut, 2, 3).reshape(width // count, -1)

    attn_gain_all = small_all[:, R]
    mlp_gain_all = small_all[:, R + 1]
    rank_out_all = device_rows(small_all[:, R + 2 : 2 * R + 2], width // (H * DK))
    bias_all = device_rows(small_all[:, 2 * R + 2 : 2 * R + 3], width // (H * DK))
    head_gain_all = device_rows(small_all[:, 2 * R + 3 : 2 * R + 4], width // DV)[:, 0]
    rank_out_z = lax.dynamic_slice_in_dim(rank_out_all, z * DK, DK).astype(BF)
    bias_z = lax.dynamic_slice_in_dim(bias_all, z * DK, DK)[:, 0]

    rows_in = group_tokens.astype(F32)
    scale_in = lax.rsqrt(jnp.mean(rows_in * rows_in, axis=1, keepdims=True) + norm_eps)
    normed_in = (rows_in * scale_in * attn_gain_all).astype(BF)
    heads = dot_plain(normed_in, input_weights)
    out_gate = heads[:, 2 * DK + DV : projected]
    low = heads.astype(BF)
    shared = jnp.concatenate([low[:, : 2 * DK], low[:, projected:]], axis=1)
    values = jnp.swapaxes(low[:, 2 * DK : 2 * DK + DV].reshape(group, Y, dvp), 0, 1)
    sent = jnp.concatenate([jnp.broadcast_to(shared[None], (Y,) + shared.shape), values], axis=2)
    sent, mlp_weights = move(next(numbers), swaps=[(sent, "y"), (mlp_weights, "z")])
    out_piece = gather_rest(out_weights)
    mlp_piece = gather_rest(mlp_weights)
    sequence = to_sequence(sent)
    queries = sequence[:, :DK]
    keys = sequence[:, DK : 2 * DK]
    rank_low = sequence[:, 2 * DK : 2 * DK + R]
    value_part = sequence[:, 2 * DK + SMALL :]
    decay_logit = dot_rows(rank_low, rank_out_z) + bias_z
    log_decay = jax.nn.log_sigmoid(decay_logit) / decay_norm

    doc_ends = jnp.cumsum(doc_lengths[0])
    positions = lax.iota(jnp.int32, total)
    segments = jnp.sum((doc_ends[None, :] <= positions[:, None]).astype(jnp.int32), axis=1)
    cut = segments.reshape(-1, CHUNK)
    last = cut[:, CHUNK - 1 :]
    before = jnp.concatenate([jnp.full((1, 1), -1, jnp.int32), last[:-1]], axis=0)
    aux = jnp.stack(
        [cut == before, cut == last, cut, jnp.broadcast_to(last == before, cut.shape)], axis=-1
    )
    aux = aux.reshape(total, 4).astype(F32)
    seg_rows = cut.astype(F32)[:, None, :]

    mixed_part, enter, scores = mix_forward(queries, keys, value_part, log_decay, aux, seg_rows)
    mixed_part = swap_y(from_sequence(mixed_part))
    mixed = jnp.swapaxes(mixed_part, 0, 1).reshape(group, DV).astype(F32)

    head_scale = lax.rsqrt(jnp.mean(mixed * mixed, axis=1, keepdims=True) + head_eps)
    head_hat = mixed * head_scale
    head_out = head_hat * head_gain_all
    sig_out = jax.nn.sigmoid(out_gate)
    silu_out = out_gate * sig_out
    gated = (head_out * silu_out).astype(BF)
    own_cotangent = blocked(cotangent)
    residual, group_cotangent = move(
        next(numbers), scatter=(dot_rows(gated, out_piece).astype(BF), "z"),
        gathers=[(own_cotangent, "z")], extras=[own_tokens],
        post=lambda total_sum, x: total_sum + x.astype(F32),
    )
    scale_mid = lax.rsqrt(jnp.mean(residual * residual, axis=1, keepdims=True) + norm_eps)
    hat_mid = residual * scale_mid
    normed_mlp = (hat_mid * mlp_gain_all).astype(BF)
    grad_normed_mlp, out_partial, mlp_partial = feed_forward(
        normed_mlp, mlp_piece, group_cotangent, next(numbers)
    )
    mlp_sums = scatter_rest(mlp_partial, ("x", "y"))

    mlp_gain_part = jnp.sum(grad_normed_mlp * hat_mid, axis=0)
    scaled = grad_normed_mlp * mlp_gain_all
    grad_residual = own_cotangent.astype(F32) + scale_mid * (
        scaled - hat_mid * jnp.mean(scaled * hat_mid, axis=1, keepdims=True)
    )
    branch_own = grad_residual.astype(BF)
    layer_out, grad_branch = move(
        next(numbers), scatter=(out_partial, "z"), gathers=[(branch_own, "z")],
        extras=[residual], post=lambda total_sum, rest: straight(total_sum + rest),
    )
    grad_gated = dot_plain(grad_branch, out_piece)
    grad_head = grad_gated * silu_out
    head_gain_part = jnp.sum(grad_head * head_hat, axis=0)
    from_head = grad_head * head_gain_all
    grad_mixed = head_scale * (
        from_head - head_hat * jnp.mean(from_head * head_hat, axis=1, keepdims=True)
    )
    grad_out_gate = (grad_gated * head_out * sig_out * (1.0 + out_gate * (1.0 - sig_out))).astype(BF)
    grad_part = to_sequence(
        swap_y(jnp.swapaxes(grad_mixed.astype(BF).reshape(group, Y, dvp), 0, 1))
    )
    dq, dk, dv, dld = mix_backward(
        queries, keys, value_part, log_decay, aux, seg_rows, enter, scores, grad_part
    )
    dlogit = (dld * jax.nn.sigmoid(-decay_logit) / decay_norm).astype(BF)
    back = from_sequence(jnp.concatenate([dq, dk, dlogit, dv], axis=1))
    side_partial = jnp.concatenate(
        [dot_cols(normed_in, grad_out_gate), dot_cols(grad_branch, gated)], axis=1
    ).astype(BF)
    back, side_partial = lax.optimization_barrier((back, side_partial))
    side_sums = scatter_rest(side_partial)
    back, mlp_rows = move(next(numbers), swaps=[(back, "y"), (mlp_sums, "z")])
    summed = jnp.sum(back[:, :, : 3 * DK].astype(F32), axis=0).astype(BF)
    grad_value = jnp.swapaxes(back[:, :, 3 * DK :], 0, 1).reshape(group, DV)
    grad_logit = summed[:, 2 * DK :]
    bias_part = jnp.sum(grad_logit.astype(F32), axis=0)
    rank_low_group = low[:, projected : projected + R]
    rank_out_part = dot_cols(grad_logit, rank_low_group)
    grad_rank = dot_plain(grad_logit, rank_out_z).astype(BF)
    grad_heads = jnp.concatenate(
        [
            summed[:, : 2 * DK], grad_value, grad_out_gate,
            jnp.pad(grad_rank, ((0, 0), (0, SMALL - R))),
        ],
        axis=1,
    )
    normed_in_partial = dot_rows(grad_heads, input_weights)
    attn_gain_part = jnp.sum(normed_in_partial * (rows_in * scale_in), axis=0)
    def to_device_rows(value, count):
        cut = value.reshape(X, C, Z, Y, rows // count, -1)
        cut = jnp.swapaxes(cut, 2, 3)
        cut = jnp.pad(cut, ((0, 0),) * 4 + ((0, rows - rows // count), (0, 0)))
        return cut.reshape(width, -1)

    def at_head(value):
        return lax.dynamic_update_slice_in_dim(
            jnp.zeros((H * DK, value.shape[1]), F32), value, z * DK, 0
        )

    near_part = dot_cols(
        normed_in, jnp.concatenate([grad_heads[:, :near], grad_heads[:, projected:]], axis=1)
    )
    small_part = jnp.concatenate(
        [
            near_part[:, near : near + R],
            attn_gain_part[:, None],
            mlp_gain_part[:, None],
            to_device_rows(at_head(rank_out_part), width // (H * DK)),
            to_device_rows(at_head(bias_part[:, None]), width // (H * DK)),
            to_device_rows(head_gain_part[:, None], width // DV),
        ],
        axis=1,
    )
    small_part = jnp.pad(small_part, ((0, 0), (0, SMALL - small_part.shape[1])))
    near_partial = jnp.concatenate([near_part[:, :near], small_part], axis=1).astype(BF)
    partial, near_partial = lax.optimization_barrier(
        (normed_in_partial.astype(BF), near_partial)
    )
    near_sums = scatter_rest(near_partial)

    def finish_tokens(back_sum, x, grad_res, gain):
        held = x.astype(F32)
        scale = lax.rsqrt(jnp.mean(held * held, axis=1, keepdims=True) + norm_eps)
        hat = held * scale
        scaled = back_sum * gain
        mean = jnp.mean(scaled * hat, axis=1, keepdims=True)
        return straight(grad_res + scale * (scaled - hat * mean))

    tokens_grad, side_rows = move(
        next(numbers), scatter=(partial, "z"), swaps=[(side_sums, "z")],
        extras=[own_tokens, grad_residual, attn_gain_all[None]], post=finish_tokens,
    )
    near_rows = move(next(numbers), swaps=[(after(near_sums, tokens_grad), "z")])[0]

    mlp_grads = join(
        [mlp_rows], [(0, 0, ff, 2, 0), (0, 0, ff, 2, 1), (0, 2 * ff, ff, 1, 0)]
    )
    query_grad, key_grad, value_grad, gate_grad, out_grad = join(
        [near_rows, side_rows],
        [
            (0, 0, DK, 1, 0), (0, DK, DK, 1, 0), (0, 2 * DK, DV, 1, 0),
            (1, 0, DV, 1, 0), (1, DV, DV, 1, 0),
        ],
    )
    small_rows = jnp.sum(near_rows[:, :, near : near + SMALL].astype(F32), axis=0)
    return (
        layer_out,
        tokens_grad,
        small_rows[:, R],
        query_grad,
        key_grad,
        value_grad,
        gate_grad,
        small_rows[:, :R],
        small_rows[: rows * H * DK // width, R + 2 : 2 * R + 2],
        small_rows[: rows * H * DK // width, 2 * R + 2],
        small_rows[: rows * DV // width, 2 * R + 3],
        out_grad,
        small_rows[:, R + 1],
        *mlp_grads,
    )


def solution(mesh):
    groups, places = mesh.shape["grp"], mesh.shape["seq"]
    wide = Mesh(mesh.devices.reshape(groups // 2, 2, H, places // H), OWN)
    split = P(OWN, None)
    line = P(OWN)
    by_sequence = P(("x", "c"), None)
    placed = (
        split, by_sequence, split, line, split, split, split, split, split, split,
        line, line, split, line, split, split, split,
    )
    return jax.shard_map(
        local,
        mesh=wide,
        in_specs=placed,
        out_specs=(
            split, split, line, split, split, split, split, split, split, line, line, split,
            line, split, split, split,
        ),
        check_vma=False,
    )
```

```python
import functools

import jax
import jax.numpy as jnp
import numpy as np
from jax import lax
from jax.experimental import pallas as pl
from jax.experimental.pallas import tpu as pltpu
from jax.sharding import Mesh
from jax.sharding import PartitionSpec as P

H = 4
DK = 256
DV = 512
R = 16
CHUNK = 128
LEVELS = 7
SMALL = 128
WAIT_FLOPS = 100_000_000
LANES = 128
TILE = 256
PIECES = 2
norm_eps = 1e-06
head_eps = 0.25
decay_norm = 16.0
BF = jnp.bfloat16
F32 = jnp.float32
REST = ("x", "c", "y")
OWN = ("x", "c", "z", "y")


def dot_plain(left, right):
    return jnp.dot(left, right, preferred_element_type=F32)


def dot_rows(left, right):
    return lax.dot_general(left, right, (((1,), (1,)), ((), ())), preferred_element_type=F32)


def dot_cols(left, right):
    return lax.dot_general(left, right, (((0,), (0,)), ((), ())), preferred_element_type=F32)


def split_two(value):
    high = value.astype(BF)
    return jnp.concatenate([high, (value - high.astype(F32)).astype(BF)], axis=1)


def sum_two(value):
    half = value.shape[1] // 2
    return value[:, :half] + value[:, half:]


def chunk_tables():
    t = np.arange(CHUNK)[:, None]
    j = np.arange(CHUNK)[None, :]
    parts = []
    level = np.full((CHUNK, CHUNK), -1, np.int32)
    for number in range(LEVELS):
        half = CHUNK >> (number + 1)
        middle = t // (2 * half) * (2 * half) + half - 1
        upper = t % (2 * half) >= half
        parts.append(np.where(upper, (j > middle) & (j <= t), (j > t) & (j <= middle)))
        pair = (t // (2 * half) == j // (2 * half)) & upper & (j % (2 * half) < half)
        level[pair] = number
    level[np.arange(CHUNK), np.arange(CHUNK)] = LEVELS
    parts.append(j <= t)
    parts.append(j > t)
    return np.concatenate(parts, axis=0).astype(np.float32), level


def upper_rows(number):
    half = CHUNK >> (number + 1)
    rows = lax.broadcasted_iota(jnp.int32, (CHUNK, 1), 0)
    return lax.rem(rows, 2 * half) >= half


def factors(ld_ref, sums_ref):
    exponents = sum_two(dot_plain(sums_ref[...], split_two(ld_ref[...])))
    return jnp.exp(exponents)


def rows_of(value, number):
    return value[number * CHUNK : (number + 1) * CHUNK]


def mix_forward_body(
    q_ref, k_ref, v_ref, ld_ref, aux_ref, seg_ref, sums_ref, level_ref,
    out_ref, enter_ref, score_ref, state,
):
    @pl.when(pl.program_id(0) == 0)
    def _():
        state[...] = jnp.zeros_like(state)

    factor = factors(ld_ref, sums_ref)
    query = q_ref[...].astype(F32) * DK ** (-0.5)
    key = k_ref[...].astype(F32)
    level = level_ref[...]
    aux = aux_ref[...]
    scores = jnp.where(level == LEVELS, dot_rows(query.astype(BF), k_ref[...]), 0.0)
    for number in range(LEVELS):
        part = rows_of(factor, number)
        pairs = dot_rows((query * part).astype(BF), (key * part).astype(BF))
        scores = jnp.where(level == number, pairs, scores)
    scores = jnp.where(aux[:, 2:3] == seg_ref[0], scores, 0.0).astype(BF)
    score_ref[0] = scores
    cumulative = rows_of(factor, LEVELS)
    enter = state[...].astype(BF)
    enter_ref[0] = enter
    lifted = (query * cumulative * aux[:, 0:1]).astype(BF)
    ending = (key * rows_of(factor, LEVELS + 1) * aux[:, 1:2]).astype(BF)
    out = dot_plain(scores, v_ref[...]) + dot_rows(lifted, enter)
    out_ref[...] = out.astype(out_ref.dtype)
    through = cumulative[CHUNK - 1 :] * aux[0:1, 3:4]
    state[...] = state[...] * through + dot_cols(v_ref[...], ending)


def mix_backward_body(
    q_ref, k_ref, v_ref, ld_ref, aux_ref, seg_ref, sums_ref, sums_t_ref, level_ref, level_t_ref,
    enter_ref, score_ref, do_ref,
    dq_ref, dk_ref, dv_ref, dld_ref, state,
):
    @pl.when(pl.program_id(0) == 0)
    def _():
        state[...] = jnp.zeros_like(state)

    factor = factors(ld_ref, sums_ref)
    scale = DK ** (-0.5)
    query = q_ref[...].astype(F32) * scale
    key = k_ref[...].astype(F32)
    value = v_ref[...]
    grad = do_ref[...]
    level = level_ref[...]
    level_t = level_t_ref[...]
    aux = aux_ref[...]
    same = aux[:, 2:3] == seg_ref[0]
    weight = jnp.where(same, dot_rows(grad, value), 0.0)
    weight_t = jnp.where(same, dot_rows(value, grad), 0.0)
    diagonal = jnp.sum(jnp.where(level == LEVELS, weight, 0.0), axis=1, keepdims=True)
    dq = diagonal * key
    dk = diagonal * query
    moved = []
    for number in range(LEVELS):
        part = rows_of(factor, number)
        left = jnp.concatenate(
            [
                jnp.where(level == number, weight, 0.0).astype(BF),
                jnp.where(level_t == number, weight_t, 0.0).astype(BF),
            ],
            axis=1,
        )
        right = jnp.concatenate([(key * part).astype(BF), (query * part).astype(BF)], axis=0)
        both = dot_plain(left, right) * part
        upper = upper_rows(number)
        dq = dq + jnp.where(upper, both, 0.0)
        dk = dk + jnp.where(upper, 0.0, both)
        moved.append(both * jnp.where(upper, query, key))
    cumulative = rows_of(factor, LEVELS)
    enter = enter_ref[0]
    after = state[...]
    after_low = after.astype(BF)
    lift = cumulative * aux[:, 0:1]
    finish = rows_of(factor, LEVELS + 1) * aux[:, 1:2]
    lifted = query * lift
    ending = key * finish
    from_enter = dot_plain(grad, enter)
    from_after = dot_plain(value, after_low)
    moved.append(lifted * from_enter)
    moved.append(ending * from_after)
    dq_ref[...] = ((dq + lift * from_enter) * scale).astype(dq_ref.dtype)
    dk_ref[...] = (dk + finish * from_after).astype(dk_ref.dtype)
    dv = dot_cols(score_ref[0], grad) + dot_rows(ending.astype(BF), after_low)
    dv_ref[...] = dv.astype(dv_ref.dtype)
    through = cumulative[CHUNK - 1 :] * aux[0:1, 3:4]
    passing = jnp.sum(after * enter.astype(F32), axis=0, keepdims=True) * through
    spread = sum_two(dot_plain(sums_t_ref[...], split_two(jnp.concatenate(moved, axis=0))))
    dld_ref[...] = spread + passing
    state[...] = after * through + dot_cols(grad, lifted.astype(BF))


def mix_specs(count, width, backward):
    def at(i):
        return count - 1 - i if backward else i

    def tokens(columns):
        return pl.BlockSpec((CHUNK, columns), lambda i: (at(i), 0))

    def chunks(rows, columns):
        return pl.BlockSpec((1, rows, columns), lambda i: (at(i), 0, 0))

    def whole(rows, columns):
        return pl.BlockSpec((rows, columns), lambda i: (0, 0))

    return tokens, chunks, whole


def mix_forward(query, key, value, log_decay, aux, seg_rows):
    total, width = value.shape
    count = total // CHUNK
    sums, level = chunk_tables()
    tokens, chunks, whole = mix_specs(count, width, False)
    return pl.pallas_call(
        mix_forward_body,
        grid=(count,),
        in_specs=[
            tokens(DK), tokens(DK), tokens(width), tokens(DK), tokens(aux.shape[1]),
            chunks(1, CHUNK), whole(*sums.shape), whole(CHUNK, CHUNK),
        ],
        out_specs=[tokens(width), chunks(width, DK), chunks(CHUNK, CHUNK)],
        out_shape=[
            jax.ShapeDtypeStruct((total, width), BF),
            jax.ShapeDtypeStruct((count, width, DK), BF),
            jax.ShapeDtypeStruct((count, CHUNK, CHUNK), BF),
        ],
        scratch_shapes=[pltpu.VMEM((width, DK), F32)],
        compiler_params=pltpu.CompilerParams(
            dimension_semantics=("arbitrary",), vmem_limit_bytes=32 * 1024 * 1024
        ),
        cost_estimate=pl.CostEstimate(
            flops=total * 2 * (8 * CHUNK * DK + 2 * width * DK + CHUNK * width + 18 * CHUNK * DK),
            bytes_accessed=total * 4096, transcendentals=total * 9 * DK,
        ),
        name="mix_forward",
    )(query, key, value, log_decay, aux, seg_rows, jnp.asarray(sums, BF), jnp.asarray(level))


def mix_backward(query, key, value, log_decay, aux, seg_rows, enter, scores, grad):
    total, width = value.shape
    count = total // CHUNK
    sums, level = chunk_tables()
    tokens, chunks, whole = mix_specs(count, width, True)
    return pl.pallas_call(
        mix_backward_body,
        grid=(count,),
        in_specs=[
            tokens(DK), tokens(DK), tokens(width), tokens(DK), tokens(aux.shape[1]),
            chunks(1, CHUNK), whole(*sums.shape), whole(*sums.shape[::-1]),
            whole(CHUNK, CHUNK), whole(CHUNK, CHUNK),
            chunks(width, DK), chunks(CHUNK, CHUNK), tokens(width),
        ],
        out_specs=[tokens(DK), tokens(DK), tokens(width), tokens(DK)],
        out_shape=[
            jax.ShapeDtypeStruct((total, DK), BF),
            jax.ShapeDtypeStruct((total, DK), BF),
            jax.ShapeDtypeStruct((total, width), BF),
            jax.ShapeDtypeStruct((total, DK), F32),
        ],
        scratch_shapes=[pltpu.VMEM((width, DK), F32)],
        compiler_params=pltpu.CompilerParams(
            dimension_semantics=("arbitrary",), vmem_limit_bytes=48 * 1024 * 1024
        ),
        cost_estimate=pl.CostEstimate(
            flops=total * 2 * (14 * CHUNK * DK + 4 * width * DK + CHUNK * width + 36 * CHUNK * DK),
            bytes_accessed=total * 6144, transcendentals=total * 9 * DK,
        ),
        name="mix_backward",
    )(
        query, key, value, log_decay, aux, seg_rows, jnp.asarray(sums, BF),
        jnp.asarray(np.ascontiguousarray(sums.T), BF), jnp.asarray(level),
        jnp.asarray(np.ascontiguousarray(level.T)), enter, scores, grad,
    )


def remote(source, target, send, arrive, axis, place):
    return pltpu.make_async_remote_copy(
        src_ref=source, dst_ref=target, send_sem=send, recv_sem=arrive,
        device_id={axis: place}, device_id_type=pl.DeviceIdType.MESH,
    )


def greet(peers):
    barrier = pltpu.get_barrier_semaphore()
    number = 0
    for present, peer in peers:
        if present is True:
            pl.semaphore_signal(
                barrier, inc=1, device_id=peer, device_id_type=pl.DeviceIdType.MESH
            )
            number = number + 1
        else:

            @pl.when(present)
            def _():
                pl.semaphore_signal(
                    barrier, inc=1, device_id=peer, device_id_type=pl.DeviceIdType.MESH
                )

            number = number + jnp.where(present, 1, 0)
    pl.semaphore_wait(barrier, number)


def line_peers(axis, count):
    me = lax.axis_index(axis)
    return [(me > 0, {axis: me - 1}), (me < count - 1, {axis: me + 1})]


def all_peers(axis, count):
    me = lax.axis_index(axis)
    return [(True, {axis: lax.rem(me + away, count)}) for away in range(1, count)]


class Gather:
    def __init__(self, axis, count, x_ref, out_ref, send, arrive, local_sem):
        self.axis, self.count, self.x_ref, self.out_ref = axis, count, x_ref, out_ref
        self.send, self.arrive = send, arrive
        self.me = lax.axis_index(axis)
        self.mine = pltpu.make_async_copy(x_ref, self.block(self.me), local_sem)

    def block(self, index):
        own = self.x_ref.shape[0]
        return self.out_ref.at[pl.ds(pl.multiple_of(index * own, own), own)]

    def copy(self, direction, step, index, source):
        return remote(
            source, self.block(index), self.send.at[direction, step],
            self.arrive.at[direction, step], self.axis,
            self.me + 1 if direction == 0 else self.me - 1,
        )

    def hop(self, direction, step):
        index = self.me - step if direction == 0 else self.me + step
        return self.copy(direction, step, index, self.x_ref if step == 0 else self.block(index))

    def landed(self, direction, step):
        index = self.me - 1 - step if direction == 0 else self.me + 1 + step
        return self.copy(direction, step, index, self.block(index))

    def holds(self, direction, step):
        return self.me - step >= 0 if direction == 0 else self.me + step <= self.count - 1

    def hands_on(self, direction, step):
        inner = self.me < self.count - 1 if direction == 0 else self.me > 0
        return self.holds(direction, step) & inner

    def start(self):
        self.mine.start()
        self.run(0)

    def run(self, first, last=None):
        for step in range(first, first + 1 if last is None else last):
            for direction in (0, 1):
                if step > 0:

                    @pl.when(self.holds(direction, step))
                    def _():
                        self.landed(direction, step - 1).wait_recv()

                if step < self.count - 1:

                    @pl.when(self.hands_on(direction, step))
                    def _():
                        self.hop(direction, step).start()

    def finish(self):
        self.finish_sends()
        self.mine.wait()

    def finish_sends(self):
        for step in range(self.count - 1):
            for direction in (0, 1):

                @pl.when(self.hands_on(direction, step))
                def _():
                    self.hop(direction, step).wait_send()

    @staticmethod
    def scratch(count):
        return [
            pltpu.SemaphoreType.DMA((2, count - 1)),
            pltpu.SemaphoreType.DMA((2, count - 1)),
            pltpu.SemaphoreType.DMA,
        ]


class Swap:
    def __init__(self, axis, count, x_ref, out_ref, send, arrive, local_sem):
        self.axis, self.count, self.x_ref, self.out_ref = axis, count, x_ref, out_ref
        self.send, self.arrive = send, arrive
        self.me = lax.axis_index(axis)
        self.mine = pltpu.make_async_copy(x_ref.at[self.me], out_ref.at[self.me], local_sem)

    def hop(self, away):
        peer = lax.rem(self.me + away, self.count)
        return remote(
            self.x_ref.at[peer], self.out_ref.at[self.me], self.send.at[away - 1],
            self.arrive.at[away - 1], self.axis, peer,
        )

    def landed(self, away):
        peer = lax.rem(self.me + self.count - away, self.count)
        return remote(
            self.x_ref.at[peer], self.out_ref.at[peer], self.send.at[away - 1],
            self.arrive.at[away - 1], self.axis, peer,
        )

    def start(self):
        self.mine.start()
        for away in range(1, self.count):
            self.hop(away).start()

    def finish(self):
        for away in range(1, self.count):
            self.landed(away).wait_recv()
        for away in range(1, self.count):
            self.hop(away).wait_send()
        self.mine.wait()

    @staticmethod
    def scratch(count):
        return [
            pltpu.SemaphoreType.DMA((count - 1,)),
            pltpu.SemaphoreType.DMA((count - 1,)),
            pltpu.SemaphoreType.DMA,
        ]


class Scatter:
    def __init__(self, axis, count, pieces, x_ref, out_ref, up, down, send, arrive):
        self.axis, self.count, self.pieces = axis, count, pieces
        self.x_ref, self.out_ref, self.held_refs = x_ref, out_ref, (up, down)
        self.send, self.arrive = send, arrive
        self.me = lax.axis_index(axis)
        self.own = out_ref.shape[0]
        self.size = self.own // pieces

    def part(self, index, piece):
        start = pl.multiple_of(index * self.own + piece * self.size, self.size)
        return self.x_ref.at[pl.ds(start, self.size)]

    def held(self, direction, number, piece):
        return self.held_refs[direction].at[number, pl.ds(piece * self.size, self.size)]

    def hop(self, direction, number, piece, source=None):
        held = self.held(direction, number, piece)
        return remote(
            held if source is None else source, held, self.send.at[direction, number, piece],
            self.arrive.at[direction, number, piece], self.axis,
            self.me + 1 if direction == 0 else self.me - 1,
        )

    def target(self, direction, number):
        return self.count - 1 - number if direction == 0 else number

    def start(self, numbers=None):
        for direction in (0, 1):

            @pl.when(self.me == (0 if direction == 0 else self.count - 1))
            def _():
                for number in range(self.count - 1) if numbers is None else numbers:
                    target = self.target(direction, number)
                    for piece in range(self.pieces):
                        self.hop(direction, number, piece, self.part(target, piece)).start()

    def stage(self, direction, number, piece):
        me, target = self.me, self.target(direction, number)
        inner = me > 0 if direction == 0 else me < self.count - 1
        passed = me < target if direction == 0 else me > target
        held = self.held(direction, number, piece)

        @pl.when(inner & (passed | (me == target)))
        def _():
            self.hop(direction, number, piece).wait_recv()

        @pl.when(inner & passed)
        def _():
            mine = self.part(target, piece)[...].astype(F32)
            held[...] = (held[...].astype(F32) + mine).astype(BF)
            self.hop(direction, number, piece).start()

    def run(self, number, far):
        for order in (0, 1):

            @pl.when((self.me >= self.count // 2) == (order == 1))
            def _():
                for piece in range(self.pieces):
                    self.stage(1 - order if far else order, number, piece)

    def finish(self):
        me, count, out_ref = self.me, self.count, self.out_ref
        for piece in range(self.pieces):
            rows = pl.ds(piece * self.size, self.size)
            out_ref[rows] = self.part(me, piece)[...].astype(F32)
            for direction in (0, 1):
                for number in range(count - 1):
                    inner = me > 0 if direction == 0 else me < count - 1

                    @pl.when((me == self.target(direction, number)) & inner)
                    def _():
                        out_ref[rows] += self.held(direction, number, piece)[...].astype(F32)

        for direction in (0, 1):
            for number in range(count - 1):
                target = self.target(direction, number)

                @pl.when(me < target if direction == 0 else me > target)
                def _():
                    for piece in range(self.pieces):
                        self.hop(direction, number, piece).wait_send()

    @staticmethod
    def scratch(count, own, columns, pieces):
        return [
            pltpu.VMEM((count - 1, own, columns), BF),
            pltpu.VMEM((count - 1, own, columns), BF),
            pltpu.SemaphoreType.DMA((2, count - 1, pieces)),
            pltpu.SemaphoreType.DMA((2, count - 1, pieces)),
        ]


class CutSwap:
    def __init__(self, axis, count, refs, out_ref, send, arrive, local_sem):
        self.axis, self.count, self.refs, self.out_ref = axis, count, refs, out_ref
        self.send, self.arrive = send, arrive
        self.me = lax.axis_index(axis)
        self.widths = [ref.shape[1] // count for ref in refs]
        self.mine = [
            pltpu.make_async_copy(self.cut(i, self.me), self.slot(i, self.me), local_sem.at[i])
            for i in range(len(refs))
        ]

    def cut(self, i, index):
        size = self.widths[i]
        return self.refs[i].at[:, pl.ds(pl.multiple_of(index * size, LANES), size)]

    def slot(self, i, index):
        return self.out_ref.at[index, :, pl.ds(sum(self.widths[:i]), self.widths[i])]

    def hop(self, away, i):
        peer = lax.rem(self.me + away, self.count)
        return remote(
            self.cut(i, peer), self.slot(i, self.me), self.send.at[away - 1, i],
            self.arrive.at[away - 1, i], self.axis, peer,
        )

    def landed(self, away, i):
        peer = lax.rem(self.me + self.count - away, self.count)
        return remote(
            self.cut(i, peer), self.slot(i, peer), self.send.at[away - 1, i],
            self.arrive.at[away - 1, i], self.axis, peer,
        )

    def each(self):
        return [(away, i) for away in range(1, self.count) for i in range(len(self.refs))]

    def start(self):
        for away, i in self.each():
            self.hop(away, i).start()
        for copy in self.mine:
            copy.start()

    def finish(self):
        for away, i in self.each():
            self.landed(away, i).wait_recv()
        for away, i in self.each():
            self.hop(away, i).wait_send()
        for copy in self.mine:
            copy.wait()

    @staticmethod
    def scratch(count, parts):
        sems = pltpu.SemaphoreType.DMA((count - 1, parts))
        return [sems, sems, pltpu.SemaphoreType.DMA((parts,))]


class Deal:
    def __init__(self, axis, count, forth, x_ref, out_ref, send, arrive, local_sem):
        self.axis, self.count, self.forth = axis, count, forth
        self.x_ref, self.out_ref, self.send, self.arrive = x_ref, out_ref, send, arrive
        self.me = lax.axis_index(axis)
        self.steps = x_ref.shape[1] if forth else x_ref.shape[0]
        self.mine = [
            pltpu.make_async_copy(self.given(self.me, k), self.got(self.me, k), local_sem.at[k])
            for k in range(self.steps)
        ]

    def given(self, device, k):
        return self.x_ref.at[device, k] if self.forth else self.x_ref.at[k, device]

    def got(self, device, k):
        return self.out_ref.at[k, device] if self.forth else self.out_ref.at[device, k]

    def hop(self, away, k):
        peer = lax.rem(self.me + away, self.count)
        return remote(
            self.given(peer, k), self.got(self.me, k), self.send.at[away - 1, k],
            self.arrive.at[away - 1, k], self.axis, peer,
        )

    def landed(self, away, k):
        peer = lax.rem(self.me + self.count - away, self.count)
        return remote(
            self.given(peer, k), self.got(peer, k), self.send.at[away - 1, k],
            self.arrive.at[away - 1, k], self.axis, peer,
        )

    def each(self):
        return [(away, k) for away in range(1, self.count) for k in range(self.steps)]

    def start(self):
        for away, k in self.each():
            self.hop(away, k).start()
        for copy in self.mine:
            copy.start()

    def finish(self):
        for away, k in self.each():
            self.landed(away, k).wait_recv()
        for away, k in self.each():
            self.hop(away, k).wait_send()
        for copy in self.mine:
            copy.wait()

    @staticmethod
    def scratch(count, steps):
        sems = pltpu.SemaphoreType.DMA((count - 1, steps))
        return [sems, sems, pltpu.SemaphoreType.DMA((steps,))]


class Spread:
    def __init__(self, sizes, cuts, out_ref, far_send, far_arrive, near_send, near_arrive):
        self.X, self.C, self.Z, self.Y = sizes
        self.cuts, self.out_ref = cuts, out_ref
        self.far_send, self.far_arrive = far_send, far_arrive
        self.near_send, self.near_arrive = near_send, near_arrive
        self.x, self.c, self.z, self.y = (lax.axis_index(name) for name in OWN)
        self.others = self.X * self.Y - 1

    def across(self, offset, sign):
        down, right = offset // self.Y, offset % self.Y
        if sign < 0:
            down, right = self.X - down, self.Y - right
        return lax.rem(self.x + down, self.X), lax.rem(self.y + right, self.Y)

    def place(self, offset, c, slot):
        x, y = self.across(offset, -1)
        z = lax.rem(self.z + self.Z - slot, self.Z)
        return self.out_ref.at[((x * self.C + c) * self.Y + y) * self.Z + z]

    def far(self, offset, slot, landed=False):
        x, y = self.across(offset, 1)
        held = self.place(offset if landed else 0, self.c, slot)
        return pltpu.make_async_remote_copy(
            src_ref=held, dst_ref=held, send_sem=self.far_send.at[offset - 1, slot],
            recv_sem=self.far_arrive.at[offset - 1, slot], device_id={"x": x, "y": y},
            device_id_type=pl.DeviceIdType.MESH,
        )

    def near(self, offset, slot, landed=False):
        held = self.place(offset, 1 - self.c if landed else self.c, slot)
        return remote(
            held, held, self.near_send.at[offset, slot],
            self.near_arrive.at[offset, slot], "c", 1 - self.c,
        )

    def peers(self):
        found = all_peers("z", self.Z) + [(True, {"c": 1 - self.c})]
        for offset in range(1, self.others + 1):
            x, y = self.across(offset, 1)
            found.append((True, {"x": x, "y": y}))
        return found

    def hand_on(self, slot):
        for i in range(len(self.cuts.refs)):
            if slot > 0:
                self.cuts.landed(slot, i).wait_recv()
            else:
                self.cuts.mine[i].wait()
        for offset in range(1, self.others + 1):
            self.far(offset, slot).start()
        self.near(0, slot).start()

    def collect(self, slot):
        for offset in range(1, self.others + 1):
            self.far(offset, slot, True).wait_recv()
            self.near(offset, slot).start()

    def finish(self):
        for slot in range(self.Z):
            for offset in range(self.others + 1):
                self.near(offset, slot, True).wait_recv()
        for slot in range(self.Z):
            for offset in range(self.others + 1):
                self.near(offset, slot).wait_send()
                if offset > 0:
                    self.far(offset, slot).wait_send()
        for away, i in self.cuts.each():
            self.cuts.hop(away, i).wait_send()

    @staticmethod
    def scratch(sizes):
        X, C, Z, Y = sizes
        far = pltpu.SemaphoreType.DMA((max(X * Y - 1, 1), Z))
        near = pltpu.SemaphoreType.DMA((X * Y, Z))
        return [far, far, near, near]


class FirstCuts(CutSwap):
    def __init__(self, spread_place, count, refs, out_ref, send, arrive, local_sem):
        self.place = spread_place
        super().__init__("z", count, refs, out_ref, send, arrive, local_sem)

    def cut(self, i, index):
        return self.refs[i] if i == len(self.refs) - 1 else super().cut(i, index)

    def slot(self, i, index):
        widths = [w for w in self.widths[:-1]] + [SMALL]
        return self.out_ref.at[self.place(index), :, pl.ds(sum(widths[:i]), widths[i])]


def spread_and_gather(weights, block, other, sizes, number):
    X, C, Z, Y = sizes
    parts = len(weights)
    rows = weights[0].shape[0]
    total = sum(w.shape[1] // Z for w in weights[:-1]) + weights[-1].shape[1]

    def body(*refs):
        w_refs, x_ref, o_ref = refs[:parts], refs[parts], refs[parts + 1]
        spread_ref, out_ref, swapped_ref = refs[parts + 2 : parts + 5]
        sems = refs[parts + 5 :]
        x, c, _, y = (lax.axis_index(name) for name in OWN)
        first = FirstCuts(
            lambda index: ((x * C + c) * Y + y) * Z + index, Z, w_refs, spread_ref, *sems[:3]
        )
        spread = Spread(sizes, first, spread_ref, *sems[3:7])
        gather = Gather("z", Z, x_ref, out_ref, *sems[7:10])
        swap = CutSwap("z", Z, [o_ref], swapped_ref, *sems[10:])
        greet(spread.peers())
        first.start()
        gather.start()
        spread.hand_on(0)
        for slot in range(1, Z):
            spread.hand_on(slot)
        for step in range(1, Z):
            gather.run(step)
            if step == Z - 2:
                swap.start()
            spread.collect(step - 1)
        spread.collect(Z - 1)
        spread.finish()
        gather.finish()
        swap.finish()

    anywhere = pl.BlockSpec(memory_space=pl.ANY)
    return pl.pallas_call(
        body,
        in_specs=[anywhere] * (parts + 2),
        out_specs=[anywhere] * 3,
        out_shape=[
            jax.ShapeDtypeStruct((X * C * Y * Z, rows, total), BF),
            jax.ShapeDtypeStruct((Z * block.shape[0],) + block.shape[1:], block.dtype),
            jax.ShapeDtypeStruct((Z, rows, other.shape[1] // Z), BF),
        ],
        scratch_shapes=CutSwap.scratch(Z, parts)
        + Spread.scratch(sizes)
        + Gather.scratch(Z)
        + CutSwap.scratch(Z, 1),
        compiler_params=pltpu.CompilerParams(collective_id=number, has_side_effects=True),
        cost_estimate=pl.CostEstimate(
            flops=WAIT_FLOPS, bytes_accessed=rows * total * X * C * Y * Z * 2, transcendentals=0
        ),
        name="spread_and_gather",
    )(*weights, block, other)


def move(
    number, scatter=None, swaps=(), gathers=(), cuts=(), deals=(), extras=(), post=None
):
    in_vmem, anywhere = pl.BlockSpec(memory_space=pltpu.VMEM), pl.BlockSpec(memory_space=pl.ANY)
    values, in_specs, shapes, out_specs, scratch = [], [], [], [], []
    flags = {}

    def scale(axis):
        return lax.axis_size(axis)

    if scatter is not None:
        partial, axis = scatter
        own = partial.shape[0] // scale(axis)
        values += [partial, *extras]
        in_specs += [in_vmem] * (1 + len(extras))
        shapes.append(jax.ShapeDtypeStruct((own, partial.shape[1]), F32))
        out_specs.append(in_vmem)
        scratch += Scatter.scratch(scale(axis), own, partial.shape[1], PIECES)
        flags = dict(vmem_limit_bytes=40 * 1024 * 1024)
    for value, axis in swaps:
        values.append(value)
        in_specs.append(anywhere)
        shapes.append(jax.ShapeDtypeStruct(value.shape, value.dtype))
        out_specs.append(anywhere)
        scratch += Swap.scratch(scale(axis))
    for block, axis in gathers:
        values.append(block)
        in_specs.append(anywhere)
        shapes.append(
            jax.ShapeDtypeStruct((scale(axis) * block.shape[0], block.shape[1]), block.dtype)
        )
        out_specs.append(anywhere)
        scratch += Gather.scratch(scale(axis))

    for weights, axis in cuts:
        values += weights
        in_specs += [anywhere] * len(weights)
        wide = sum(w.shape[1] for w in weights) // scale(axis)
        shapes.append(
            jax.ShapeDtypeStruct((scale(axis), weights[0].shape[0], wide), weights[0].dtype)
        )
        out_specs.append(anywhere)
        scratch += CutSwap.scratch(scale(axis), len(weights))
    for value, axis, forth in deals:
        first, second = value.shape[:2]
        values.append(value)
        in_specs.append(anywhere)
        shapes.append(jax.ShapeDtypeStruct((second, first) + value.shape[2:], value.dtype))
        out_specs.append(anywhere)
        scratch += Deal.scratch(scale(axis), second if forth else first)

    def body(*refs):
        ins = list(refs[: len(values)])
        outs = list(refs[len(values) : len(values) + len(shapes)])
        sems = list(refs[len(values) + len(shapes) :])
        peers = {}
        adding, extra_refs, swapping, gathering = None, (), [], []
        if scatter is not None:
            axis = scatter[1]
            adding = Scatter(axis, scale(axis), PIECES, ins.pop(0), outs.pop(0), *sems[:4])
            extra_refs, ins, sems = ins[: len(extras)], ins[len(extras) :], sems[4:]
            peers[axis] = line_peers(axis, scale(axis))
        for _, axis in gathers:
            peers[axis] = line_peers(axis, scale(axis))
        for _, axis in swaps:
            peers[axis] = all_peers(axis, scale(axis))
            swapping.append(Swap(axis, scale(axis), ins.pop(0), outs.pop(0), *sems[:3]))
            sems = sems[3:]
        for _, axis in gathers:
            gathering.append(Gather(axis, scale(axis), ins.pop(0), outs.pop(0), *sems[:3]))
            sems = sems[3:]
        for weights, axis in cuts:
            peers[axis] = all_peers(axis, scale(axis))
            taken, ins = ins[: len(weights)], ins[len(weights) :]
            swapping.append(CutSwap(axis, scale(axis), taken, outs.pop(0), *sems[:3]))
            sems = sems[3:]
        for _, axis, forth in deals:
            peers[axis] = all_peers(axis, scale(axis))
            swapping.append(
                Deal(axis, scale(axis), forth, ins.pop(0), outs.pop(0), *sems[:3])
            )
            sems = sems[3:]
        greet([peer for found in peers.values() for peer in found])
        for part in gathering + ([adding] if adding else []) + swapping:
            part.start()
        steps = max([part.count for part in gathering + ([adding] if adding else [])] + [0])
        for part in gathering:
            part.run(1)
        for step in range(1, steps):
            if adding:
                adding.run(step - 1, False)
            for part in gathering:
                if step + 1 < part.count:
                    part.run(step + 1)
            if adding:
                adding.run(step - 1, True)
        if adding:
            adding.finish()
            if post is not None:
                adding.out_ref[...] = post(adding.out_ref[...], *[r[...] for r in extra_refs])
        for part in swapping + gathering:
            part.finish()

    size = sum(v.size for v in values)
    return pl.pallas_call(
        body,
        in_specs=in_specs,
        out_specs=out_specs,
        out_shape=shapes,
        scratch_shapes=scratch,
        compiler_params=pltpu.CompilerParams(
            collective_id=number, has_side_effects=True, **flags
        ),
        cost_estimate=pl.CostEstimate(
            flops=WAIT_FLOPS, bytes_accessed=size * 4, transcendentals=0
        ),
        name="move",
    )(*values)


def feed_forward(normed_own, mlp_piece, cotangent, number):
    count = lax.axis_size("z")
    own, width = normed_own.shape
    group, ff = own * count, mlp_piece.shape[1] // 3
    half = group // 2
    places = lax.axis_size("x")
    block = width // (2 * places)
    per = block // TILE

    def body(x_ref, w_hbm, c_hbm, sum_ref, down_ref, grad_hbm,
             w_ref, d_ref, c_ref, normed, hidden_grad, hidden, grads, partial, stage, received,
             load_sem, hand_send, hand_arrive, store_sem, pair_send, pair_arrive, gather_send, gather_arrive, local_sem, up, down, send, arrive):
        me, core = lax.axis_index("z"), lax.axis_index("c")
        load_c = pltpu.make_async_copy(c_hbm, c_ref, load_sem.at[2 * places])

        def weights(place, late, by):
            rows = pl.ds(pl.multiple_of((place * 2 + by) * block, block), block)
            target = (w_ref if late else d_ref).at[rows]
            at = pl.ds(0, 2 * ff) if late else pl.ds(2 * ff, ff)
            return w_hbm.at[pl.ds(place * block, block), at], target

        def load(place, late):
            return pltpu.make_async_copy(
                *weights(place, late, core), load_sem.at[place * 2 + late]
            )

        def hand(place, late, by=core):
            return remote(
                *weights(place, late, by), hand_send.at[place, late], hand_arrive.at[place, late],
                "c", 1 - core,
            )

        def loaded(late):
            for place in range(places):
                load(place, late).wait()
                hand(place, late, 1 - core).wait_recv()

        load_c.start()
        gather = Gather("z", count, x_ref, normed, gather_send, gather_arrive, local_sem)
        scatter = Scatter("z", count, PIECES, partial, sum_ref, up, down, send, arrive)
        greet(line_peers("z", count) + [(True, {"c": 1 - core})])
        gather.start()
        for late in (0, 1):
            for place in range(places):
                load(place, late).start()
                hand(place, late).start()
        load_c.wait()
        loaded(0)

        def tile_of(index, size):
            return pl.ds(pl.multiple_of(index * size, size), size)

        def spans(total):
            return [pl.ds(at, min(TILE, total - at)) for at in range(0, total, TILE)]

        for at in spans(ff):
            hidden_grad[:, at] = dot_plain(c_ref[...], d_ref[:, at])
        loaded(1)
        lower = me < count // 2
        nearer = me // (count // 2)

        def forward(rows):
            for at in spans(ff):
                up_at = pl.ds(ff + at.start, at.size)
                gate = dot_plain(normed[rows], w_ref[:, at])
                upper = dot_plain(normed[rows], w_ref[:, up_at])
                grad = hidden_grad[rows, at]
                sig = jax.nn.sigmoid(gate)
                silu = gate * sig
                hidden[rows, at] = (silu * upper).astype(BF)
                grad_gate = grad * upper * sig * (1.0 + gate * (1.0 - sig))
                grads[rows, at] = grad_gate.astype(BF)
                grads[rows, up_at] = (grad * silu).astype(BF)

        def backward(rows):
            for at in spans(width):
                partial[rows, at] = dot_rows(grads[rows], w_ref[at]).astype(BF)

        kept = width // 2 // TILE

        def rows_kept(number, by):
            start = (number // per * 2 + by) * block + number % per * TILE
            return pl.ds(pl.multiple_of(start, TILE), TILE)

        def store(number):
            return pltpu.make_async_copy(
                stage.at[number % 2], grad_hbm.at[pl.ds(number * TILE, TILE)],
                store_sem.at[number % 2],
            )

        def pass_over(number):
            return remote(
                stage.at[number % 2], received.at[number], pair_send.at[number % 2],
                pair_arrive.at[number], "c", 1 - core,
            )

        def weight_rows(i):
            ours, number = i >= kept, i % kept
            if i >= 2:
                if i - 2 >= kept:
                    store(i - 2 - kept).wait()
                else:
                    pass_over(i - 2).wait_send()
            at = rows_kept(number, core if ours else 1 - core)
            slot = i % 2
            top = dot_cols(normed[:, at], grads[...])
            low = dot_cols(c_ref[:, at], hidden[...])
            if ours:
                pass_over(number).wait_recv()
                top = top + received[number, :, : 2 * ff].astype(F32)
                low = low + received[number, :, 2 * ff :].astype(F32)
            stage[slot, :, : 2 * ff] = top.astype(BF)
            stage[slot, :, 2 * ff :] = low.astype(BF)
            if ours:
                store(number).start()
            else:
                pass_over(number).start()
            at = pl.ds(i * TILE, TILE)
            down_ref[:, at] = dot_rows(hidden[...], d_ref[at]).astype(BF)

        def away(near):
            block = jnp.where(lower, count // 2, count // 2 - 1)
            end = jnp.where(lower, count - 1, 0)
            return tile_of(block if near else end, own)

        gather.run(1)
        gather.mine.wait()
        forward(tile_of(nearer, half))
        gather.run(2)
        forward(away(True))
        gather.run(3)
        forward(away(False))
        backward(away(False))
        scatter.start([0])
        backward(away(True))
        scatter.start([1])
        backward(tile_of(nearer, half))
        scatter.start([2])
        units = list(range(width // TILE))
        stages = [(step, far) for step in range(count - 1) for far in (False, True)]
        spare = len(units) - len(stages)
        for i in units[: max(spare, 0)]:
            weight_rows(i)
        rest = units[max(spare, 0) :]
        for step, far in stages:
            scatter.run(step, far)
            if rest:
                weight_rows(rest.pop(0))
        scatter.finish()
        gather.finish_sends()
        for place in range(places):
            for late in (0, 1):
                hand(place, late).wait_send()
        for number in range(kept - 2, kept):
            store(number).wait()

    in_vmem, anywhere = pl.BlockSpec(memory_space=pltpu.VMEM), pl.BlockSpec(memory_space=pl.ANY)
    return pl.pallas_call(
        body,
        in_specs=[in_vmem, anywhere, anywhere],
        out_specs=[in_vmem, in_vmem, anywhere],
        out_shape=[
            jax.ShapeDtypeStruct((own, width), F32),
            jax.ShapeDtypeStruct((group, width), BF),
            jax.ShapeDtypeStruct((width // 2, 3 * ff), BF),
        ],
        scratch_shapes=[
            pltpu.VMEM((width, 2 * ff), BF),
            pltpu.VMEM((width, ff), BF),
            pltpu.VMEM((group, width), BF),
            pltpu.VMEM((group, width), BF),
            pltpu.VMEM((group, ff), F32),
            pltpu.VMEM((group, ff), BF),
            pltpu.VMEM((group, 2 * ff), BF),
            pltpu.VMEM((group, width), BF),
            pltpu.VMEM((2, TILE, 3 * ff), BF),
            pltpu.VMEM((width // 2 // TILE, TILE, 3 * ff), BF),
            pltpu.SemaphoreType.DMA((2 * places + 1,)),
            pltpu.SemaphoreType.DMA((places, 2)),
            pltpu.SemaphoreType.DMA((places, 2)),
            pltpu.SemaphoreType.DMA((2,)),
            pltpu.SemaphoreType.DMA((2,)),
            pltpu.SemaphoreType.DMA((width // 2 // TILE,)),
        ]
        + Gather.scratch(count)
        + Scatter.scratch(count, own, width, PIECES),
        compiler_params=pltpu.CompilerParams(
            collective_id=number, has_side_effects=True, vmem_limit_bytes=60 * 1024 * 1024
        ),
        cost_estimate=pl.CostEstimate(
            flops=WAIT_FLOPS, bytes_accessed=width * ff * 12, transcendentals=0
        ),
        name="feed_forward",
    )(normed_own, mlp_piece, cotangent)


def join(values, parts):
    Z, rows = values[0].shape[:2]

    def body(*refs):
        ins, outs = refs[: len(values)], refs[len(values) :]
        for out_ref, (index, start, size) in zip(outs, parts):
            out_ref[...] = ins[index][0, :, start : start + size].astype(F32)

    return pl.pallas_call(
        body,
        grid=(Z,),
        in_specs=[pl.BlockSpec((1,) + v.shape[1:], lambda i: (i, 0, 0)) for v in values],
        out_specs=[pl.BlockSpec((rows, part[2]), lambda i: (0, i)) for part in parts],
        out_shape=[jax.ShapeDtypeStruct((rows, Z * part[2]), F32) for part in parts],
        compiler_params=pltpu.CompilerParams(dimension_semantics=("arbitrary",)),
        name="join",
    )(*values)


def local(
    tokens, doc_lengths, cotangent, attn_gain, query_weight, key_weight, value_weight, gate_weight,
    rank_in, rank_out, decay_bias, head_gain, out_weight, mlp_gain, mlp_gate_weight,
    mlp_up_weight, down_weight,
):
    own, width = tokens.shape
    rows = query_weight.shape[0]
    X, C, Z, Y = (lax.axis_size(name) for name in OWN)
    z = lax.axis_index("z")
    group = own * Z
    total = group * Y
    ff = down_weight.shape[1] // Z
    dvp = DV // Y

    def blocked(value):
        lead = value.shape[:-1]
        cut = value.reshape(lead + (X, C, Z, Y, rows))
        return jnp.swapaxes(cut, -3, -2).reshape(lead + (width,))

    def straight(value):
        found = []
        for start in range(0, width, Z * Y * rows):
            for at_z in range(Z):
                for at_y in range(Y):
                    first_lane = start + (at_y * Z + at_z) * rows
                    found.append(value[:, first_lane : first_lane + rows])
        return jnp.concatenate(found, axis=1)

    def pad_rows(value):
        flat = value.reshape(value.shape[0], -1)
        return jnp.pad(flat, ((0, rows - flat.shape[0]), (0, 0)))

    numbers = iter(range(32))

    def deal(value, forth):
        return move(next(numbers), deals=[(value, "y", forth)])[0]

    def after(value, *others):
        return lax.optimization_barrier((value,) + others)[0]

    def scatter_rest(value, axes=REST):
        sums = lax.psum_scatter(value, axes, scatter_dimension=0, tiled=True)
        return sums.reshape(Z, rows, -1)

    def gather_rest(value, axes=REST):
        return lax.all_gather(value.reshape(Z * rows, -1), axes, axis=0, tiled=True)

    small = jnp.concatenate(
        [
            rank_in, pad_rows(attn_gain), pad_rows(mlp_gain), pad_rows(rank_out),
            pad_rows(decay_bias), pad_rows(head_gain),
        ],
        axis=1,
    )
    small = jnp.pad(small, ((0, 0), (0, SMALL - small.shape[1])))
    own_tokens = blocked(tokens)
    input_weights, group_tokens, out_weights = spread_and_gather(
        [query_weight, key_weight, value_weight, gate_weight, small],
        own_tokens, out_weight, (X, C, Z, Y), next(numbers),
    )
    input_weights = input_weights.reshape(width, -1)

    projected = 2 * DK + 2 * DV
    near = 2 * DK + DV
    small_all = input_weights[:, projected:].astype(F32)

    def device_rows(value, count):
        cut = value.reshape(X, C, Y, Z, rows, -1)[:, :, :, :, : rows // count]
        return jnp.swapaxes(cut, 2, 3).reshape(width // count, -1)

    attn_gain_all = small_all[:, R]
    mlp_gain_all = small_all[:, R + 1]
    rank_out_all = device_rows(small_all[:, R + 2 : 2 * R + 2], width // (H * DK))
    bias_all = device_rows(small_all[:, 2 * R + 2 : 2 * R + 3], width // (H * DK))
    head_gain_all = device_rows(small_all[:, 2 * R + 3 : 2 * R + 4], width // DV)[:, 0]
    rank_out_z = lax.dynamic_slice_in_dim(rank_out_all, z * DK, DK).astype(BF)
    bias_z = lax.dynamic_slice_in_dim(bias_all, z * DK, DK)[:, 0]

    rows_in = group_tokens.astype(F32)
    scale_in = lax.rsqrt(jnp.mean(rows_in * rows_in, axis=1, keepdims=True) + norm_eps)
    normed_in = (rows_in * scale_in * attn_gain_all).astype(BF)
    heads = dot_plain(normed_in, input_weights)
    out_gate = heads[:, 2 * DK + DV : projected]
    low = heads.astype(BF)
    shared = jnp.concatenate([low[:, : 2 * DK], low[:, projected:]], axis=1)
    values = jnp.swapaxes(low[:, 2 * DK : 2 * DK + DV].reshape(group, Y, dvp), 0, 1)
    sent = jnp.concatenate([jnp.broadcast_to(shared[None], (Y,) + shared.shape), values], axis=2)
    mlp_weights, sequence = move(
        next(numbers), cuts=[([mlp_gate_weight, mlp_up_weight, down_weight], "z")],
        deals=[(sent.reshape(Y, Z, own, -1), "y", True)],
    )
    out_piece = gather_rest(out_weights)
    mlp_piece = gather_rest(mlp_weights, ("x", "y"))
    sequence = sequence.reshape(total, -1)
    queries = sequence[:, :DK]
    keys = sequence[:, DK : 2 * DK]
    rank_low = sequence[:, 2 * DK : 2 * DK + R]
    value_part = sequence[:, 2 * DK + SMALL :]
    decay_logit = dot_rows(rank_low, rank_out_z) + bias_z
    log_decay = jax.nn.log_sigmoid(decay_logit) / decay_norm

    doc_ends = jnp.cumsum(doc_lengths[0])
    positions = lax.iota(jnp.int32, total)
    segments = jnp.sum((doc_ends[None, :] <= positions[:, None]).astype(jnp.int32), axis=1)
    cut = segments.reshape(-1, CHUNK)
    last = cut[:, CHUNK - 1 :]
    before = jnp.concatenate([jnp.full((1, 1), -1, jnp.int32), last[:-1]], axis=0)
    aux = jnp.stack(
        [cut == before, cut == last, cut, jnp.broadcast_to(last == before, cut.shape)], axis=-1
    )
    aux = aux.reshape(total, 4).astype(F32)
    seg_rows = cut.astype(F32)[:, None, :]

    mixed_part, enter, scores = mix_forward(queries, keys, value_part, log_decay, aux, seg_rows)
    mixed_part = deal(mixed_part.reshape(Z, Y, own, dvp), False).reshape(Y, group, dvp)
    mixed = jnp.swapaxes(mixed_part, 0, 1).reshape(group, DV).astype(F32)

    head_scale = lax.rsqrt(jnp.mean(mixed * mixed, axis=1, keepdims=True) + head_eps)
    head_hat = mixed * head_scale
    head_out = head_hat * head_gain_all
    sig_out = jax.nn.sigmoid(out_gate)
    silu_out = out_gate * sig_out
    gated = (head_out * silu_out).astype(BF)
    own_cotangent = blocked(cotangent)
    residual, group_cotangent = move(
        next(numbers), scatter=(dot_rows(gated, out_piece).astype(BF), "z"),
        gathers=[(own_cotangent, "z")], extras=[own_tokens],
        post=lambda total_sum, x: total_sum + x.astype(F32),
    )
    scale_mid = lax.rsqrt(jnp.mean(residual * residual, axis=1, keepdims=True) + norm_eps)
    hat_mid = residual * scale_mid
    normed_mlp = (hat_mid * mlp_gain_all).astype(BF)
    grad_normed_mlp, out_partial, mlp_partial = feed_forward(
        normed_mlp, mlp_piece, group_cotangent, next(numbers)
    )
    mlp_sums = scatter_rest(mlp_partial, ("x", "y"))

    mlp_gain_part = jnp.sum(grad_normed_mlp * hat_mid, axis=0)
    scaled = grad_normed_mlp * mlp_gain_all
    grad_residual = own_cotangent.astype(F32) + scale_mid * (
        scaled - hat_mid * jnp.mean(scaled * hat_mid, axis=1, keepdims=True)
    )
    branch_own = grad_residual.astype(BF)
    layer_out, grad_branch = move(
        next(numbers), scatter=(out_partial, "z"), gathers=[(branch_own, "z")],
        extras=[residual], post=lambda total_sum, rest: straight(total_sum + rest),
    )
    grad_gated = dot_plain(grad_branch, out_piece)
    grad_head = grad_gated * silu_out
    head_gain_part = jnp.sum(grad_head * head_hat, axis=0)
    from_head = grad_head * head_gain_all
    grad_mixed = head_scale * (
        from_head - head_hat * jnp.mean(from_head * head_hat, axis=1, keepdims=True)
    )
    grad_out_gate = (grad_gated * head_out * sig_out * (1.0 + out_gate * (1.0 - sig_out))).astype(BF)
    grad_cut = jnp.swapaxes(grad_mixed.astype(BF).reshape(group, Y, dvp), 0, 1)
    grad_part = deal(grad_cut.reshape(Y, Z, own, dvp), True).reshape(total, dvp)
    dq, dk, dv, dld = mix_backward(
        queries, keys, value_part, log_decay, aux, seg_rows, enter, scores, grad_part
    )
    dlogit = (dld * jax.nn.sigmoid(-decay_logit) / decay_norm).astype(BF)
    back = jnp.concatenate([dq, dk, dlogit, dv], axis=1).reshape(Z, Y, own, -1)
    side_partial = jnp.concatenate(
        [dot_cols(normed_in, grad_out_gate), dot_cols(grad_branch, gated)], axis=1
    ).astype(BF)
    back, side_partial = lax.optimization_barrier((back, side_partial))
    side_sums = scatter_rest(side_partial)
    mlp_rows, back = move(
        next(numbers), swaps=[(mlp_sums, "z")], deals=[(back, "y", False)]
    )
    back = back.reshape(Y, group, -1)
    summed = jnp.sum(back[:, :, : 3 * DK].astype(F32), axis=0).astype(BF)
    grad_value = jnp.swapaxes(back[:, :, 3 * DK :], 0, 1).reshape(group, DV)
    grad_logit = summed[:, 2 * DK :]
    bias_part = jnp.sum(grad_logit.astype(F32), axis=0)
    rank_low_group = low[:, projected : projected + R]
    rank_out_part = dot_cols(grad_logit, rank_low_group)
    grad_rank = dot_plain(grad_logit, rank_out_z).astype(BF)
    grad_heads = jnp.concatenate(
        [
            summed[:, : 2 * DK], grad_value, grad_out_gate,
            jnp.pad(grad_rank, ((0, 0), (0, SMALL - R))),
        ],
        axis=1,
    )
    normed_in_partial = dot_rows(grad_heads, input_weights)
    attn_gain_part = jnp.sum(normed_in_partial * (rows_in * scale_in), axis=0)
    def to_device_rows(value, count):
        cut = value.reshape(X, C, Z, Y, rows // count, -1)
        cut = jnp.swapaxes(cut, 2, 3)
        cut = jnp.pad(cut, ((0, 0),) * 4 + ((0, rows - rows // count), (0, 0)))
        return cut.reshape(width, -1)

    def at_head(value):
        return lax.dynamic_update_slice_in_dim(
            jnp.zeros((H * DK, value.shape[1]), F32), value, z * DK, 0
        )

    near_part = dot_cols(
        normed_in, jnp.concatenate([grad_heads[:, :near], grad_heads[:, projected:]], axis=1)
    )
    small_part = jnp.concatenate(
        [
            near_part[:, near : near + R],
            attn_gain_part[:, None],
            mlp_gain_part[:, None],
            to_device_rows(at_head(rank_out_part), width // (H * DK)),
            to_device_rows(at_head(bias_part[:, None]), width // (H * DK)),
            to_device_rows(head_gain_part[:, None], width // DV),
        ],
        axis=1,
    )
    small_part = jnp.pad(small_part, ((0, 0), (0, SMALL - small_part.shape[1])))
    near_partial = jnp.concatenate([near_part[:, :near], small_part], axis=1).astype(BF)
    partial, near_partial = lax.optimization_barrier(
        (normed_in_partial.astype(BF), near_partial)
    )
    near_sums = scatter_rest(near_partial)

    def finish_tokens(back_sum, x, grad_res, gain):
        held = x.astype(F32)
        scale = lax.rsqrt(jnp.mean(held * held, axis=1, keepdims=True) + norm_eps)
        hat = held * scale
        scaled = back_sum * gain
        mean = jnp.mean(scaled * hat, axis=1, keepdims=True)
        return straight(grad_res + scale * (scaled - hat * mean))

    tokens_grad, side_rows = move(
        next(numbers), scatter=(partial, "z"), swaps=[(side_sums, "z")],
        extras=[own_tokens, grad_residual, attn_gain_all[None]], post=finish_tokens,
    )
    near_rows = move(next(numbers), swaps=[(after(near_sums, tokens_grad), "z")])[0]

    mlp_grads = join(
        [mlp_rows], [(0, 0, ff), (0, ff, ff), (0, 2 * ff, ff)]
    )
    query_grad, key_grad, value_grad, gate_grad, out_grad = join(
        [near_rows, side_rows],
        [
            (0, 0, DK), (0, DK, DK), (0, 2 * DK, DV), (1, 0, DV), (1, DV, DV),
        ],
    )
    small_rows = jnp.sum(near_rows[:, :, near : near + SMALL].astype(F32), axis=0)
    return (
        layer_out,
        tokens_grad,
        small_rows[:, R],
        query_grad,
        key_grad,
        value_grad,
        gate_grad,
        small_rows[:, :R],
        small_rows[: rows * H * DK // width, R + 2 : 2 * R + 2],
        small_rows[: rows * H * DK // width, 2 * R + 2],
        small_rows[: rows * DV // width, 2 * R + 3],
        out_grad,
        small_rows[:, R + 1],
        *mlp_grads,
    )


def solution(mesh):
    groups, places = mesh.shape["grp"], mesh.shape["seq"]
    wide = Mesh(mesh.devices.reshape(groups // 2, 2, H, places // H), OWN)
    split = P(OWN, None)
    line = P(OWN)
    by_sequence = P(("x", "c"), None)
    placed = (
        split, by_sequence, split, line, split, split, split, split, split, split,
        line, line, split, line, split, split, split,
    )
    return jax.shard_map(
        local,
        mesh=wide,
        in_specs=placed,
        out_specs=(
            split, split, line, split, split, split, split, split, split, line, line, split,
            line, split, split, split,
        ),
        check_vma=False,
    )
```

```python
import functools

import jax
import jax.numpy as jnp
import numpy as np
from jax import lax
from jax.experimental import pallas as pl
from jax.experimental.pallas import tpu as pltpu
from jax.sharding import Mesh
from jax.sharding import PartitionSpec as P

H = 4
DK = 256
DV = 512
R = 16
CHUNK = 128
LEVELS = 7
SMALL = 128
RANK_AT = 32
HEAD_AT = 64
WAIT_FLOPS = 100_000_000
LANES = 128
TILE = 256
PIECES = 2
norm_eps = 1e-06
head_eps = 0.25
decay_norm = 16.0
BF = jnp.bfloat16
F32 = jnp.float32
REST = ("x", "c", "y")
OWN = ("x", "c", "z", "y")


def dot_plain(left, right):
    return jnp.dot(left, right, preferred_element_type=F32)


def dot_rows(left, right):
    return lax.dot_general(left, right, (((1,), (1,)), ((), ())), preferred_element_type=F32)


def dot_cols(left, right):
    return lax.dot_general(left, right, (((0,), (0,)), ((), ())), preferred_element_type=F32)


def split_two(value):
    high = value.astype(BF)
    return jnp.concatenate([high, (value - high.astype(F32)).astype(BF)], axis=1)


def sum_two(value):
    half = value.shape[1] // 2
    return value[:, :half] + value[:, half:]


def chunk_tables():
    t = np.arange(CHUNK)[:, None]
    j = np.arange(CHUNK)[None, :]
    parts = []
    level = np.full((CHUNK, CHUNK), -1, np.int32)
    for number in range(LEVELS):
        half = CHUNK >> (number + 1)
        middle = t // (2 * half) * (2 * half) + half - 1
        upper = t % (2 * half) >= half
        parts.append(np.where(upper, (j > middle) & (j <= t), (j > t) & (j <= middle)))
        pair = (t // (2 * half) == j // (2 * half)) & upper & (j % (2 * half) < half)
        level[pair] = number
    level[np.arange(CHUNK), np.arange(CHUNK)] = LEVELS
    parts.append(j <= t)
    parts.append(j > t)
    return np.concatenate(parts, axis=0).astype(np.float32), level


def upper_rows(number):
    half = CHUNK >> (number + 1)
    rows = lax.broadcasted_iota(jnp.int32, (CHUNK, 1), 0)
    return lax.rem(rows, 2 * half) >= half


def factors(ld_ref, sums_ref):
    exponents = sum_two(dot_plain(sums_ref[...], split_two(ld_ref[...])))
    return jnp.exp(exponents)


def rows_of(value, number):
    return value[number * CHUNK : (number + 1) * CHUNK]


def mix_forward_body(
    q_ref, k_ref, v_ref, ld_ref, aux_ref, seg_ref, sums_ref, level_ref,
    out_ref, enter_ref, score_ref, state,
):
    @pl.when(pl.program_id(0) == 0)
    def _():
        state[...] = jnp.zeros_like(state)

    factor = factors(ld_ref, sums_ref)
    query = q_ref[...].astype(F32) * DK ** (-0.5)
    key = k_ref[...].astype(F32)
    level = level_ref[...]
    aux = aux_ref[...]
    scores = jnp.where(level == LEVELS, dot_rows(query.astype(BF), k_ref[...]), 0.0)
    for number in range(LEVELS):
        part = rows_of(factor, number)
        pairs = dot_rows((query * part).astype(BF), (key * part).astype(BF))
        scores = jnp.where(level == number, pairs, scores)
    scores = jnp.where(aux[:, 2:3] == seg_ref[0], scores, 0.0).astype(BF)
    score_ref[0] = scores
    cumulative = rows_of(factor, LEVELS)
    enter = state[...].astype(BF)
    enter_ref[0] = enter
    lifted = (query * cumulative * aux[:, 0:1]).astype(BF)
    ending = (key * rows_of(factor, LEVELS + 1) * aux[:, 1:2]).astype(BF)
    out = dot_plain(scores, v_ref[...]) + dot_rows(lifted, enter)
    out_ref[...] = out.astype(out_ref.dtype)
    through = cumulative[CHUNK - 1 :] * aux[0:1, 3:4]
    state[...] = state[...] * through + dot_cols(v_ref[...], ending)


def mix_backward_body(
    q_ref, k_ref, v_ref, ld_ref, aux_ref, seg_ref, sums_ref, sums_t_ref, level_ref, level_t_ref,
    enter_ref, score_ref, do_ref,
    dq_ref, dk_ref, dv_ref, dld_ref, state,
):
    @pl.when(pl.program_id(0) == 0)
    def _():
        state[...] = jnp.zeros_like(state)

    factor = factors(ld_ref, sums_ref)
    scale = DK ** (-0.5)
    query = q_ref[...].astype(F32) * scale
    key = k_ref[...].astype(F32)
    value = v_ref[...]
    grad = do_ref[...]
    level = level_ref[...]
    level_t = level_t_ref[...]
    aux = aux_ref[...]
    same = aux[:, 2:3] == seg_ref[0]
    weight = jnp.where(same, dot_rows(grad, value), 0.0)
    weight_t = jnp.where(same, dot_rows(value, grad), 0.0)
    diagonal = jnp.sum(jnp.where(level == LEVELS, weight, 0.0), axis=1, keepdims=True)
    dq = diagonal * key
    dk = diagonal * query
    moved = []
    for number in range(LEVELS):
        part = rows_of(factor, number)
        left = jnp.concatenate(
            [
                jnp.where(level == number, weight, 0.0).astype(BF),
                jnp.where(level_t == number, weight_t, 0.0).astype(BF),
            ],
            axis=1,
        )
        right = jnp.concatenate([(key * part).astype(BF), (query * part).astype(BF)], axis=0)
        both = dot_plain(left, right) * part
        upper = upper_rows(number)
        dq = dq + jnp.where(upper, both, 0.0)
        dk = dk + jnp.where(upper, 0.0, both)
        moved.append(both * jnp.where(upper, query, key))
    cumulative = rows_of(factor, LEVELS)
    enter = enter_ref[0]
    after = state[...]
    after_low = after.astype(BF)
    lift = cumulative * aux[:, 0:1]
    finish = rows_of(factor, LEVELS + 1) * aux[:, 1:2]
    lifted = query * lift
    ending = key * finish
    from_enter = dot_plain(grad, enter)
    from_after = dot_plain(value, after_low)
    moved.append(lifted * from_enter)
    moved.append(ending * from_after)
    dq_ref[...] = ((dq + lift * from_enter) * scale).astype(dq_ref.dtype)
    dk_ref[...] = (dk + finish * from_after).astype(dk_ref.dtype)
    dv = dot_cols(score_ref[0], grad) + dot_rows(ending.astype(BF), after_low)
    dv_ref[...] = dv.astype(dv_ref.dtype)
    through = cumulative[CHUNK - 1 :] * aux[0:1, 3:4]
    passing = jnp.sum(after * enter.astype(F32), axis=0, keepdims=True) * through
    spread = sum_two(dot_plain(sums_t_ref[...], split_two(jnp.concatenate(moved, axis=0))))
    dld_ref[...] = spread + passing
    state[...] = after * through + dot_cols(grad, lifted.astype(BF))


def mix_specs(count, width, backward):
    def at(i):
        return count - 1 - i if backward else i

    def tokens(columns):
        return pl.BlockSpec((CHUNK, columns), lambda i: (at(i), 0))

    def chunks(rows, columns):
        return pl.BlockSpec((1, rows, columns), lambda i: (at(i), 0, 0))

    def whole(rows, columns):
        return pl.BlockSpec((rows, columns), lambda i: (0, 0))

    return tokens, chunks, whole


def mix_forward(query, key, value, log_decay, aux, seg_rows):
    total, width = value.shape
    count = total // CHUNK
    sums, level = chunk_tables()
    tokens, chunks, whole = mix_specs(count, width, False)
    return pl.pallas_call(
        mix_forward_body,
        grid=(count,),
        in_specs=[
            tokens(DK), tokens(DK), tokens(width), tokens(DK), tokens(aux.shape[1]),
            chunks(1, CHUNK), whole(*sums.shape), whole(CHUNK, CHUNK),
        ],
        out_specs=[tokens(width), chunks(width, DK), chunks(CHUNK, CHUNK)],
        out_shape=[
            jax.ShapeDtypeStruct((total, width), BF),
            jax.ShapeDtypeStruct((count, width, DK), BF),
            jax.ShapeDtypeStruct((count, CHUNK, CHUNK), BF),
        ],
        scratch_shapes=[pltpu.VMEM((width, DK), F32)],
        compiler_params=pltpu.CompilerParams(
            dimension_semantics=("arbitrary",), vmem_limit_bytes=32 * 1024 * 1024
        ),
        cost_estimate=pl.CostEstimate(
            flops=total * 2 * (8 * CHUNK * DK + 2 * width * DK + CHUNK * width + 18 * CHUNK * DK),
            bytes_accessed=total * 4096, transcendentals=total * 9 * DK,
        ),
        name="mix_forward",
    )(query, key, value, log_decay, aux, seg_rows, jnp.asarray(sums, BF), jnp.asarray(level))


def mix_backward(query, key, value, log_decay, aux, seg_rows, enter, scores, grad):
    total, width = value.shape
    count = total // CHUNK
    sums, level = chunk_tables()
    tokens, chunks, whole = mix_specs(count, width, True)
    return pl.pallas_call(
        mix_backward_body,
        grid=(count,),
        in_specs=[
            tokens(DK), tokens(DK), tokens(width), tokens(DK), tokens(aux.shape[1]),
            chunks(1, CHUNK), whole(*sums.shape), whole(*sums.shape[::-1]),
            whole(CHUNK, CHUNK), whole(CHUNK, CHUNK),
            chunks(width, DK), chunks(CHUNK, CHUNK), tokens(width),
        ],
        out_specs=[tokens(DK), tokens(DK), tokens(width), tokens(DK)],
        out_shape=[
            jax.ShapeDtypeStruct((total, DK), BF),
            jax.ShapeDtypeStruct((total, DK), BF),
            jax.ShapeDtypeStruct((total, width), BF),
            jax.ShapeDtypeStruct((total, DK), F32),
        ],
        scratch_shapes=[pltpu.VMEM((width, DK), F32)],
        compiler_params=pltpu.CompilerParams(
            dimension_semantics=("arbitrary",), vmem_limit_bytes=48 * 1024 * 1024
        ),
        cost_estimate=pl.CostEstimate(
            flops=total * 2 * (14 * CHUNK * DK + 4 * width * DK + CHUNK * width + 36 * CHUNK * DK),
            bytes_accessed=total * 6144, transcendentals=total * 9 * DK,
        ),
        name="mix_backward",
    )(
        query, key, value, log_decay, aux, seg_rows, jnp.asarray(sums, BF),
        jnp.asarray(np.ascontiguousarray(sums.T), BF), jnp.asarray(level),
        jnp.asarray(np.ascontiguousarray(level.T)), enter, scores, grad,
    )


def remote(source, target, send, arrive, axis, place):
    return pltpu.make_async_remote_copy(
        src_ref=source, dst_ref=target, send_sem=send, recv_sem=arrive,
        device_id={axis: place}, device_id_type=pl.DeviceIdType.MESH,
    )


def greet(peers):
    barrier = pltpu.get_barrier_semaphore()
    number = 0
    for present, peer in peers:
        if present is True:
            pl.semaphore_signal(
                barrier, inc=1, device_id=peer, device_id_type=pl.DeviceIdType.MESH
            )
            number = number + 1
        else:

            @pl.when(present)
            def _():
                pl.semaphore_signal(
                    barrier, inc=1, device_id=peer, device_id_type=pl.DeviceIdType.MESH
                )

            number = number + jnp.where(present, 1, 0)
    pl.semaphore_wait(barrier, number)


def line_peers(axis, count):
    me = lax.axis_index(axis)
    return [(me > 0, {axis: me - 1}), (me < count - 1, {axis: me + 1})]


def all_peers(axis, count):
    me = lax.axis_index(axis)
    return [(True, {axis: lax.rem(me + away, count)}) for away in range(1, count)]


class Gather:
    def __init__(self, axis, count, x_ref, out_ref, send, arrive, local_sem):
        self.axis, self.count, self.x_ref, self.out_ref = axis, count, x_ref, out_ref
        self.send, self.arrive = send, arrive
        self.me = lax.axis_index(axis)
        self.mine = pltpu.make_async_copy(x_ref, self.block(self.me), local_sem)

    def block(self, index):
        own = self.x_ref.shape[0]
        return self.out_ref.at[pl.ds(pl.multiple_of(index * own, own), own)]

    def copy(self, direction, step, index, source):
        return remote(
            source, self.block(index), self.send.at[direction, step],
            self.arrive.at[direction, step], self.axis,
            self.me + 1 if direction == 0 else self.me - 1,
        )

    def hop(self, direction, step):
        index = self.me - step if direction == 0 else self.me + step
        return self.copy(direction, step, index, self.x_ref if step == 0 else self.block(index))

    def landed(self, direction, step):
        index = self.me - 1 - step if direction == 0 else self.me + 1 + step
        return self.copy(direction, step, index, self.block(index))

    def holds(self, direction, step):
        return self.me - step >= 0 if direction == 0 else self.me + step <= self.count - 1

    def hands_on(self, direction, step):
        inner = self.me < self.count - 1 if direction == 0 else self.me > 0
        return self.holds(direction, step) & inner

    def start(self):
        self.mine.start()
        self.run(0)

    def run(self, first, last=None):
        for step in range(first, first + 1 if last is None else last):
            for direction in (0, 1):
                if step > 0:

                    @pl.when(self.holds(direction, step))
                    def _():
                        self.landed(direction, step - 1).wait_recv()

                if step < self.count - 1:

                    @pl.when(self.hands_on(direction, step))
                    def _():
                        self.hop(direction, step).start()

    def finish(self):
        self.finish_sends()
        self.mine.wait()

    def finish_sends(self):
        for step in range(self.count - 1):
            for direction in (0, 1):

                @pl.when(self.hands_on(direction, step))
                def _():
                    self.hop(direction, step).wait_send()

    @staticmethod
    def scratch(count):
        return [
            pltpu.SemaphoreType.DMA((2, count - 1)),
            pltpu.SemaphoreType.DMA((2, count - 1)),
            pltpu.SemaphoreType.DMA,
        ]


class Swap:
    def __init__(self, axis, count, x_ref, out_ref, send, arrive, local_sem):
        self.axis, self.count, self.x_ref, self.out_ref = axis, count, x_ref, out_ref
        self.send, self.arrive = send, arrive
        self.me = lax.axis_index(axis)
        self.mine = pltpu.make_async_copy(x_ref.at[self.me], out_ref.at[self.me], local_sem)

    def hop(self, away):
        peer = lax.rem(self.me + away, self.count)
        return remote(
            self.x_ref.at[peer], self.out_ref.at[self.me], self.send.at[away - 1],
            self.arrive.at[away - 1], self.axis, peer,
        )

    def landed(self, away):
        peer = lax.rem(self.me + self.count - away, self.count)
        return remote(
            self.x_ref.at[peer], self.out_ref.at[peer], self.send.at[away - 1],
            self.arrive.at[away - 1], self.axis, peer,
        )

    def start(self):
        self.mine.start()
        for away in range(1, self.count):
            self.hop(away).start()

    def finish(self):
        for away in range(1, self.count):
            self.landed(away).wait_recv()
        for away in range(1, self.count):
            self.hop(away).wait_send()
        self.mine.wait()

    @staticmethod
    def scratch(count):
        return [
            pltpu.SemaphoreType.DMA((count - 1,)),
            pltpu.SemaphoreType.DMA((count - 1,)),
            pltpu.SemaphoreType.DMA,
        ]


class Scatter:
    def __init__(self, axis, count, pieces, x_ref, out_ref, up, down, send, arrive):
        self.axis, self.count, self.pieces = axis, count, pieces
        self.x_ref, self.out_ref, self.held_refs = x_ref, out_ref, (up, down)
        self.send, self.arrive = send, arrive
        self.me = lax.axis_index(axis)
        self.own = out_ref.shape[0]
        self.size = self.own // pieces

    def part(self, index, piece):
        start = pl.multiple_of(index * self.own + piece * self.size, self.size)
        return self.x_ref.at[pl.ds(start, self.size)]

    def held(self, direction, number, piece):
        return self.held_refs[direction].at[number, pl.ds(piece * self.size, self.size)]

    def hop(self, direction, number, piece, source=None):
        held = self.held(direction, number, piece)
        return remote(
            held if source is None else source, held, self.send.at[direction, number, piece],
            self.arrive.at[direction, number, piece], self.axis,
            self.me + 1 if direction == 0 else self.me - 1,
        )

    def target(self, direction, number):
        return self.count - 1 - number if direction == 0 else number

    def start(self, numbers=None):
        for direction in (0, 1):

            @pl.when(self.me == (0 if direction == 0 else self.count - 1))
            def _():
                for number in range(self.count - 1) if numbers is None else numbers:
                    target = self.target(direction, number)
                    for piece in range(self.pieces):
                        self.hop(direction, number, piece, self.part(target, piece)).start()

    def stage(self, direction, number, piece):
        me, target = self.me, self.target(direction, number)
        inner = me > 0 if direction == 0 else me < self.count - 1
        passed = me < target if direction == 0 else me > target
        held = self.held(direction, number, piece)

        @pl.when(inner & (passed | (me == target)))
        def _():
            self.hop(direction, number, piece).wait_recv()

        @pl.when(inner & passed)
        def _():
            mine = self.part(target, piece)[...].astype(F32)
            held[...] = (held[...].astype(F32) + mine).astype(BF)
            self.hop(direction, number, piece).start()

    def run(self, number, far):
        for order in (0, 1):

            @pl.when((self.me >= self.count // 2) == (order == 1))
            def _():
                for piece in range(self.pieces):
                    self.stage(1 - order if far else order, number, piece)

    def finish(self):
        me, count, out_ref = self.me, self.count, self.out_ref
        for piece in range(self.pieces):
            rows = pl.ds(piece * self.size, self.size)
            out_ref[rows] = self.part(me, piece)[...].astype(F32)
            for direction in (0, 1):
                for number in range(count - 1):
                    inner = me > 0 if direction == 0 else me < count - 1

                    @pl.when((me == self.target(direction, number)) & inner)
                    def _():
                        out_ref[rows] += self.held(direction, number, piece)[...].astype(F32)

        for direction in (0, 1):
            for number in range(count - 1):
                target = self.target(direction, number)

                @pl.when(me < target if direction == 0 else me > target)
                def _():
                    for piece in range(self.pieces):
                        self.hop(direction, number, piece).wait_send()

    @staticmethod
    def scratch(count, own, columns, pieces):
        return [
            pltpu.VMEM((count - 1, own, columns), BF),
            pltpu.VMEM((count - 1, own, columns), BF),
            pltpu.SemaphoreType.DMA((2, count - 1, pieces)),
            pltpu.SemaphoreType.DMA((2, count - 1, pieces)),
        ]


class CutSwap:
    def __init__(self, axis, count, refs, out_ref, send, arrive, local_sem):
        self.axis, self.count, self.refs, self.out_ref = axis, count, refs, out_ref
        self.send, self.arrive = send, arrive
        self.me = lax.axis_index(axis)
        self.widths = [ref.shape[1] // count for ref in refs]
        self.mine = [
            pltpu.make_async_copy(self.cut(i, self.me), self.slot(i, self.me), local_sem.at[i])
            for i in range(len(refs))
        ]

    def cut(self, i, index):
        size = self.widths[i]
        return self.refs[i].at[:, pl.ds(pl.multiple_of(index * size, LANES), size)]

    def slot(self, i, index):
        return self.out_ref.at[index, :, pl.ds(sum(self.widths[:i]), self.widths[i])]

    def hop(self, away, i):
        peer = lax.rem(self.me + away, self.count)
        return remote(
            self.cut(i, peer), self.slot(i, self.me), self.send.at[away - 1, i],
            self.arrive.at[away - 1, i], self.axis, peer,
        )

    def landed(self, away, i):
        peer = lax.rem(self.me + self.count - away, self.count)
        return remote(
            self.cut(i, peer), self.slot(i, peer), self.send.at[away - 1, i],
            self.arrive.at[away - 1, i], self.axis, peer,
        )

    def each(self):
        return [(away, i) for away in range(1, self.count) for i in range(len(self.refs))]

    def start(self):
        for away, i in self.each():
            self.hop(away, i).start()
        for copy in self.mine:
            copy.start()

    def finish(self):
        for away, i in self.each():
            self.landed(away, i).wait_recv()
        for away, i in self.each():
            self.hop(away, i).wait_send()
        for copy in self.mine:
            copy.wait()

    @staticmethod
    def scratch(count, parts):
        sems = pltpu.SemaphoreType.DMA((count - 1, parts))
        return [sems, sems, pltpu.SemaphoreType.DMA((parts,))]


class Deal:
    def __init__(self, axis, count, forth, x_ref, out_ref, send, arrive, local_sem):
        self.axis, self.count, self.forth = axis, count, forth
        self.x_ref, self.out_ref, self.send, self.arrive = x_ref, out_ref, send, arrive
        self.me = lax.axis_index(axis)
        self.steps = x_ref.shape[1] if forth else x_ref.shape[0]
        self.mine = [
            pltpu.make_async_copy(self.given(self.me, k), self.got(self.me, k), local_sem.at[k])
            for k in range(self.steps)
        ]

    def given(self, device, k):
        return self.x_ref.at[device, k] if self.forth else self.x_ref.at[k, device]

    def got(self, device, k):
        return self.out_ref.at[k, device] if self.forth else self.out_ref.at[device, k]

    def hop(self, away, k):
        peer = lax.rem(self.me + away, self.count)
        return remote(
            self.given(peer, k), self.got(self.me, k), self.send.at[away - 1, k],
            self.arrive.at[away - 1, k], self.axis, peer,
        )

    def landed(self, away, k):
        peer = lax.rem(self.me + self.count - away, self.count)
        return remote(
            self.given(peer, k), self.got(peer, k), self.send.at[away - 1, k],
            self.arrive.at[away - 1, k], self.axis, peer,
        )

    def each(self):
        return [(away, k) for away in range(1, self.count) for k in range(self.steps)]

    def start(self):
        for away, k in self.each():
            self.hop(away, k).start()
        for copy in self.mine:
            copy.start()

    def finish(self):
        for away, k in self.each():
            self.landed(away, k).wait_recv()
        for away, k in self.each():
            self.hop(away, k).wait_send()
        for copy in self.mine:
            copy.wait()

    @staticmethod
    def scratch(count, steps):
        sems = pltpu.SemaphoreType.DMA((count - 1, steps))
        return [sems, sems, pltpu.SemaphoreType.DMA((steps,))]


class Spread:
    def __init__(self, sizes, cuts, out_ref, far_send, far_arrive, near_send, near_arrive):
        self.X, self.C, self.Z, self.Y = sizes
        self.cuts, self.out_ref = cuts, out_ref
        self.far_send, self.far_arrive = far_send, far_arrive
        self.near_send, self.near_arrive = near_send, near_arrive
        self.x, self.c, self.z, self.y = (lax.axis_index(name) for name in OWN)
        self.others = self.X * self.Y - 1

    def across(self, offset, sign):
        down, right = offset // self.Y, offset % self.Y
        if sign < 0:
            down, right = self.X - down, self.Y - right
        return lax.rem(self.x + down, self.X), lax.rem(self.y + right, self.Y)

    def place(self, offset, c, slot):
        x, y = self.across(offset, -1)
        z = lax.rem(self.z + self.Z - slot, self.Z)
        return self.out_ref.at[((x * self.C + c) * self.Y + y) * self.Z + z]

    def far(self, offset, slot, landed=False):
        x, y = self.across(offset, 1)
        held = self.place(offset if landed else 0, self.c, slot)
        return pltpu.make_async_remote_copy(
            src_ref=held, dst_ref=held, send_sem=self.far_send.at[offset - 1, slot],
            recv_sem=self.far_arrive.at[offset - 1, slot], device_id={"x": x, "y": y},
            device_id_type=pl.DeviceIdType.MESH,
        )

    def near(self, offset, slot, landed=False):
        held = self.place(offset, 1 - self.c if landed else self.c, slot)
        return remote(
            held, held, self.near_send.at[offset, slot],
            self.near_arrive.at[offset, slot], "c", 1 - self.c,
        )

    def peers(self):
        found = all_peers("z", self.Z) + [(True, {"c": 1 - self.c})]
        for offset in range(1, self.others + 1):
            x, y = self.across(offset, 1)
            found.append((True, {"x": x, "y": y}))
        return found

    def hand_on(self, slot):
        for i in range(len(self.cuts.refs)):
            if slot > 0:
                self.cuts.landed(slot, i).wait_recv()
            else:
                self.cuts.mine[i].wait()
        for offset in range(1, self.others + 1):
            self.far(offset, slot).start()
        self.near(0, slot).start()

    def collect(self, slot):
        for offset in range(1, self.others + 1):
            self.far(offset, slot, True).wait_recv()
            self.near(offset, slot).start()

    def finish(self):
        for slot in range(self.Z):
            for offset in range(self.others + 1):
                self.near(offset, slot, True).wait_recv()
        for slot in range(self.Z):
            for offset in range(self.others + 1):
                self.near(offset, slot).wait_send()
                if offset > 0:
                    self.far(offset, slot).wait_send()
        for away, i in self.cuts.each():
            self.cuts.hop(away, i).wait_send()

    @staticmethod
    def scratch(sizes):
        X, C, Z, Y = sizes
        far = pltpu.SemaphoreType.DMA((max(X * Y - 1, 1), Z))
        near = pltpu.SemaphoreType.DMA((X * Y, Z))
        return [far, far, near, near]


class FirstCuts(CutSwap):
    def __init__(self, spread_place, count, refs, out_ref, send, arrive, local_sem):
        self.place = spread_place
        super().__init__("z", count, refs, out_ref, send, arrive, local_sem)

    def cut(self, i, index):
        return self.refs[i] if i == len(self.refs) - 1 else super().cut(i, index)

    def slot(self, i, index):
        widths = [w for w in self.widths[:-1]] + [SMALL]
        return self.out_ref.at[self.place(index), :, pl.ds(sum(widths[:i]), widths[i])]


def spread_and_gather(weights, block, other, sizes, number):
    X, C, Z, Y = sizes
    parts = len(weights)
    rows = weights[0].shape[0]
    total = sum(w.shape[1] // Z for w in weights[:-1]) + weights[-1].shape[1]

    def body(*refs):
        w_refs, x_ref, o_ref = refs[:parts], refs[parts], refs[parts + 1]
        spread_ref, out_ref, swapped_ref = refs[parts + 2 : parts + 5]
        sems = refs[parts + 5 :]
        x, c, _, y = (lax.axis_index(name) for name in OWN)
        first = FirstCuts(
            lambda index: ((x * C + c) * Y + y) * Z + index, Z, w_refs, spread_ref, *sems[:3]
        )
        spread = Spread(sizes, first, spread_ref, *sems[3:7])
        gather = Gather("z", Z, x_ref, out_ref, *sems[7:10])
        swap = CutSwap("z", Z, [o_ref], swapped_ref, *sems[10:])
        greet(spread.peers())
        first.start()
        gather.start()
        spread.hand_on(0)
        for slot in range(1, Z):
            spread.hand_on(slot)
        for step in range(1, Z):
            gather.run(step)
            if step == Z - 2:
                swap.start()
            spread.collect(step - 1)
        spread.collect(Z - 1)
        spread.finish()
        gather.finish()
        swap.finish()

    anywhere = pl.BlockSpec(memory_space=pl.ANY)
    return pl.pallas_call(
        body,
        in_specs=[anywhere] * (parts + 2),
        out_specs=[anywhere] * 3,
        out_shape=[
            jax.ShapeDtypeStruct((X * C * Y * Z, rows, total), BF),
            jax.ShapeDtypeStruct((Z * block.shape[0],) + block.shape[1:], block.dtype),
            jax.ShapeDtypeStruct((Z, rows, other.shape[1] // Z), BF),
        ],
        scratch_shapes=CutSwap.scratch(Z, parts)
        + Spread.scratch(sizes)
        + Gather.scratch(Z)
        + CutSwap.scratch(Z, 1),
        compiler_params=pltpu.CompilerParams(collective_id=number, has_side_effects=True),
        cost_estimate=pl.CostEstimate(
            flops=WAIT_FLOPS, bytes_accessed=rows * total * X * C * Y * Z * 2, transcendentals=0
        ),
        name="spread_and_gather",
    )(*weights, block, other)


def move(
    number, scatter=None, swaps=(), gathers=(), cuts=(), deals=(), extras=(), post=None
):
    in_vmem, anywhere = pl.BlockSpec(memory_space=pltpu.VMEM), pl.BlockSpec(memory_space=pl.ANY)
    values, in_specs, shapes, out_specs, scratch = [], [], [], [], []
    flags = {}

    def scale(axis):
        return lax.axis_size(axis)

    if scatter is not None:
        partial, axis = scatter
        own = partial.shape[0] // scale(axis)
        values += [partial, *extras]
        in_specs += [in_vmem] * (1 + len(extras))
        shapes.append(jax.ShapeDtypeStruct((own, partial.shape[1]), F32))
        out_specs.append(in_vmem)
        scratch += Scatter.scratch(scale(axis), own, partial.shape[1], PIECES)
        flags = dict(vmem_limit_bytes=40 * 1024 * 1024)
    for value, axis in swaps:
        values.append(value)
        in_specs.append(anywhere)
        shapes.append(jax.ShapeDtypeStruct(value.shape, value.dtype))
        out_specs.append(anywhere)
        scratch += Swap.scratch(scale(axis))
    for block, axis in gathers:
        values.append(block)
        in_specs.append(anywhere)
        shapes.append(
            jax.ShapeDtypeStruct((scale(axis) * block.shape[0], block.shape[1]), block.dtype)
        )
        out_specs.append(anywhere)
        scratch += Gather.scratch(scale(axis))

    for weights, axis in cuts:
        values += weights
        in_specs += [anywhere] * len(weights)
        wide = sum(w.shape[1] for w in weights) // scale(axis)
        shapes.append(
            jax.ShapeDtypeStruct((scale(axis), weights[0].shape[0], wide), weights[0].dtype)
        )
        out_specs.append(anywhere)
        scratch += CutSwap.scratch(scale(axis), len(weights))
    for value, axis, forth in deals:
        first, second = value.shape[:2]
        values.append(value)
        in_specs.append(anywhere)
        shapes.append(jax.ShapeDtypeStruct((second, first) + value.shape[2:], value.dtype))
        out_specs.append(anywhere)
        scratch += Deal.scratch(scale(axis), second if forth else first)

    def body(*refs):
        ins = list(refs[: len(values)])
        outs = list(refs[len(values) : len(values) + len(shapes)])
        sems = list(refs[len(values) + len(shapes) :])
        peers = {}
        adding, extra_refs, swapping, gathering = None, (), [], []
        if scatter is not None:
            axis = scatter[1]
            adding = Scatter(axis, scale(axis), PIECES, ins.pop(0), outs.pop(0), *sems[:4])
            extra_refs, ins, sems = ins[: len(extras)], ins[len(extras) :], sems[4:]
            peers[axis] = line_peers(axis, scale(axis))
        for _, axis in gathers:
            peers[axis] = line_peers(axis, scale(axis))
        for _, axis in swaps:
            peers[axis] = all_peers(axis, scale(axis))
            swapping.append(Swap(axis, scale(axis), ins.pop(0), outs.pop(0), *sems[:3]))
            sems = sems[3:]
        for _, axis in gathers:
            gathering.append(Gather(axis, scale(axis), ins.pop(0), outs.pop(0), *sems[:3]))
            sems = sems[3:]
        for weights, axis in cuts:
            peers[axis] = all_peers(axis, scale(axis))
            taken, ins = ins[: len(weights)], ins[len(weights) :]
            swapping.append(CutSwap(axis, scale(axis), taken, outs.pop(0), *sems[:3]))
            sems = sems[3:]
        for _, axis, forth in deals:
            peers[axis] = all_peers(axis, scale(axis))
            swapping.append(
                Deal(axis, scale(axis), forth, ins.pop(0), outs.pop(0), *sems[:3])
            )
            sems = sems[3:]
        greet([peer for found in peers.values() for peer in found])
        for part in gathering + ([adding] if adding else []) + swapping:
            part.start()
        steps = max([part.count for part in gathering + ([adding] if adding else [])] + [0])
        for part in gathering:
            part.run(1)
        for step in range(1, steps):
            if adding:
                adding.run(step - 1, False)
            for part in gathering:
                if step + 1 < part.count:
                    part.run(step + 1)
            if adding:
                adding.run(step - 1, True)
        if adding:
            adding.finish()
            if post is not None:
                adding.out_ref[...] = post(adding.out_ref[...], *[r[...] for r in extra_refs])
        for part in swapping + gathering:
            part.finish()

    size = sum(v.size for v in values)
    return pl.pallas_call(
        body,
        in_specs=in_specs,
        out_specs=out_specs,
        out_shape=shapes,
        scratch_shapes=scratch,
        compiler_params=pltpu.CompilerParams(
            collective_id=number, has_side_effects=True, **flags
        ),
        cost_estimate=pl.CostEstimate(
            flops=WAIT_FLOPS, bytes_accessed=size * 4, transcendentals=0
        ),
        name="move",
    )(*values)


def feed_forward(normed_own, mlp_piece, cotangent, number):
    count = lax.axis_size("z")
    own, width = normed_own.shape
    group, ff = own * count, mlp_piece.shape[1] // 3
    half = group // 2
    block = width // (2 * lax.axis_size("x"))

    def body(x_ref, w_hbm, c_hbm, sum_ref, down_ref, grad_hbm,
             w_ref, d_ref, c_ref, normed, hidden_grad, hidden, grads, partial, stage, received,
             load_sem, store_sem, pair_send, pair_arrive, gather_send, gather_arrive, local_sem, up, down, send, arrive):
        me, core = lax.axis_index("z"), lax.axis_index("c")
        loads = [
            pltpu.make_async_copy(source, target, load_sem.at[i])
            for i, (source, target) in enumerate(
                [
                    (c_hbm, c_ref),
                    (w_hbm.at[:, pl.ds(2 * ff, ff)], d_ref),
                    (w_hbm.at[:, pl.ds(0, 2 * ff)], w_ref),
                ]
            )
        ]
        for load in loads:
            load.start()
        gather = Gather("z", count, x_ref, normed, gather_send, gather_arrive, local_sem)
        scatter = Scatter("z", count, PIECES, partial, sum_ref, up, down, send, arrive)
        greet(line_peers("z", count) + [(True, {"c": 1 - core})])
        gather.start()
        loads[0].wait()
        loads[1].wait()

        def tile_of(index, size):
            return pl.ds(pl.multiple_of(index * size, size), size)

        def spans(total):
            return [pl.ds(at, min(TILE, total - at)) for at in range(0, total, TILE)]

        for at in spans(ff):
            hidden_grad[:, at] = dot_plain(c_ref[...], d_ref[:, at])
        loads[2].wait()
        lower = me < count // 2
        nearer = me // (count // 2)

        def forward(rows):
            for at in spans(ff):
                up_at = pl.ds(ff + at.start, at.size)
                gate = dot_plain(normed[rows], w_ref[:, at])
                upper = dot_plain(normed[rows], w_ref[:, up_at])
                grad = hidden_grad[rows, at]
                sig = jax.nn.sigmoid(gate)
                silu = gate * sig
                hidden[rows, at] = (silu * upper).astype(BF)
                grad_gate = grad * upper * sig * (1.0 + gate * (1.0 - sig))
                grads[rows, at] = grad_gate.astype(BF)
                grads[rows, up_at] = (grad * silu).astype(BF)

        def backward(rows):
            for at in spans(width):
                partial[rows, at] = dot_rows(grads[rows], w_ref[at]).astype(BF)

        kept = width // 2 // TILE
        rows_kept = functools.partial(rows_of_core, block)

        def store(number):
            return pltpu.make_async_copy(
                stage.at[number % 2], grad_hbm.at[pl.ds(number * TILE, TILE)],
                store_sem.at[number % 2],
            )

        def pass_over(number):
            return remote(
                stage.at[number % 2], received.at[number], pair_send.at[number % 2],
                pair_arrive.at[number], "c", 1 - core,
            )

        def weight_rows(i):
            ours, number = i >= kept, i % kept
            if i >= 2:
                if i - 2 >= kept:
                    store(i - 2 - kept).wait()
                else:
                    pass_over(i - 2).wait_send()
            at = rows_kept(number, core if ours else 1 - core)
            slot = i % 2
            top = dot_cols(normed[:, at], grads[...])
            low = dot_cols(c_ref[:, at], hidden[...])
            if ours:
                pass_over(number).wait_recv()
                top = top + received[number, :, : 2 * ff].astype(F32)
                low = low + received[number, :, 2 * ff :].astype(F32)
            stage[slot, :, : 2 * ff] = top.astype(BF)
            stage[slot, :, 2 * ff :] = low.astype(BF)
            if ours:
                store(number).start()
            else:
                pass_over(number).start()
            at = pl.ds(i * TILE, TILE)
            down_ref[:, at] = dot_rows(hidden[...], d_ref[at]).astype(BF)

        def away(near):
            block = jnp.where(lower, count // 2, count // 2 - 1)
            end = jnp.where(lower, count - 1, 0)
            return tile_of(block if near else end, own)

        gather.run(1)
        gather.mine.wait()
        forward(tile_of(nearer, half))
        gather.run(2)
        forward(away(True))
        gather.run(3)
        forward(away(False))
        backward(away(False))
        scatter.start([0])
        backward(away(True))
        scatter.start([1])
        backward(tile_of(nearer, half))
        scatter.start([2])
        units = list(range(width // TILE))
        stages = [(step, far) for step in range(count - 1) for far in (False, True)]
        spare = len(units) - len(stages)
        for i in units[: max(spare, 0)]:
            weight_rows(i)
        rest = units[max(spare, 0) :]
        for step, far in stages:
            scatter.run(step, far)
            if rest:
                weight_rows(rest.pop(0))
        scatter.finish()
        gather.finish_sends()
        for number in range(kept - 2, kept):
            store(number).wait()

    in_vmem, anywhere = pl.BlockSpec(memory_space=pltpu.VMEM), pl.BlockSpec(memory_space=pl.ANY)
    return pl.pallas_call(
        body,
        in_specs=[in_vmem, anywhere, anywhere],
        out_specs=[in_vmem, in_vmem, anywhere],
        out_shape=[
            jax.ShapeDtypeStruct((own, width), F32),
            jax.ShapeDtypeStruct((group, width), BF),
            jax.ShapeDtypeStruct((width // 2, 3 * ff), BF),
        ],
        scratch_shapes=[
            pltpu.VMEM((width, 2 * ff), BF),
            pltpu.VMEM((width, ff), BF),
            pltpu.VMEM((group, width), BF),
            pltpu.VMEM((group, width), BF),
            pltpu.VMEM((group, ff), F32),
            pltpu.VMEM((group, ff), BF),
            pltpu.VMEM((group, 2 * ff), BF),
            pltpu.VMEM((group, width), BF),
            pltpu.VMEM((2, TILE, 3 * ff), BF),
            pltpu.VMEM((width // 2 // TILE, TILE, 3 * ff), BF),
            pltpu.SemaphoreType.DMA((3,)),
            pltpu.SemaphoreType.DMA((2,)),
            pltpu.SemaphoreType.DMA((2,)),
            pltpu.SemaphoreType.DMA((width // 2 // TILE,)),
        ]
        + Gather.scratch(count)
        + Scatter.scratch(count, own, width, PIECES),
        compiler_params=pltpu.CompilerParams(
            collective_id=number, has_side_effects=True, vmem_limit_bytes=60 * 1024 * 1024
        ),
        cost_estimate=pl.CostEstimate(
            flops=WAIT_FLOPS, bytes_accessed=width * ff * 12, transcendentals=0
        ),
        name="feed_forward",
    )(normed_own, mlp_piece, cotangent)


def rows_of_core(block, number, by):
    per = block // TILE
    start = (number // per * 2 + by) * block + number % per * TILE
    return pl.ds(pl.multiple_of(start, TILE), TILE)


def attention_end(
    grad_heads, normed, small, weights, side, extras, post, sizes, number
):
    X, C, Z, Y = sizes
    group, total = grad_heads.shape
    width = normed.shape[1]
    own = group // Z
    near, skip = 2 * DK + DV, 2 * DK + 2 * DV
    wide = near + SMALL
    rows = width // (X * C * Y * Z)
    piece = Z * rows
    block = width // (C * X)
    kept = width // 2 // TILE
    others = X * Y - 1

    def body(*refs):
        gh_ref, normed_ref, small_ref = refs[:3]
        extra_refs = refs[3 : 3 + len(extras)]
        w_hbm, side_ref, out_ref, near_out, side_out = refs[3 + len(extras) : 8 + len(extras)]
        (w_ref, partial, given, received, sums, parts, final, load_sem, pair_send, pair_arrive,
         far_send, far_arrive) = refs[8 + len(extras) : 20 + len(extras)]
        sems = refs[20 + len(extras) :]
        x, core, me, y = (lax.axis_index(name) for name in OWN)
        scatter = Scatter("z", Z, PIECES, partial, out_ref, *sems[:4])
        near_swap = Swap("z", Z, final, near_out, *sems[4:7])
        side_swap = Swap("z", Z, side_ref, side_out, *sems[7:10])
        load = pltpu.make_async_copy(w_hbm, w_ref, load_sem)
        load.start()

        def across(offset, sign):
            down, right = offset // Y, offset % Y
            if sign < 0:
                down, right = X - down, Y - right
            return lax.rem(x + down, X), lax.rem(y + right, Y)

        peers = all_peers("z", Z) + [(True, {"c": 1 - core})]
        for offset in range(1, others + 1):
            to_x, to_y = across(offset, 1)
            peers.append((True, {"x": to_x, "y": to_y}))
        greet(peers)

        def backward(at_rows):
            for at in range(0, width, TILE):
                columns = pl.ds(at, TILE)
                partial[at_rows, columns] = dot_rows(gh_ref[at_rows], w_ref[columns]).astype(BF)

        def rows_at(index, size):
            return pl.ds(pl.multiple_of(index * size, size), size)

        lower = me < Z // 2
        load.wait()
        backward(rows_at(jnp.where(lower, Z - 1, 0), own))
        scatter.start([0])
        backward(rows_at(jnp.where(lower, Z // 2, Z // 2 - 1), own))
        scatter.start([1])
        backward(rows_at(me // (Z // 2), group // 2))
        scatter.start([2])

        def pass_over(i):
            return remote(
                given.at[i], received.at[i], pair_send.at[i], pair_arrive.at[i], "c", 1 - core
            )

        def products(i, by):
            at = rows_of_core(block, i, by)
            top = dot_cols(normed_ref[:, at], gh_ref[:, :near])
            low = dot_cols(normed_ref[:, at], gh_ref[:, skip:]) + small_ref[at]
            return top, low

        for i in range(kept):
            top, low = products(i, 1 - core)
            given[i, :, :near] = top.astype(BF)
            given[i, :, near:] = low.astype(BF)
            pass_over(i).start()
        for i in range(kept):
            top, low = products(i, core)
            pass_over(i).wait_recv()
            at = pl.ds(i * TILE, TILE)
            sums[at, :near] = (top + received[i, :, :near].astype(F32)).astype(BF)
            sums[at, near:] = (low + received[i, :, near:].astype(F32)).astype(BF)

        def far(offset, by=1):
            to_x, to_y = across(offset, by)
            return pltpu.make_async_remote_copy(
                src_ref=sums.at[rows_at(to_x * Y + to_y, piece)], dst_ref=parts.at[offset - 1],
                send_sem=far_send.at[offset - 1], recv_sem=far_arrive.at[offset - 1],
                device_id={"x": to_x, "y": to_y}, device_id_type=pl.DeviceIdType.MESH,
            )

        for offset in range(1, others + 1):
            far(offset).start()
        for step in range(Z - 2):
            scatter.run(step, False)
            scatter.run(step, True)
        side_swap.start()
        own_sum = sums[rows_at(x * Y + y, piece)].astype(F32)
        for offset in range(1, others + 1):
            far(offset).wait_recv()
            own_sum = own_sum + parts[offset - 1].astype(F32)
        for index in range(Z):
            final[index] = own_sum[index * rows : (index + 1) * rows].astype(BF)
        near_swap.start()
        scatter.run(Z - 2, False)
        scatter.run(Z - 2, True)
        scatter.finish()
        out_ref[...] = post(out_ref[...], *[r[...] for r in extra_refs])
        side_swap.finish()
        near_swap.finish()
        for offset in range(1, others + 1):
            far(offset).wait_send()
        for i in range(kept):
            pass_over(i).wait_send()

    in_vmem, anywhere = pl.BlockSpec(memory_space=pltpu.VMEM), pl.BlockSpec(memory_space=pl.ANY)
    return pl.pallas_call(
        body,
        in_specs=[in_vmem] * (3 + len(extras)) + [anywhere] * 2,
        out_specs=[in_vmem, anywhere, anywhere],
        out_shape=[
            jax.ShapeDtypeStruct((own, width), F32),
            jax.ShapeDtypeStruct((Z, rows, wide), BF),
            jax.ShapeDtypeStruct(side.shape, BF),
        ],
        scratch_shapes=[
            pltpu.VMEM((width, total), BF),
            pltpu.VMEM((group, width), BF),
            pltpu.VMEM((kept, TILE, wide), BF),
            pltpu.VMEM((kept, TILE, wide), BF),
            pltpu.VMEM((width // 2, wide), BF),
            pltpu.VMEM((max(others, 1), piece, wide), BF),
            pltpu.VMEM((Z, rows, wide), BF),
            pltpu.SemaphoreType.DMA,
            pltpu.SemaphoreType.DMA((kept,)),
            pltpu.SemaphoreType.DMA((kept,)),
            pltpu.SemaphoreType.DMA((max(others, 1),)),
            pltpu.SemaphoreType.DMA((max(others, 1),)),
        ]
        + Scatter.scratch(Z, own, width, PIECES)
        + Swap.scratch(Z)
        + Swap.scratch(Z),
        compiler_params=pltpu.CompilerParams(
            collective_id=number, has_side_effects=True, vmem_limit_bytes=56 * 1024 * 1024
        ),
        cost_estimate=pl.CostEstimate(
            flops=WAIT_FLOPS, bytes_accessed=width * total * 6, transcendentals=0
        ),
        name="attention_end",
    )(grad_heads, normed, small, *extras, weights, side)


def join(values, parts, weights=()):
    Z, rows = values[0].shape[:2]

    def body(*refs):
        ins, refs = refs[: len(values)], refs[len(values) :]
        w_refs, outs = refs[: len(weights)], refs[len(weights) :]
        moment = jnp.zeros((rows, 1), F32)
        for number, (out_ref, (index, start, size)) in enumerate(zip(outs, parts)):
            held = ins[index][0, :, start : start + size].astype(F32)
            out_ref[...] = held
            if number < len(weights):
                product = held * w_refs[number][...].astype(F32)
                moment = moment + jnp.sum(product, axis=1, keepdims=True)
        if weights:
            before = jnp.where(pl.program_id(0) == 0, 0.0, outs[-1][...])
            outs[-1][...] = before + moment

    return pl.pallas_call(
        body,
        grid=(Z,),
        in_specs=[pl.BlockSpec((1,) + v.shape[1:], lambda i: (i, 0, 0)) for v in values]
        + [pl.BlockSpec((rows, w.shape[1] // Z), lambda i: (0, i)) for w in weights],
        out_specs=[pl.BlockSpec((rows, part[2]), lambda i: (0, i)) for part in parts]
        + [pl.BlockSpec((rows, LANES), lambda i: (0, 0))] * (len(weights) > 0),
        out_shape=[jax.ShapeDtypeStruct((rows, Z * part[2]), F32) for part in parts]
        + [jax.ShapeDtypeStruct((rows, LANES), F32)] * (len(weights) > 0),
        compiler_params=pltpu.CompilerParams(dimension_semantics=("arbitrary",)),
        name="join",
    )(*values, *weights)


def local(
    tokens, doc_lengths, cotangent, attn_gain, query_weight, key_weight, value_weight, gate_weight,
    rank_in, rank_out, decay_bias, head_gain, out_weight, mlp_gain, mlp_gate_weight,
    mlp_up_weight, down_weight,
):
    own, width = tokens.shape
    rows = query_weight.shape[0]
    X, C, Z, Y = (lax.axis_size(name) for name in OWN)
    z = lax.axis_index("z")
    group = own * Z
    total = group * Y
    ff = down_weight.shape[1] // Z
    dvp = DV // Y

    def blocked(value):
        lead = value.shape[:-1]
        cut = value.reshape(lead + (X, C, Z, Y, rows))
        return jnp.swapaxes(cut, -3, -2).reshape(lead + (width,))

    def straight(value):
        found = []
        for start in range(0, width, Z * Y * rows):
            for at_z in range(Z):
                for at_y in range(Y):
                    first_lane = start + (at_y * Z + at_z) * rows
                    found.append(value[:, first_lane : first_lane + rows])
        return jnp.concatenate(found, axis=1)

    def pad_rows(value):
        flat = value.reshape(value.shape[0], -1)
        return jnp.pad(flat, ((0, rows - flat.shape[0]), (0, 0)))

    numbers = iter(range(32))

    def deal(value, forth):
        return move(next(numbers), deals=[(value, "y", forth)])[0]

    def after(value, *others):
        return lax.optimization_barrier((value,) + others)[0]

    def scatter_rest(value, axes=REST):
        sums = lax.psum_scatter(value, axes, scatter_dimension=0, tiled=True)
        return sums.reshape(Z, rows, -1)

    def gather_rest(value, axes=REST):
        return lax.all_gather(value.reshape(Z * rows, -1), axes, axis=0, tiled=True)

    small = jnp.concatenate(
        [
            rank_in, pad_rows(attn_gain), pad_rows(mlp_gain), pad_rows(rank_out),
            pad_rows(decay_bias), pad_rows(head_gain),
        ],
        axis=1,
    )
    small = jnp.pad(small, ((0, 0), (0, SMALL - small.shape[1])))
    own_tokens = blocked(tokens)
    input_weights, group_tokens, out_weights = spread_and_gather(
        [query_weight, key_weight, value_weight, gate_weight, small],
        own_tokens, out_weight, (X, C, Z, Y), next(numbers),
    )
    input_weights = input_weights.reshape(width, -1)

    projected = 2 * DK + 2 * DV
    near = 2 * DK + DV
    small_all = input_weights[:, projected:].astype(F32)

    def device_rows(value, count):
        cut = value.reshape(X, C, Y, Z, rows, -1)[:, :, :, :, : rows // count]
        return jnp.swapaxes(cut, 2, 3).reshape(width // count, -1)

    attn_gain_all = small_all[:, R]
    mlp_gain_all = small_all[:, R + 1]
    rank_out_all = device_rows(small_all[:, R + 2 : 2 * R + 2], width // (H * DK))
    bias_all = device_rows(small_all[:, 2 * R + 2 : 2 * R + 3], width // (H * DK))
    head_gain_all = device_rows(small_all[:, 2 * R + 3 : 2 * R + 4], width // DV)[:, 0]
    rank_out_z = lax.dynamic_slice_in_dim(rank_out_all, z * DK, DK).astype(BF)
    bias_z = lax.dynamic_slice_in_dim(bias_all, z * DK, DK)[:, 0]

    def to_device_rows(value, count):
        cut = value.reshape(X, C, Z, Y, rows // count, -1)
        cut = jnp.swapaxes(cut, 2, 3)
        cut = jnp.pad(cut, ((0, 0),) * 4 + ((0, rows - rows // count), (0, 0)))
        return cut.reshape(width, -1)

    def at_head(value):
        return lax.dynamic_update_slice_in_dim(
            jnp.zeros((H * DK, value.shape[1]), F32), value, z * DK, 0
        )

    rows_in = group_tokens.astype(F32)
    scale_in = lax.rsqrt(jnp.mean(rows_in * rows_in, axis=1, keepdims=True) + norm_eps)
    normed_in = (rows_in * scale_in * attn_gain_all).astype(BF)
    heads = dot_plain(normed_in, input_weights)
    out_gate = heads[:, 2 * DK + DV : projected]
    low = heads.astype(BF)
    rank_beside_one = jnp.concatenate(
        [
            jnp.zeros((group, RANK_AT), BF), low[:, projected : projected + R],
            jnp.ones((group, 1), BF), jnp.zeros((group, SMALL - RANK_AT - R - 1), BF),
        ],
        axis=1,
    )
    shared = jnp.concatenate([low[:, : 2 * DK], low[:, projected:]], axis=1)
    values = jnp.swapaxes(low[:, 2 * DK : 2 * DK + DV].reshape(group, Y, dvp), 0, 1)
    sent = jnp.concatenate([jnp.broadcast_to(shared[None], (Y,) + shared.shape), values], axis=2)
    mlp_weights, sequence = move(
        next(numbers), cuts=[([mlp_gate_weight, mlp_up_weight, down_weight], "z")],
        deals=[(sent.reshape(Y, Z, own, -1), "y", True)],
    )
    out_piece = gather_rest(out_weights)
    mlp_piece = gather_rest(mlp_weights)
    sequence = sequence.reshape(total, -1)
    queries = sequence[:, :DK]
    keys = sequence[:, DK : 2 * DK]
    rank_low = sequence[:, 2 * DK : 2 * DK + R]
    value_part = sequence[:, 2 * DK + SMALL :]
    decay_logit = dot_rows(rank_low, rank_out_z) + bias_z
    log_decay = jax.nn.log_sigmoid(decay_logit) / decay_norm

    doc_ends = jnp.cumsum(doc_lengths[0])
    positions = lax.iota(jnp.int32, total)
    segments = jnp.sum((doc_ends[None, :] <= positions[:, None]).astype(jnp.int32), axis=1)
    cut = segments.reshape(-1, CHUNK)
    last = cut[:, CHUNK - 1 :]
    before = jnp.concatenate([jnp.full((1, 1), -1, jnp.int32), last[:-1]], axis=0)
    aux = jnp.stack(
        [cut == before, cut == last, cut, jnp.broadcast_to(last == before, cut.shape)], axis=-1
    )
    aux = aux.reshape(total, 4).astype(F32)
    seg_rows = cut.astype(F32)[:, None, :]

    mixed_part, enter, scores = mix_forward(queries, keys, value_part, log_decay, aux, seg_rows)
    mixed_part = deal(mixed_part.reshape(Z, Y, own, dvp), False).reshape(Y, group, dvp)
    mixed = jnp.swapaxes(mixed_part, 0, 1).reshape(group, DV).astype(F32)

    head_scale = lax.rsqrt(jnp.mean(mixed * mixed, axis=1, keepdims=True) + head_eps)
    head_hat = mixed * head_scale
    head_out = head_hat * head_gain_all
    sig_out = jax.nn.sigmoid(out_gate)
    silu_out = out_gate * sig_out
    gated = (head_out * silu_out).astype(BF)
    own_cotangent = blocked(cotangent)
    residual, group_cotangent = move(
        next(numbers), scatter=(dot_rows(gated, out_piece).astype(BF), "z"),
        gathers=[(own_cotangent, "z")], extras=[own_tokens],
        post=lambda total_sum, x: total_sum + x.astype(F32),
    )
    scale_mid = lax.rsqrt(jnp.mean(residual * residual, axis=1, keepdims=True) + norm_eps)
    hat_mid = residual * scale_mid
    normed_mlp = (hat_mid * mlp_gain_all).astype(BF)
    grad_normed_mlp, out_partial, mlp_partial = feed_forward(
        normed_mlp, mlp_piece, group_cotangent, next(numbers)
    )
    mlp_sums = scatter_rest(mlp_partial, ("x", "y"))

    scaled = grad_normed_mlp * mlp_gain_all
    grad_residual = own_cotangent.astype(F32) + scale_mid * (
        scaled - hat_mid * jnp.mean(scaled * hat_mid, axis=1, keepdims=True)
    )
    branch_own = grad_residual.astype(BF)
    layer_out, grad_branch = move(
        next(numbers), scatter=(out_partial, "z"), gathers=[(branch_own, "z")],
        extras=[residual], post=lambda total_sum, rest: straight(total_sum + rest),
    )
    grad_gated = dot_plain(grad_branch, out_piece)
    grad_head = grad_gated * silu_out
    head_gain_part = jnp.sum(grad_head * head_hat, axis=0)
    head_small = jnp.pad(
        to_device_rows(head_gain_part[:, None], width // DV), ((0, 0), (HEAD_AT, SMALL - HEAD_AT - 1))
    )
    from_head = grad_head * head_gain_all
    grad_mixed = head_scale * (
        from_head - head_hat * jnp.mean(from_head * head_hat, axis=1, keepdims=True)
    )
    grad_out_gate = (grad_gated * head_out * sig_out * (1.0 + out_gate * (1.0 - sig_out))).astype(BF)
    grad_cut = jnp.swapaxes(grad_mixed.astype(BF).reshape(group, Y, dvp), 0, 1)
    grad_part = deal(grad_cut.reshape(Y, Z, own, dvp), True).reshape(total, dvp)
    dq, dk, dv, dld = mix_backward(
        queries, keys, value_part, log_decay, aux, seg_rows, enter, scores, grad_part
    )
    dlogit = (dld * jax.nn.sigmoid(-decay_logit) / decay_norm).astype(BF)
    back = jnp.concatenate([dq, dk, dlogit, dv], axis=1).reshape(Z, Y, own, -1)
    side_partial = jnp.concatenate(
        [dot_cols(normed_in, grad_out_gate), dot_cols(grad_branch, gated)], axis=1
    ).astype(BF)
    back, side_partial = lax.optimization_barrier((back, side_partial))
    side_sums = scatter_rest(after(side_partial, mlp_sums))
    mlp_rows, back = move(
        next(numbers), swaps=[(mlp_sums, "z")], deals=[(back, "y", False)]
    )
    back = back.reshape(Y, group, -1)
    summed = jnp.sum(back[:, :, : 3 * DK].astype(F32), axis=0).astype(BF)
    grad_value = jnp.swapaxes(back[:, :, 3 * DK :], 0, 1).reshape(group, DV)
    grad_logit = summed[:, 2 * DK :]
    rank_out_part = dot_cols(grad_logit, rank_beside_one)
    grad_rank = dot_plain(grad_logit, rank_out_z).astype(BF)
    grad_heads = jnp.concatenate(
        [
            summed[:, : 2 * DK], grad_value, grad_out_gate,
            jnp.pad(grad_rank, ((0, 0), (0, SMALL - R))),
        ],
        axis=1,
    )
    small_part = to_device_rows(at_head(rank_out_part), width // (H * DK)) + head_small

    def finish_tokens(back_sum, x, grad_res, gain):
        held = x.astype(F32)
        scale = lax.rsqrt(jnp.mean(held * held, axis=1, keepdims=True) + norm_eps)
        hat = held * scale
        scaled = back_sum * gain
        mean = jnp.mean(scaled * hat, axis=1, keepdims=True)
        return straight(grad_res + scale * (scaled - hat * mean))

    tokens_grad, near_rows, side_rows = attention_end(
        grad_heads, normed_in, small_part, input_weights, side_sums,
        [own_tokens, grad_residual, attn_gain_all[None]], finish_tokens, (X, C, Z, Y),
        next(numbers),
    )
    *mlp_grads, mlp_moments = join(
        [mlp_rows], [(0, 0, ff), (0, ff, ff), (0, 2 * ff, ff)], [mlp_gate_weight, mlp_up_weight]
    )
    query_grad, key_grad, value_grad, gate_grad, out_grad, moments = join(
        [near_rows, side_rows],
        [
            (0, 0, DK), (0, DK, DK), (0, 2 * DK, DV), (1, 0, DV), (1, DV, DV),
        ],
        [query_weight, key_weight, value_weight, gate_weight],
    )
    small_rows = jnp.sum(near_rows[:, :, near : near + SMALL].astype(F32), axis=0)
    rank_in_grad = small_rows[:, :R]
    moment = moments[:, 0] + jnp.sum(rank_in_grad * rank_in.astype(F32), axis=1)
    return (
        layer_out,
        tokens_grad,
        moment / attn_gain.astype(F32),
        query_grad,
        key_grad,
        value_grad,
        gate_grad,
        rank_in_grad,
        small_rows[: rows * H * DK // width, RANK_AT : RANK_AT + R],
        small_rows[: rows * H * DK // width, RANK_AT + R],
        small_rows[: rows * DV // width, HEAD_AT],
        out_grad,
        mlp_moments[:, 0] / mlp_gain.astype(F32),
        *mlp_grads,
    )


def solution(mesh):
    groups, places = mesh.shape["grp"], mesh.shape["seq"]
    wide = Mesh(mesh.devices.reshape(groups // 2, 2, H, places // H), OWN)
    split = P(OWN, None)
    line = P(OWN)
    by_sequence = P(("x", "c"), None)
    placed = (
        split, by_sequence, split, line, split, split, split, split, split, split,
        line, line, split, line, split, split, split,
    )
    return jax.shard_map(
        local,
        mesh=wide,
        in_specs=placed,
        out_specs=(
            split, split, line, split, split, split, split, split, split, line, line, split,
            line, split, split, split,
        ),
        check_vma=False,
    )
```

```python
import functools

import jax
import jax.numpy as jnp
import numpy as np
from jax import lax
from jax.experimental import pallas as pl
from jax.experimental.pallas import tpu as pltpu
from jax.sharding import Mesh
from jax.sharding import PartitionSpec as P

H = 4
DK = 256
DV = 512
R = 16
CHUNK = 128
LEVELS = 7
SMALL = 128
RANK_AT = 32
HEAD_AT = 64
WAIT_FLOPS = 100_000_000
LANES = 128
TILE = 256
PIECES = 2
norm_eps = 1e-06
head_eps = 0.25
decay_norm = 16.0
BF = jnp.bfloat16
F32 = jnp.float32
REST = ("x", "c", "y")
OWN = ("x", "c", "z", "y")


def dot_plain(left, right):
    return jnp.dot(left, right, preferred_element_type=F32)


def dot_rows(left, right):
    return lax.dot_general(left, right, (((1,), (1,)), ((), ())), preferred_element_type=F32)


def dot_cols(left, right):
    return lax.dot_general(left, right, (((0,), (0,)), ((), ())), preferred_element_type=F32)


def split_two(value):
    high = value.astype(BF)
    return jnp.concatenate([high, (value - high.astype(F32)).astype(BF)], axis=1)


def sum_two(value):
    half = value.shape[1] // 2
    return value[:, :half] + value[:, half:]


def chunk_tables():
    t = np.arange(CHUNK)[:, None]
    j = np.arange(CHUNK)[None, :]
    parts = []
    level = np.full((CHUNK, CHUNK), -1, np.int32)
    for number in range(LEVELS):
        half = CHUNK >> (number + 1)
        middle = t // (2 * half) * (2 * half) + half - 1
        upper = t % (2 * half) >= half
        parts.append(np.where(upper, (j > middle) & (j <= t), (j > t) & (j <= middle)))
        pair = (t // (2 * half) == j // (2 * half)) & upper & (j % (2 * half) < half)
        level[pair] = number
    level[np.arange(CHUNK), np.arange(CHUNK)] = LEVELS
    parts.append(j <= t)
    parts.append(j > t)
    return np.concatenate(parts, axis=0).astype(np.float32), level


def upper_rows(number):
    half = CHUNK >> (number + 1)
    rows = lax.broadcasted_iota(jnp.int32, (CHUNK, 1), 0)
    return lax.rem(rows, 2 * half) >= half


def factors(ld_ref, sums_ref):
    exponents = sum_two(dot_plain(sums_ref[...], split_two(ld_ref[...])))
    return jnp.exp(exponents)


def rows_of(value, number):
    return value[number * CHUNK : (number + 1) * CHUNK]


def mix_forward_body(
    q_ref, k_ref, v_ref, ld_ref, aux_ref, seg_ref, sums_ref, level_ref,
    out_ref, enter_ref, score_ref, state,
):
    @pl.when(pl.program_id(0) == 0)
    def _():
        state[...] = jnp.zeros_like(state)

    factor = factors(ld_ref, sums_ref)
    query = q_ref[...].astype(F32) * DK ** (-0.5)
    key = k_ref[...].astype(F32)
    level = level_ref[...]
    aux = aux_ref[...]
    scores = jnp.where(level == LEVELS, dot_rows(query.astype(BF), k_ref[...]), 0.0)
    for number in range(LEVELS):
        part = rows_of(factor, number)
        pairs = dot_rows((query * part).astype(BF), (key * part).astype(BF))
        scores = jnp.where(level == number, pairs, scores)
    scores = jnp.where(aux[:, 2:3] == seg_ref[0], scores, 0.0).astype(BF)
    score_ref[0] = scores
    cumulative = rows_of(factor, LEVELS)
    enter = state[...].astype(BF)
    enter_ref[0] = enter
    lifted = (query * cumulative * aux[:, 0:1]).astype(BF)
    ending = (key * rows_of(factor, LEVELS + 1) * aux[:, 1:2]).astype(BF)
    out = dot_plain(scores, v_ref[...]) + dot_rows(lifted, enter)
    out_ref[...] = out.astype(out_ref.dtype)
    through = cumulative[CHUNK - 1 :] * aux[0:1, 3:4]
    state[...] = state[...] * through + dot_cols(v_ref[...], ending)


def mix_backward_body(
    q_ref, k_ref, v_ref, ld_ref, aux_ref, seg_ref, sums_ref, sums_t_ref, level_ref, level_t_ref,
    enter_ref, score_ref, do_ref,
    dq_ref, dk_ref, dv_ref, dld_ref, state,
):
    @pl.when(pl.program_id(0) == 0)
    def _():
        state[...] = jnp.zeros_like(state)

    factor = factors(ld_ref, sums_ref)
    scale = DK ** (-0.5)
    query = q_ref[...].astype(F32) * scale
    key = k_ref[...].astype(F32)
    value = v_ref[...]
    grad = do_ref[...]
    level = level_ref[...]
    level_t = level_t_ref[...]
    aux = aux_ref[...]
    same = aux[:, 2:3] == seg_ref[0]
    weight = jnp.where(same, dot_rows(grad, value), 0.0)
    weight_t = jnp.where(same, dot_rows(value, grad), 0.0)
    diagonal = jnp.sum(jnp.where(level == LEVELS, weight, 0.0), axis=1, keepdims=True)
    dq = diagonal * key
    dk = diagonal * query
    moved = []
    for number in range(LEVELS):
        part = rows_of(factor, number)
        left = jnp.concatenate(
            [
                jnp.where(level == number, weight, 0.0).astype(BF),
                jnp.where(level_t == number, weight_t, 0.0).astype(BF),
            ],
            axis=1,
        )
        right = jnp.concatenate([(key * part).astype(BF), (query * part).astype(BF)], axis=0)
        both = dot_plain(left, right) * part
        upper = upper_rows(number)
        dq = dq + jnp.where(upper, both, 0.0)
        dk = dk + jnp.where(upper, 0.0, both)
        moved.append(both * jnp.where(upper, query, key))
    cumulative = rows_of(factor, LEVELS)
    enter = enter_ref[0]
    after = state[...]
    after_low = after.astype(BF)
    lift = cumulative * aux[:, 0:1]
    finish = rows_of(factor, LEVELS + 1) * aux[:, 1:2]
    lifted = query * lift
    ending = key * finish
    from_enter = dot_plain(grad, enter)
    from_after = dot_plain(value, after_low)
    moved.append(lifted * from_enter)
    moved.append(ending * from_after)
    dq_ref[...] = ((dq + lift * from_enter) * scale).astype(dq_ref.dtype)
    dk_ref[...] = (dk + finish * from_after).astype(dk_ref.dtype)
    dv = dot_cols(score_ref[0], grad) + dot_rows(ending.astype(BF), after_low)
    dv_ref[...] = dv.astype(dv_ref.dtype)
    through = cumulative[CHUNK - 1 :] * aux[0:1, 3:4]
    passing = jnp.sum(after * enter.astype(F32), axis=0, keepdims=True) * through
    spread = sum_two(dot_plain(sums_t_ref[...], split_two(jnp.concatenate(moved, axis=0))))
    dld_ref[...] = spread + passing
    state[...] = after * through + dot_cols(grad, lifted.astype(BF))


def mix_specs(count, width, backward):
    def at(i):
        return count - 1 - i if backward else i

    def tokens(columns):
        return pl.BlockSpec((CHUNK, columns), lambda i: (at(i), 0))

    def chunks(rows, columns):
        return pl.BlockSpec((1, rows, columns), lambda i: (at(i), 0, 0))

    def whole(rows, columns):
        return pl.BlockSpec((rows, columns), lambda i: (0, 0))

    return tokens, chunks, whole


def mix_forward(query, key, value, log_decay, aux, seg_rows):
    total, width = value.shape
    count = total // CHUNK
    sums, level = chunk_tables()
    tokens, chunks, whole = mix_specs(count, width, False)
    return pl.pallas_call(
        mix_forward_body,
        grid=(count,),
        in_specs=[
            tokens(DK), tokens(DK), tokens(width), tokens(DK), tokens(aux.shape[1]),
            chunks(1, CHUNK), whole(*sums.shape), whole(CHUNK, CHUNK),
        ],
        out_specs=[tokens(width), chunks(width, DK), chunks(CHUNK, CHUNK)],
        out_shape=[
            jax.ShapeDtypeStruct((total, width), BF),
            jax.ShapeDtypeStruct((count, width, DK), BF),
            jax.ShapeDtypeStruct((count, CHUNK, CHUNK), BF),
        ],
        scratch_shapes=[pltpu.VMEM((width, DK), F32)],
        compiler_params=pltpu.CompilerParams(
            dimension_semantics=("arbitrary",), vmem_limit_bytes=32 * 1024 * 1024
        ),
        cost_estimate=pl.CostEstimate(
            flops=total * 2 * (8 * CHUNK * DK + 2 * width * DK + CHUNK * width + 18 * CHUNK * DK),
            bytes_accessed=total * 4096, transcendentals=total * 9 * DK,
        ),
        name="mix_forward",
    )(query, key, value, log_decay, aux, seg_rows, jnp.asarray(sums, BF), jnp.asarray(level))


def mix_backward(query, key, value, log_decay, aux, seg_rows, enter, scores, grad):
    total, width = value.shape
    count = total // CHUNK
    sums, level = chunk_tables()
    tokens, chunks, whole = mix_specs(count, width, True)
    return pl.pallas_call(
        mix_backward_body,
        grid=(count,),
        in_specs=[
            tokens(DK), tokens(DK), tokens(width), tokens(DK), tokens(aux.shape[1]),
            chunks(1, CHUNK), whole(*sums.shape), whole(*sums.shape[::-1]),
            whole(CHUNK, CHUNK), whole(CHUNK, CHUNK),
            chunks(width, DK), chunks(CHUNK, CHUNK), tokens(width),
        ],
        out_specs=[tokens(DK), tokens(DK), tokens(width), tokens(DK)],
        out_shape=[
            jax.ShapeDtypeStruct((total, DK), BF),
            jax.ShapeDtypeStruct((total, DK), BF),
            jax.ShapeDtypeStruct((total, width), BF),
            jax.ShapeDtypeStruct((total, DK), F32),
        ],
        scratch_shapes=[pltpu.VMEM((width, DK), F32)],
        compiler_params=pltpu.CompilerParams(
            dimension_semantics=("arbitrary",), vmem_limit_bytes=48 * 1024 * 1024
        ),
        cost_estimate=pl.CostEstimate(
            flops=total * 2 * (14 * CHUNK * DK + 4 * width * DK + CHUNK * width + 36 * CHUNK * DK),
            bytes_accessed=total * 6144, transcendentals=total * 9 * DK,
        ),
        name="mix_backward",
    )(
        query, key, value, log_decay, aux, seg_rows, jnp.asarray(sums, BF),
        jnp.asarray(np.ascontiguousarray(sums.T), BF), jnp.asarray(level),
        jnp.asarray(np.ascontiguousarray(level.T)), enter, scores, grad,
    )


def remote(source, target, send, arrive, axis, place):
    return pltpu.make_async_remote_copy(
        src_ref=source, dst_ref=target, send_sem=send, recv_sem=arrive,
        device_id={axis: place}, device_id_type=pl.DeviceIdType.MESH,
    )


def greet(peers):
    barrier = pltpu.get_barrier_semaphore()
    number = 0
    for present, peer in peers:
        if present is True:
            pl.semaphore_signal(
                barrier, inc=1, device_id=peer, device_id_type=pl.DeviceIdType.MESH
            )
            number = number + 1
        else:

            @pl.when(present)
            def _():
                pl.semaphore_signal(
                    barrier, inc=1, device_id=peer, device_id_type=pl.DeviceIdType.MESH
                )

            number = number + jnp.where(present, 1, 0)
    pl.semaphore_wait(barrier, number)


def line_peers(axis, count):
    me = lax.axis_index(axis)
    return [(me > 0, {axis: me - 1}), (me < count - 1, {axis: me + 1})]


def all_peers(axis, count):
    me = lax.axis_index(axis)
    return [(True, {axis: lax.rem(me + away, count)}) for away in range(1, count)]


class Gather:
    def __init__(self, axis, count, x_ref, out_ref, send, arrive, local_sem):
        self.axis, self.count, self.x_ref, self.out_ref = axis, count, x_ref, out_ref
        self.send, self.arrive = send, arrive
        self.me = lax.axis_index(axis)
        self.mine = pltpu.make_async_copy(x_ref, self.block(self.me), local_sem)

    def block(self, index):
        own = self.x_ref.shape[0]
        return self.out_ref.at[pl.ds(pl.multiple_of(index * own, own), own)]

    def copy(self, direction, step, index, source):
        return remote(
            source, self.block(index), self.send.at[direction, step],
            self.arrive.at[direction, step], self.axis,
            self.me + 1 if direction == 0 else self.me - 1,
        )

    def hop(self, direction, step):
        index = self.me - step if direction == 0 else self.me + step
        return self.copy(direction, step, index, self.x_ref if step == 0 else self.block(index))

    def landed(self, direction, step):
        index = self.me - 1 - step if direction == 0 else self.me + 1 + step
        return self.copy(direction, step, index, self.block(index))

    def holds(self, direction, step):
        return self.me - step >= 0 if direction == 0 else self.me + step <= self.count - 1

    def hands_on(self, direction, step):
        inner = self.me < self.count - 1 if direction == 0 else self.me > 0
        return self.holds(direction, step) & inner

    def start(self):
        self.mine.start()
        self.run(0)

    def run(self, first, last=None):
        for step in range(first, first + 1 if last is None else last):
            for direction in (0, 1):
                if step > 0:

                    @pl.when(self.holds(direction, step))
                    def _():
                        self.landed(direction, step - 1).wait_recv()

                if step < self.count - 1:

                    @pl.when(self.hands_on(direction, step))
                    def _():
                        self.hop(direction, step).start()

    def finish(self):
        self.finish_sends()
        self.mine.wait()

    def finish_sends(self):
        for step in range(self.count - 1):
            for direction in (0, 1):

                @pl.when(self.hands_on(direction, step))
                def _():
                    self.hop(direction, step).wait_send()

    @staticmethod
    def scratch(count):
        return [
            pltpu.SemaphoreType.DMA((2, count - 1)),
            pltpu.SemaphoreType.DMA((2, count - 1)),
            pltpu.SemaphoreType.DMA,
        ]


class Swap:
    def __init__(self, axis, count, x_ref, out_ref, send, arrive, local_sem):
        self.axis, self.count, self.x_ref, self.out_ref = axis, count, x_ref, out_ref
        self.send, self.arrive = send, arrive
        self.me = lax.axis_index(axis)
        self.mine = pltpu.make_async_copy(x_ref.at[self.me], out_ref.at[self.me], local_sem)

    def hop(self, away):
        peer = lax.rem(self.me + away, self.count)
        return remote(
            self.x_ref.at[peer], self.out_ref.at[self.me], self.send.at[away - 1],
            self.arrive.at[away - 1], self.axis, peer,
        )

    def landed(self, away):
        peer = lax.rem(self.me + self.count - away, self.count)
        return remote(
            self.x_ref.at[peer], self.out_ref.at[peer], self.send.at[away - 1],
            self.arrive.at[away - 1], self.axis, peer,
        )

    def start(self):
        self.mine.start()
        for away in range(1, self.count):
            self.hop(away).start()

    def finish(self):
        for away in range(1, self.count):
            self.landed(away).wait_recv()
        for away in range(1, self.count):
            self.hop(away).wait_send()
        self.mine.wait()

    @staticmethod
    def scratch(count):
        return [
            pltpu.SemaphoreType.DMA((count - 1,)),
            pltpu.SemaphoreType.DMA((count - 1,)),
            pltpu.SemaphoreType.DMA,
        ]


class Scatter:
    def __init__(self, axis, count, pieces, x_ref, out_ref, up, down, send, arrive):
        self.axis, self.count, self.pieces = axis, count, pieces
        self.x_ref, self.out_ref, self.held_refs = x_ref, out_ref, (up, down)
        self.send, self.arrive = send, arrive
        self.me = lax.axis_index(axis)
        self.own = out_ref.shape[0]
        self.size = self.own // pieces

    def part(self, index, piece):
        start = pl.multiple_of(index * self.own + piece * self.size, self.size)
        return self.x_ref.at[pl.ds(start, self.size)]

    def held(self, direction, number, piece):
        return self.held_refs[direction].at[number, pl.ds(piece * self.size, self.size)]

    def hop(self, direction, number, piece, source=None):
        held = self.held(direction, number, piece)
        return remote(
            held if source is None else source, held, self.send.at[direction, number, piece],
            self.arrive.at[direction, number, piece], self.axis,
            self.me + 1 if direction == 0 else self.me - 1,
        )

    def target(self, direction, number):
        return self.count - 1 - number if direction == 0 else number

    def start(self, numbers=None):
        for direction in (0, 1):

            @pl.when(self.me == (0 if direction == 0 else self.count - 1))
            def _():
                for number in range(self.count - 1) if numbers is None else numbers:
                    target = self.target(direction, number)
                    for piece in range(self.pieces):
                        self.hop(direction, number, piece, self.part(target, piece)).start()

    def stage(self, direction, number, piece):
        me, target = self.me, self.target(direction, number)
        inner = me > 0 if direction == 0 else me < self.count - 1
        passed = me < target if direction == 0 else me > target
        held = self.held(direction, number, piece)

        @pl.when(inner & (passed | (me == target)))
        def _():
            self.hop(direction, number, piece).wait_recv()

        @pl.when(inner & passed)
        def _():
            mine = self.part(target, piece)[...].astype(F32)
            held[...] = (held[...].astype(F32) + mine).astype(BF)
            self.hop(direction, number, piece).start()

    def run(self, number, far):
        for order in (0, 1):

            @pl.when((self.me >= self.count // 2) == (order == 1))
            def _():
                for piece in range(self.pieces):
                    self.stage(1 - order if far else order, number, piece)

    def finish(self):
        me, count, out_ref = self.me, self.count, self.out_ref
        for piece in range(self.pieces):
            rows = pl.ds(piece * self.size, self.size)
            out_ref[rows] = self.part(me, piece)[...].astype(F32)
            for direction in (0, 1):
                for number in range(count - 1):
                    inner = me > 0 if direction == 0 else me < count - 1

                    @pl.when((me == self.target(direction, number)) & inner)
                    def _():
                        out_ref[rows] += self.held(direction, number, piece)[...].astype(F32)

        for direction in (0, 1):
            for number in range(count - 1):
                target = self.target(direction, number)

                @pl.when(me < target if direction == 0 else me > target)
                def _():
                    for piece in range(self.pieces):
                        self.hop(direction, number, piece).wait_send()

    @staticmethod
    def scratch(count, own, columns, pieces):
        return [
            pltpu.VMEM((count - 1, own, columns), BF),
            pltpu.VMEM((count - 1, own, columns), BF),
            pltpu.SemaphoreType.DMA((2, count - 1, pieces)),
            pltpu.SemaphoreType.DMA((2, count - 1, pieces)),
        ]


class CutSwap:
    def __init__(self, axis, count, refs, out_ref, send, arrive, local_sem):
        self.axis, self.count, self.refs, self.out_ref = axis, count, refs, out_ref
        self.send, self.arrive = send, arrive
        self.me = lax.axis_index(axis)
        self.widths = [ref.shape[1] // count for ref in refs]
        self.mine = [
            pltpu.make_async_copy(self.cut(i, self.me), self.slot(i, self.me), local_sem.at[i])
            for i in range(len(refs))
        ]

    def cut(self, i, index):
        size = self.widths[i]
        return self.refs[i].at[:, pl.ds(pl.multiple_of(index * size, LANES), size)]

    def slot(self, i, index):
        return self.out_ref.at[index, :, pl.ds(sum(self.widths[:i]), self.widths[i])]

    def hop(self, away, i):
        peer = lax.rem(self.me + away, self.count)
        return remote(
            self.cut(i, peer), self.slot(i, self.me), self.send.at[away - 1, i],
            self.arrive.at[away - 1, i], self.axis, peer,
        )

    def landed(self, away, i):
        peer = lax.rem(self.me + self.count - away, self.count)
        return remote(
            self.cut(i, peer), self.slot(i, peer), self.send.at[away - 1, i],
            self.arrive.at[away - 1, i], self.axis, peer,
        )

    def each(self):
        return [(away, i) for away in range(1, self.count) for i in range(len(self.refs))]

    def start(self):
        for away, i in self.each():
            self.hop(away, i).start()
        for copy in self.mine:
            copy.start()

    def finish(self):
        for away, i in self.each():
            self.landed(away, i).wait_recv()
        for away, i in self.each():
            self.hop(away, i).wait_send()
        for copy in self.mine:
            copy.wait()

    @staticmethod
    def scratch(count, parts):
        sems = pltpu.SemaphoreType.DMA((count - 1, parts))
        return [sems, sems, pltpu.SemaphoreType.DMA((parts,))]


class Deal:
    def __init__(self, axis, count, forth, x_ref, out_ref, send, arrive, local_sem):
        self.axis, self.count, self.forth = axis, count, forth
        self.x_ref, self.out_ref, self.send, self.arrive = x_ref, out_ref, send, arrive
        self.me = lax.axis_index(axis)
        self.steps = x_ref.shape[1] if forth else x_ref.shape[0]
        self.mine = [
            pltpu.make_async_copy(self.given(self.me, k), self.got(self.me, k), local_sem.at[k])
            for k in range(self.steps)
        ]

    def given(self, device, k):
        return self.x_ref.at[device, k] if self.forth else self.x_ref.at[k, device]

    def got(self, device, k):
        return self.out_ref.at[k, device] if self.forth else self.out_ref.at[device, k]

    def hop(self, away, k):
        peer = lax.rem(self.me + away, self.count)
        return remote(
            self.given(peer, k), self.got(self.me, k), self.send.at[away - 1, k],
            self.arrive.at[away - 1, k], self.axis, peer,
        )

    def landed(self, away, k):
        peer = lax.rem(self.me + self.count - away, self.count)
        return remote(
            self.given(peer, k), self.got(peer, k), self.send.at[away - 1, k],
            self.arrive.at[away - 1, k], self.axis, peer,
        )

    def each(self):
        return [(away, k) for away in range(1, self.count) for k in range(self.steps)]

    def start(self):
        for away, k in self.each():
            self.hop(away, k).start()
        for copy in self.mine:
            copy.start()

    def finish(self):
        for away, k in self.each():
            self.landed(away, k).wait_recv()
        for away, k in self.each():
            self.hop(away, k).wait_send()
        for copy in self.mine:
            copy.wait()

    @staticmethod
    def scratch(count, steps):
        sems = pltpu.SemaphoreType.DMA((count - 1, steps))
        return [sems, sems, pltpu.SemaphoreType.DMA((steps,))]


class Spread:
    def __init__(self, sizes, cuts, out_ref, far_send, far_arrive, near_send, near_arrive):
        self.X, self.C, self.Z, self.Y = sizes
        self.cuts, self.out_ref = cuts, out_ref
        self.far_send, self.far_arrive = far_send, far_arrive
        self.near_send, self.near_arrive = near_send, near_arrive
        self.x, self.c, self.z, self.y = (lax.axis_index(name) for name in OWN)
        self.others = self.X * self.Y - 1

    def across(self, offset, sign):
        down, right = offset // self.Y, offset % self.Y
        if sign < 0:
            down, right = self.X - down, self.Y - right
        return lax.rem(self.x + down, self.X), lax.rem(self.y + right, self.Y)

    def place(self, offset, c, slot):
        x, y = self.across(offset, -1)
        z = lax.rem(self.z + self.Z - slot, self.Z)
        return self.out_ref.at[((x * self.C + c) * self.Y + y) * self.Z + z]

    def far(self, offset, slot, landed=False):
        x, y = self.across(offset, 1)
        held = self.place(offset if landed else 0, self.c, slot)
        return pltpu.make_async_remote_copy(
            src_ref=held, dst_ref=held, send_sem=self.far_send.at[offset - 1, slot],
            recv_sem=self.far_arrive.at[offset - 1, slot], device_id={"x": x, "y": y},
            device_id_type=pl.DeviceIdType.MESH,
        )

    def near(self, offset, slot, landed=False):
        held = self.place(offset, 1 - self.c if landed else self.c, slot)
        return remote(
            held, held, self.near_send.at[offset, slot],
            self.near_arrive.at[offset, slot], "c", 1 - self.c,
        )

    def peers(self):
        found = all_peers("z", self.Z) + [(True, {"c": 1 - self.c})]
        for offset in range(1, self.others + 1):
            x, y = self.across(offset, 1)
            found.append((True, {"x": x, "y": y}))
        return found

    def hand_on(self, slot):
        for i in range(len(self.cuts.refs)):
            if slot > 0:
                self.cuts.landed(slot, i).wait_recv()
            else:
                self.cuts.mine[i].wait()
        for offset in range(1, self.others + 1):
            self.far(offset, slot).start()
        self.near(0, slot).start()

    def collect(self, slot):
        for offset in range(1, self.others + 1):
            self.far(offset, slot, True).wait_recv()
            self.near(offset, slot).start()

    def finish(self):
        for slot in range(self.Z):
            for offset in range(self.others + 1):
                self.near(offset, slot, True).wait_recv()
        for slot in range(self.Z):
            for offset in range(self.others + 1):
                self.near(offset, slot).wait_send()
                if offset > 0:
                    self.far(offset, slot).wait_send()
        for away, i in self.cuts.each():
            self.cuts.hop(away, i).wait_send()

    @staticmethod
    def scratch(sizes):
        X, C, Z, Y = sizes
        far = pltpu.SemaphoreType.DMA((max(X * Y - 1, 1), Z))
        near = pltpu.SemaphoreType.DMA((X * Y, Z))
        return [far, far, near, near]


class FirstCuts(CutSwap):
    def __init__(self, spread_place, count, refs, out_ref, send, arrive, local_sem):
        self.place = spread_place
        super().__init__("z", count, refs, out_ref, send, arrive, local_sem)

    def cut(self, i, index):
        return self.refs[i] if i == len(self.refs) - 1 else super().cut(i, index)

    def slot(self, i, index):
        widths = [w for w in self.widths[:-1]] + [SMALL]
        return self.out_ref.at[self.place(index), :, pl.ds(sum(widths[:i]), widths[i])]


def spread_and_gather(weights, block, others, sizes, number):
    X, C, Z, Y = sizes
    parts = len(weights)
    rows = weights[0].shape[0]
    total = sum(w.shape[1] // Z for w in weights[:-1]) + weights[-1].shape[1]

    def body(*refs):
        extra = len(others)
        w_refs, x_ref, o_refs = refs[:parts], refs[parts], refs[parts + 1 : parts + 1 + extra]
        spread_ref, out_ref, swapped_ref = refs[parts + 1 + extra : parts + 4 + extra]
        sems = refs[parts + 4 + extra :]
        x, c, _, y = (lax.axis_index(name) for name in OWN)
        first = FirstCuts(
            lambda index: ((x * C + c) * Y + y) * Z + index, Z, w_refs, spread_ref, *sems[:3]
        )
        spread = Spread(sizes, first, spread_ref, *sems[3:7])
        gather = Gather("z", Z, x_ref, out_ref, *sems[7:10])
        swap = CutSwap("z", Z, o_refs, swapped_ref, *sems[10:])
        greet(spread.peers())
        first.start()
        gather.start()
        spread.hand_on(0)
        for slot in range(1, Z):
            spread.hand_on(slot)
        for step in range(1, Z):
            gather.run(step)
            if step == Z - 2:
                swap.start()
            spread.collect(step - 1)
        spread.collect(Z - 1)
        spread.finish()
        gather.finish()
        swap.finish()

    anywhere = pl.BlockSpec(memory_space=pl.ANY)
    return pl.pallas_call(
        body,
        in_specs=[anywhere] * (parts + 1 + len(others)),
        out_specs=[anywhere] * 3,
        out_shape=[
            jax.ShapeDtypeStruct((X * C * Y * Z, rows, total), BF),
            jax.ShapeDtypeStruct((Z * block.shape[0],) + block.shape[1:], block.dtype),
            jax.ShapeDtypeStruct((Z, rows, sum(w.shape[1] for w in others) // Z), BF),
        ],
        scratch_shapes=CutSwap.scratch(Z, parts)
        + Spread.scratch(sizes)
        + Gather.scratch(Z)
        + CutSwap.scratch(Z, len(others)),
        compiler_params=pltpu.CompilerParams(collective_id=number, has_side_effects=True),
        cost_estimate=pl.CostEstimate(
            flops=WAIT_FLOPS, bytes_accessed=rows * total * X * C * Y * Z * 2, transcendentals=0
        ),
        name="spread_and_gather",
    )(*weights, block, *others)


def move(
    number, scatter=None, swaps=(), gathers=(), cuts=(), deals=(), extras=(), post=None
):
    in_vmem, anywhere = pl.BlockSpec(memory_space=pltpu.VMEM), pl.BlockSpec(memory_space=pl.ANY)
    values, in_specs, shapes, out_specs, scratch = [], [], [], [], []
    flags = {}

    def scale(axis):
        return lax.axis_size(axis)

    if scatter is not None:
        partial, axis = scatter
        own = partial.shape[0] // scale(axis)
        values += [partial, *extras]
        in_specs += [in_vmem] * (1 + len(extras))
        shapes.append(jax.ShapeDtypeStruct((own, partial.shape[1]), F32))
        out_specs.append(in_vmem)
        scratch += Scatter.scratch(scale(axis), own, partial.shape[1], PIECES)
        flags = dict(vmem_limit_bytes=40 * 1024 * 1024)
    for value, axis in swaps:
        values.append(value)
        in_specs.append(anywhere)
        shapes.append(jax.ShapeDtypeStruct(value.shape, value.dtype))
        out_specs.append(anywhere)
        scratch += Swap.scratch(scale(axis))
    for block, axis in gathers:
        values.append(block)
        in_specs.append(anywhere)
        shapes.append(
            jax.ShapeDtypeStruct((scale(axis) * block.shape[0], block.shape[1]), block.dtype)
        )
        out_specs.append(anywhere)
        scratch += Gather.scratch(scale(axis))

    for weights, axis in cuts:
        values += weights
        in_specs += [anywhere] * len(weights)
        wide = sum(w.shape[1] for w in weights) // scale(axis)
        shapes.append(
            jax.ShapeDtypeStruct((scale(axis), weights[0].shape[0], wide), weights[0].dtype)
        )
        out_specs.append(anywhere)
        scratch += CutSwap.scratch(scale(axis), len(weights))
    for value, axis, forth in deals:
        first, second = value.shape[:2]
        values.append(value)
        in_specs.append(anywhere)
        shapes.append(jax.ShapeDtypeStruct((second, first) + value.shape[2:], value.dtype))
        out_specs.append(anywhere)
        scratch += Deal.scratch(scale(axis), second if forth else first)

    def body(*refs):
        ins = list(refs[: len(values)])
        outs = list(refs[len(values) : len(values) + len(shapes)])
        sems = list(refs[len(values) + len(shapes) :])
        peers = {}
        adding, extra_refs, swapping, gathering = None, (), [], []
        if scatter is not None:
            axis = scatter[1]
            adding = Scatter(axis, scale(axis), PIECES, ins.pop(0), outs.pop(0), *sems[:4])
            extra_refs, ins, sems = ins[: len(extras)], ins[len(extras) :], sems[4:]
            peers[axis] = line_peers(axis, scale(axis))
        for _, axis in gathers:
            peers[axis] = line_peers(axis, scale(axis))
        for _, axis in swaps:
            peers[axis] = all_peers(axis, scale(axis))
            swapping.append(Swap(axis, scale(axis), ins.pop(0), outs.pop(0), *sems[:3]))
            sems = sems[3:]
        for _, axis in gathers:
            gathering.append(Gather(axis, scale(axis), ins.pop(0), outs.pop(0), *sems[:3]))
            sems = sems[3:]
        for weights, axis in cuts:
            peers[axis] = all_peers(axis, scale(axis))
            taken, ins = ins[: len(weights)], ins[len(weights) :]
            swapping.append(CutSwap(axis, scale(axis), taken, outs.pop(0), *sems[:3]))
            sems = sems[3:]
        for _, axis, forth in deals:
            peers[axis] = all_peers(axis, scale(axis))
            swapping.append(
                Deal(axis, scale(axis), forth, ins.pop(0), outs.pop(0), *sems[:3])
            )
            sems = sems[3:]
        greet([peer for found in peers.values() for peer in found])
        for part in gathering + ([adding] if adding else []) + swapping:
            part.start()
        steps = max([part.count for part in gathering + ([adding] if adding else [])] + [0])
        for part in gathering:
            part.run(1)
        for step in range(1, steps):
            if adding:
                adding.run(step - 1, False)
            for part in gathering:
                if step + 1 < part.count:
                    part.run(step + 1)
            if adding:
                adding.run(step - 1, True)
        if adding:
            adding.finish()
            if post is not None:
                adding.out_ref[...] = post(adding.out_ref[...], *[r[...] for r in extra_refs])
        for part in swapping + gathering:
            part.finish()

    size = sum(v.size for v in values)
    return pl.pallas_call(
        body,
        in_specs=in_specs,
        out_specs=out_specs,
        out_shape=shapes,
        scratch_shapes=scratch,
        compiler_params=pltpu.CompilerParams(
            collective_id=number, has_side_effects=True, **flags
        ),
        cost_estimate=pl.CostEstimate(
            flops=WAIT_FLOPS, bytes_accessed=size * 4, transcendentals=0
        ),
        name="move",
    )(*values)


def feed_forward(normed_own, mlp_piece, out_down, cotangent, number):
    count = lax.axis_size("z")
    own, width = normed_own.shape
    group, ff = own * count, mlp_piece.shape[1] // 2
    half = group // 2
    block = width // (2 * lax.axis_size("x"))

    def body(x_ref, w_hbm, d_hbm, c_hbm, sum_ref, down_ref, grad_hbm,
             w_ref, d_ref, c_ref, normed, hidden_grad, hidden, grads, partial, stage, received,
             load_sem, store_sem, pair_send, pair_arrive, gather_send, gather_arrive, local_sem, up, down, send, arrive):
        me, core = lax.axis_index("z"), lax.axis_index("c")
        loads = [
            pltpu.make_async_copy(source, target, load_sem.at[i])
            for i, (source, target) in enumerate(
                [(c_hbm, c_ref), (d_hbm.at[:, pl.ds(DV, ff)], d_ref), (w_hbm, w_ref)]
            )
        ]
        for load in loads:
            load.start()
        gather = Gather("z", count, x_ref, normed, gather_send, gather_arrive, local_sem)
        scatter = Scatter("z", count, PIECES, partial, sum_ref, up, down, send, arrive)
        greet(line_peers("z", count) + [(True, {"c": 1 - core})])
        gather.start()
        loads[0].wait()
        loads[1].wait()

        def tile_of(index, size):
            return pl.ds(pl.multiple_of(index * size, size), size)

        def spans(total):
            return [pl.ds(at, min(TILE, total - at)) for at in range(0, total, TILE)]

        for at in spans(ff):
            hidden_grad[:, at] = dot_plain(c_ref[...], d_ref[:, at])
        loads[2].wait()
        lower = me < count // 2
        nearer = me // (count // 2)

        def forward(rows):
            for at in spans(ff):
                up_at = pl.ds(ff + at.start, at.size)
                gate = dot_plain(normed[rows], w_ref[:, at])
                upper = dot_plain(normed[rows], w_ref[:, up_at])
                grad = hidden_grad[rows, at]
                sig = jax.nn.sigmoid(gate)
                silu = gate * sig
                hidden[rows, at] = (silu * upper).astype(BF)
                grad_gate = grad * upper * sig * (1.0 + gate * (1.0 - sig))
                grads[rows, at] = grad_gate.astype(BF)
                grads[rows, up_at] = (grad * silu).astype(BF)

        def backward(rows):
            for at in spans(width):
                partial[rows, at] = dot_rows(grads[rows], w_ref[at]).astype(BF)

        kept = width // 2 // TILE
        rows_kept = functools.partial(rows_of_core, block)

        def store(number):
            return pltpu.make_async_copy(
                stage.at[number % 2], grad_hbm.at[pl.ds(number * TILE, TILE)],
                store_sem.at[number % 2],
            )

        def pass_over(number):
            return remote(
                stage.at[number % 2], received.at[number], pair_send.at[number % 2],
                pair_arrive.at[number], "c", 1 - core,
            )

        def weight_rows(i):
            ours, number = i >= kept, i % kept
            if i >= 2:
                if i - 2 >= kept:
                    store(i - 2 - kept).wait()
                else:
                    pass_over(i - 2).wait_send()
            at = rows_kept(number, core if ours else 1 - core)
            slot = i % 2
            top = dot_cols(normed[:, at], grads[...])
            low = dot_cols(c_ref[:, at], hidden[...])
            if ours:
                pass_over(number).wait_recv()
                top = top + received[number, :, : 2 * ff].astype(F32)
                low = low + received[number, :, 2 * ff :].astype(F32)
            stage[slot, :, : 2 * ff] = top.astype(BF)
            stage[slot, :, 2 * ff :] = low.astype(BF)
            if ours:
                store(number).start()
            else:
                pass_over(number).start()
            at = pl.ds(i * TILE, TILE)
            down_ref[:, at] = dot_rows(hidden[...], d_ref[at]).astype(BF)

        def away(near):
            block = jnp.where(lower, count // 2, count // 2 - 1)
            end = jnp.where(lower, count - 1, 0)
            return tile_of(block if near else end, own)

        gather.run(1)
        gather.mine.wait()
        forward(tile_of(nearer, half))
        gather.run(2)
        forward(away(True))
        gather.run(3)
        forward(away(False))
        backward(away(False))
        scatter.start([0])
        backward(away(True))
        scatter.start([1])
        backward(tile_of(nearer, half))
        scatter.start([2])
        units = list(range(width // TILE))
        stages = [(step, far) for step in range(count - 1) for far in (False, True)]
        spare = len(units) - len(stages)
        for i in units[: max(spare, 0)]:
            weight_rows(i)
        rest = units[max(spare, 0) :]
        for step, far in stages:
            scatter.run(step, far)
            if rest:
                weight_rows(rest.pop(0))
        scatter.finish()
        gather.finish_sends()
        for number in range(kept - 2, kept):
            store(number).wait()

    in_vmem, anywhere = pl.BlockSpec(memory_space=pltpu.VMEM), pl.BlockSpec(memory_space=pl.ANY)
    return pl.pallas_call(
        body,
        in_specs=[in_vmem, anywhere, anywhere, anywhere],
        out_specs=[in_vmem, in_vmem, anywhere],
        out_shape=[
            jax.ShapeDtypeStruct((own, width), F32),
            jax.ShapeDtypeStruct((group, width), BF),
            jax.ShapeDtypeStruct((width // 2, 3 * ff), BF),
        ],
        scratch_shapes=[
            pltpu.VMEM((width, 2 * ff), BF),
            pltpu.VMEM((width, ff), BF),
            pltpu.VMEM((group, width), BF),
            pltpu.VMEM((group, width), BF),
            pltpu.VMEM((group, ff), F32),
            pltpu.VMEM((group, ff), BF),
            pltpu.VMEM((group, 2 * ff), BF),
            pltpu.VMEM((group, width), BF),
            pltpu.VMEM((2, TILE, 3 * ff), BF),
            pltpu.VMEM((width // 2 // TILE, TILE, 3 * ff), BF),
            pltpu.SemaphoreType.DMA((3,)),
            pltpu.SemaphoreType.DMA((2,)),
            pltpu.SemaphoreType.DMA((2,)),
            pltpu.SemaphoreType.DMA((width // 2 // TILE,)),
        ]
        + Gather.scratch(count)
        + Scatter.scratch(count, own, width, PIECES),
        compiler_params=pltpu.CompilerParams(
            collective_id=number, has_side_effects=True, vmem_limit_bytes=60 * 1024 * 1024
        ),
        cost_estimate=pl.CostEstimate(
            flops=WAIT_FLOPS, bytes_accessed=width * ff * 12, transcendentals=0
        ),
        name="feed_forward",
    )(normed_own, mlp_piece, out_down, cotangent)


def rows_of_core(block, number, by):
    per = block // TILE
    start = (number // per * 2 + by) * block + number % per * TILE
    return pl.ds(pl.multiple_of(start, TILE), TILE)


def attention_end(
    grad_heads, normed, small, weights, side, extras, post, sizes, number
):
    X, C, Z, Y = sizes
    group, total = grad_heads.shape
    width = normed.shape[1]
    own = group // Z
    near, skip = 2 * DK + DV, 2 * DK + 2 * DV
    wide = near + SMALL
    rows = width // (X * C * Y * Z)
    piece = Z * rows
    block = width // (C * X)
    kept = width // 2 // TILE
    others = X * Y - 1

    def body(*refs):
        gh_ref, normed_ref, small_ref = refs[:3]
        extra_refs = refs[3 : 3 + len(extras)]
        w_hbm, side_ref, out_ref, near_out, side_out = refs[3 + len(extras) : 8 + len(extras)]
        (w_ref, partial, given, received, sums, parts, final, load_sem, pair_send, pair_arrive,
         far_send, far_arrive) = refs[8 + len(extras) : 20 + len(extras)]
        sems = refs[20 + len(extras) :]
        x, core, me, y = (lax.axis_index(name) for name in OWN)
        scatter = Scatter("z", Z, PIECES, partial, out_ref, *sems[:4])
        near_swap = Swap("z", Z, final, near_out, *sems[4:7])
        side_swap = Swap("z", Z, side_ref, side_out, *sems[7:10])
        load = pltpu.make_async_copy(w_hbm, w_ref, load_sem)
        load.start()

        def across(offset, sign):
            down, right = offset // Y, offset % Y
            if sign < 0:
                down, right = X - down, Y - right
            return lax.rem(x + down, X), lax.rem(y + right, Y)

        peers = all_peers("z", Z) + [(True, {"c": 1 - core})]
        for offset in range(1, others + 1):
            to_x, to_y = across(offset, 1)
            peers.append((True, {"x": to_x, "y": to_y}))
        greet(peers)

        def backward(at_rows):
            for at in range(0, width, TILE):
                columns = pl.ds(at, TILE)
                partial[at_rows, columns] = dot_rows(gh_ref[at_rows], w_ref[columns]).astype(BF)

        def rows_at(index, size):
            return pl.ds(pl.multiple_of(index * size, size), size)

        lower = me < Z // 2
        load.wait()
        backward(rows_at(jnp.where(lower, Z - 1, 0), own))
        scatter.start([0])
        backward(rows_at(jnp.where(lower, Z // 2, Z // 2 - 1), own))
        scatter.start([1])
        backward(rows_at(me // (Z // 2), group // 2))
        scatter.start([2])

        def pass_over(i):
            return remote(
                given.at[i], received.at[i], pair_send.at[i], pair_arrive.at[i], "c", 1 - core
            )

        def products(i, by):
            at = rows_of_core(block, i, by)
            top = dot_cols(normed_ref[:, at], gh_ref[:, :near])
            low = dot_cols(normed_ref[:, at], gh_ref[:, skip:]) + small_ref[at]
            return top, low

        for i in range(kept):
            top, low = products(i, 1 - core)
            given[i, :, :near] = top.astype(BF)
            given[i, :, near:] = low.astype(BF)
            pass_over(i).start()
        for i in range(kept):
            top, low = products(i, core)
            pass_over(i).wait_recv()
            at = pl.ds(i * TILE, TILE)
            sums[at, :near] = (top + received[i, :, :near].astype(F32)).astype(BF)
            sums[at, near:] = (low + received[i, :, near:].astype(F32)).astype(BF)

        def far(offset, by=1):
            to_x, to_y = across(offset, by)
            return pltpu.make_async_remote_copy(
                src_ref=sums.at[rows_at(to_x * Y + to_y, piece)], dst_ref=parts.at[offset - 1],
                send_sem=far_send.at[offset - 1], recv_sem=far_arrive.at[offset - 1],
                device_id={"x": to_x, "y": to_y}, device_id_type=pl.DeviceIdType.MESH,
            )

        for offset in range(1, others + 1):
            far(offset).start()
        for step in range(Z - 2):
            scatter.run(step, False)
            scatter.run(step, True)
        side_swap.start()
        own_sum = sums[rows_at(x * Y + y, piece)].astype(F32)
        for offset in range(1, others + 1):
            far(offset).wait_recv()
            own_sum = own_sum + parts[offset - 1].astype(F32)
        for index in range(Z):
            final[index] = own_sum[index * rows : (index + 1) * rows].astype(BF)
        near_swap.start()
        scatter.run(Z - 2, False)
        scatter.run(Z - 2, True)
        scatter.finish()
        out_ref[...] = post(out_ref[...], *[r[...] for r in extra_refs])
        side_swap.finish()
        near_swap.finish()
        for offset in range(1, others + 1):
            far(offset).wait_send()
        for i in range(kept):
            pass_over(i).wait_send()

    in_vmem, anywhere = pl.BlockSpec(memory_space=pltpu.VMEM), pl.BlockSpec(memory_space=pl.ANY)
    return pl.pallas_call(
        body,
        in_specs=[in_vmem] * (3 + len(extras)) + [anywhere] * 2,
        out_specs=[in_vmem, anywhere, anywhere],
        out_shape=[
            jax.ShapeDtypeStruct((own, width), F32),
            jax.ShapeDtypeStruct((Z, rows, wide), BF),
            jax.ShapeDtypeStruct(side.shape, BF),
        ],
        scratch_shapes=[
            pltpu.VMEM((width, total), BF),
            pltpu.VMEM((group, width), BF),
            pltpu.VMEM((kept, TILE, wide), BF),
            pltpu.VMEM((kept, TILE, wide), BF),
            pltpu.VMEM((width // 2, wide), BF),
            pltpu.VMEM((max(others, 1), piece, wide), BF),
            pltpu.VMEM((Z, rows, wide), BF),
            pltpu.SemaphoreType.DMA,
            pltpu.SemaphoreType.DMA((kept,)),
            pltpu.SemaphoreType.DMA((kept,)),
            pltpu.SemaphoreType.DMA((max(others, 1),)),
            pltpu.SemaphoreType.DMA((max(others, 1),)),
        ]
        + Scatter.scratch(Z, own, width, PIECES)
        + Swap.scratch(Z)
        + Swap.scratch(Z),
        compiler_params=pltpu.CompilerParams(
            collective_id=number, has_side_effects=True, vmem_limit_bytes=56 * 1024 * 1024
        ),
        cost_estimate=pl.CostEstimate(
            flops=WAIT_FLOPS, bytes_accessed=width * total * 6, transcendentals=0
        ),
        name="attention_end",
    )(grad_heads, normed, small, *extras, weights, side)


def join(values, parts, weights=()):
    Z, rows = values[0].shape[:2]

    def body(*refs):
        ins, refs = refs[: len(values)], refs[len(values) :]
        w_refs, outs = refs[: len(weights)], refs[len(weights) :]
        moment = jnp.zeros((rows, 1), F32)
        for number, (out_ref, (index, start, size)) in enumerate(zip(outs, parts)):
            held = ins[index][0, :, start : start + size].astype(F32)
            out_ref[...] = held
            if number < len(weights):
                product = held * w_refs[number][...].astype(F32)
                moment = moment + jnp.sum(product, axis=1, keepdims=True)
        if weights:
            before = jnp.where(pl.program_id(0) == 0, 0.0, outs[-1][...])
            outs[-1][...] = before + moment

    return pl.pallas_call(
        body,
        grid=(Z,),
        in_specs=[pl.BlockSpec((1,) + v.shape[1:], lambda i: (i, 0, 0)) for v in values]
        + [pl.BlockSpec((rows, w.shape[1] // Z), lambda i: (0, i)) for w in weights],
        out_specs=[pl.BlockSpec((rows, part[2]), lambda i: (0, i)) for part in parts]
        + [pl.BlockSpec((rows, LANES), lambda i: (0, 0))] * (len(weights) > 0),
        out_shape=[jax.ShapeDtypeStruct((rows, Z * part[2]), F32) for part in parts]
        + [jax.ShapeDtypeStruct((rows, LANES), F32)] * (len(weights) > 0),
        compiler_params=pltpu.CompilerParams(dimension_semantics=("arbitrary",)),
        name="join",
    )(*values, *weights)


def local(
    tokens, doc_lengths, cotangent, attn_gain, query_weight, key_weight, value_weight, gate_weight,
    rank_in, rank_out, decay_bias, head_gain, out_weight, mlp_gain, mlp_gate_weight,
    mlp_up_weight, down_weight,
):
    own, width = tokens.shape
    rows = query_weight.shape[0]
    X, C, Z, Y = (lax.axis_size(name) for name in OWN)
    z = lax.axis_index("z")
    group = own * Z
    total = group * Y
    ff = down_weight.shape[1] // Z
    dvp = DV // Y

    def blocked(value):
        lead = value.shape[:-1]
        cut = value.reshape(lead + (X, C, Z, Y, rows))
        return jnp.swapaxes(cut, -3, -2).reshape(lead + (width,))

    def straight(value):
        found = []
        for start in range(0, width, Z * Y * rows):
            for at_z in range(Z):
                for at_y in range(Y):
                    first_lane = start + (at_y * Z + at_z) * rows
                    found.append(value[:, first_lane : first_lane + rows])
        return jnp.concatenate(found, axis=1)

    def pad_rows(value):
        flat = value.reshape(value.shape[0], -1)
        return jnp.pad(flat, ((0, rows - flat.shape[0]), (0, 0)))

    numbers = iter(range(32))

    def deal(value, forth):
        return move(next(numbers), deals=[(value, "y", forth)])[0]

    def after(value, *others):
        return lax.optimization_barrier((value,) + others)[0]

    def scatter_rest(value, axes=REST):
        sums = lax.psum_scatter(value, axes, scatter_dimension=0, tiled=True)
        return sums.reshape(Z, rows, -1)

    def gather_rest(value, axes=REST):
        return lax.all_gather(value.reshape(Z * rows, -1), axes, axis=0, tiled=True)

    small = jnp.concatenate(
        [
            rank_in, pad_rows(attn_gain), pad_rows(mlp_gain), pad_rows(rank_out),
            pad_rows(decay_bias), pad_rows(head_gain),
        ],
        axis=1,
    )
    small = jnp.pad(small, ((0, 0), (0, SMALL - small.shape[1])))
    own_tokens = blocked(tokens)
    input_weights, group_tokens, out_weights = spread_and_gather(
        [query_weight, key_weight, value_weight, gate_weight, small],
        own_tokens, [out_weight, down_weight], (X, C, Z, Y), next(numbers),
    )
    input_weights = input_weights.reshape(width, -1)

    projected = 2 * DK + 2 * DV
    near = 2 * DK + DV
    small_all = input_weights[:, projected:].astype(F32)

    def device_rows(value, count):
        cut = value.reshape(X, C, Y, Z, rows, -1)[:, :, :, :, : rows // count]
        return jnp.swapaxes(cut, 2, 3).reshape(width // count, -1)

    attn_gain_all = small_all[:, R]
    mlp_gain_all = small_all[:, R + 1]
    rank_out_all = device_rows(small_all[:, R + 2 : 2 * R + 2], width // (H * DK))
    bias_all = device_rows(small_all[:, 2 * R + 2 : 2 * R + 3], width // (H * DK))
    head_gain_all = device_rows(small_all[:, 2 * R + 3 : 2 * R + 4], width // DV)[:, 0]
    rank_out_z = lax.dynamic_slice_in_dim(rank_out_all, z * DK, DK).astype(BF)
    bias_z = lax.dynamic_slice_in_dim(bias_all, z * DK, DK)[:, 0]

    def to_device_rows(value, count):
        cut = value.reshape(X, C, Z, Y, rows // count, -1)
        cut = jnp.swapaxes(cut, 2, 3)
        cut = jnp.pad(cut, ((0, 0),) * 4 + ((0, rows - rows // count), (0, 0)))
        return cut.reshape(width, -1)

    def at_head(value):
        return lax.dynamic_update_slice_in_dim(
            jnp.zeros((H * DK, value.shape[1]), F32), value, z * DK, 0
        )

    rows_in = group_tokens.astype(F32)
    scale_in = lax.rsqrt(jnp.mean(rows_in * rows_in, axis=1, keepdims=True) + norm_eps)
    normed_in = (rows_in * scale_in * attn_gain_all).astype(BF)
    heads = dot_plain(normed_in, input_weights)
    out_gate = heads[:, 2 * DK + DV : projected]
    low = heads.astype(BF)
    rank_beside_one = jnp.concatenate(
        [
            jnp.zeros((group, RANK_AT), BF), low[:, projected : projected + R],
            jnp.ones((group, 1), BF), jnp.zeros((group, SMALL - RANK_AT - R - 1), BF),
        ],
        axis=1,
    )
    shared = jnp.concatenate([low[:, : 2 * DK], low[:, projected:]], axis=1)
    values = jnp.swapaxes(low[:, 2 * DK : 2 * DK + DV].reshape(group, Y, dvp), 0, 1)
    sent = jnp.concatenate([jnp.broadcast_to(shared[None], (Y,) + shared.shape), values], axis=2)
    mlp_weights, sequence = move(
        next(numbers), cuts=[([mlp_gate_weight, mlp_up_weight], "z")],
        deals=[(sent.reshape(Y, Z, own, -1), "y", True)],
    )
    out_down = gather_rest(out_weights)
    out_piece = out_down[:, :DV]
    mlp_piece = gather_rest(mlp_weights)
    sequence = sequence.reshape(total, -1)
    queries = sequence[:, :DK]
    keys = sequence[:, DK : 2 * DK]
    rank_low = sequence[:, 2 * DK : 2 * DK + R]
    value_part = sequence[:, 2 * DK + SMALL :]
    decay_logit = dot_rows(rank_low, rank_out_z) + bias_z
    log_decay = jax.nn.log_sigmoid(decay_logit) / decay_norm

    doc_ends = jnp.cumsum(doc_lengths[0])
    positions = lax.iota(jnp.int32, total)
    segments = jnp.sum((doc_ends[None, :] <= positions[:, None]).astype(jnp.int32), axis=1)
    cut = segments.reshape(-1, CHUNK)
    last = cut[:, CHUNK - 1 :]
    before = jnp.concatenate([jnp.full((1, 1), -1, jnp.int32), last[:-1]], axis=0)
    aux = jnp.stack(
        [cut == before, cut == last, cut, jnp.broadcast_to(last == before, cut.shape)], axis=-1
    )
    aux = aux.reshape(total, 4).astype(F32)
    seg_rows = cut.astype(F32)[:, None, :]

    mixed_part, enter, scores = mix_forward(queries, keys, value_part, log_decay, aux, seg_rows)
    mixed_part = deal(mixed_part.reshape(Z, Y, own, dvp), False).reshape(Y, group, dvp)
    mixed = jnp.swapaxes(mixed_part, 0, 1).reshape(group, DV).astype(F32)

    head_scale = lax.rsqrt(jnp.mean(mixed * mixed, axis=1, keepdims=True) + head_eps)
    head_hat = mixed * head_scale
    head_out = head_hat * head_gain_all
    sig_out = jax.nn.sigmoid(out_gate)
    silu_out = out_gate * sig_out
    gated = (head_out * silu_out).astype(BF)
    own_cotangent = blocked(cotangent)
    residual, group_cotangent = move(
        next(numbers), scatter=(dot_rows(gated, out_piece).astype(BF), "z"),
        gathers=[(own_cotangent, "z")], extras=[own_tokens],
        post=lambda total_sum, x: total_sum + x.astype(F32),
    )
    scale_mid = lax.rsqrt(jnp.mean(residual * residual, axis=1, keepdims=True) + norm_eps)
    hat_mid = residual * scale_mid
    normed_mlp = (hat_mid * mlp_gain_all).astype(BF)
    grad_normed_mlp, out_partial, mlp_partial = feed_forward(
        normed_mlp, mlp_piece, out_down, group_cotangent, next(numbers)
    )
    mlp_sums = scatter_rest(mlp_partial, ("x", "y"))

    scaled = grad_normed_mlp * mlp_gain_all
    grad_residual = own_cotangent.astype(F32) + scale_mid * (
        scaled - hat_mid * jnp.mean(scaled * hat_mid, axis=1, keepdims=True)
    )
    branch_own = grad_residual.astype(BF)
    layer_out, grad_branch = move(
        next(numbers), scatter=(out_partial, "z"), gathers=[(branch_own, "z")],
        extras=[residual], post=lambda total_sum, rest: straight(total_sum + rest),
    )
    grad_gated = dot_plain(grad_branch, out_piece)
    grad_head = grad_gated * silu_out
    head_gain_part = jnp.sum(grad_head * head_hat, axis=0)
    head_small = jnp.pad(
        to_device_rows(head_gain_part[:, None], width // DV), ((0, 0), (HEAD_AT, SMALL - HEAD_AT - 1))
    )
    from_head = grad_head * head_gain_all
    grad_mixed = head_scale * (
        from_head - head_hat * jnp.mean(from_head * head_hat, axis=1, keepdims=True)
    )
    grad_out_gate = (grad_gated * head_out * sig_out * (1.0 + out_gate * (1.0 - sig_out))).astype(BF)
    grad_cut = jnp.swapaxes(grad_mixed.astype(BF).reshape(group, Y, dvp), 0, 1)
    grad_part = deal(grad_cut.reshape(Y, Z, own, dvp), True).reshape(total, dvp)
    dq, dk, dv, dld = mix_backward(
        queries, keys, value_part, log_decay, aux, seg_rows, enter, scores, grad_part
    )
    dlogit = (dld * jax.nn.sigmoid(-decay_logit) / decay_norm).astype(BF)
    back = jnp.concatenate([dq, dk, dlogit, dv], axis=1).reshape(Z, Y, own, -1)
    side_partial = jnp.concatenate(
        [dot_cols(normed_in, grad_out_gate), dot_cols(grad_branch, gated)], axis=1
    ).astype(BF)
    back, side_partial = lax.optimization_barrier((back, side_partial))
    side_sums = scatter_rest(after(side_partial, mlp_sums))
    mlp_rows, back = move(
        next(numbers), swaps=[(mlp_sums, "z")], deals=[(back, "y", False)]
    )
    back = back.reshape(Y, group, -1)
    summed = jnp.sum(back[:, :, : 3 * DK].astype(F32), axis=0).astype(BF)
    grad_value = jnp.swapaxes(back[:, :, 3 * DK :], 0, 1).reshape(group, DV)
    grad_logit = summed[:, 2 * DK :]
    rank_out_part = dot_cols(grad_logit, rank_beside_one)
    grad_rank = dot_plain(grad_logit, rank_out_z).astype(BF)
    grad_heads = jnp.concatenate(
        [
            summed[:, : 2 * DK], grad_value, grad_out_gate,
            jnp.pad(grad_rank, ((0, 0), (0, SMALL - R))),
        ],
        axis=1,
    )
    small_part = to_device_rows(at_head(rank_out_part), width // (H * DK)) + head_small

    def finish_tokens(back_sum, x, grad_res, gain):
        held = x.astype(F32)
        scale = lax.rsqrt(jnp.mean(held * held, axis=1, keepdims=True) + norm_eps)
        hat = held * scale
        scaled = back_sum * gain
        mean = jnp.mean(scaled * hat, axis=1, keepdims=True)
        return straight(grad_res + scale * (scaled - hat * mean))

    tokens_grad, near_rows, side_rows = attention_end(
        grad_heads, normed_in, small_part, input_weights, side_sums,
        [own_tokens, grad_residual, attn_gain_all[None]], finish_tokens, (X, C, Z, Y),
        next(numbers),
    )
    *mlp_grads, mlp_moments = join(
        [mlp_rows], [(0, 0, ff), (0, ff, ff), (0, 2 * ff, ff)], [mlp_gate_weight, mlp_up_weight]
    )
    query_grad, key_grad, value_grad, gate_grad, out_grad, moments = join(
        [near_rows, side_rows],
        [
            (0, 0, DK), (0, DK, DK), (0, 2 * DK, DV), (1, 0, DV), (1, DV, DV),
        ],
        [query_weight, key_weight, value_weight, gate_weight],
    )
    small_rows = jnp.sum(near_rows[:, :, near : near + SMALL].astype(F32), axis=0)
    rank_in_grad = small_rows[:, :R]
    moment = moments[:, 0] + jnp.sum(rank_in_grad * rank_in.astype(F32), axis=1)
    return (
        layer_out,
        tokens_grad,
        moment / attn_gain.astype(F32),
        query_grad,
        key_grad,
        value_grad,
        gate_grad,
        rank_in_grad,
        small_rows[: rows * H * DK // width, RANK_AT : RANK_AT + R],
        small_rows[: rows * H * DK // width, RANK_AT + R],
        small_rows[: rows * DV // width, HEAD_AT],
        out_grad,
        mlp_moments[:, 0] / mlp_gain.astype(F32),
        *mlp_grads,
    )


def solution(mesh):
    groups, places = mesh.shape["grp"], mesh.shape["seq"]
    wide = Mesh(mesh.devices.reshape(groups // 2, 2, H, places // H), OWN)
    split = P(OWN, None)
    line = P(OWN)
    by_sequence = P(("x", "c"), None)
    placed = (
        split, by_sequence, split, line, split, split, split, split, split, split,
        line, line, split, line, split, split, split,
    )
    return jax.shard_map(
        local,
        mesh=wide,
        in_specs=placed,
        out_specs=(
            split, split, line, split, split, split, split, split, split, line, line, split,
            line, split, split, split,
        ),
        check_vma=False,
    )
```

```python
import functools

import jax
import jax.numpy as jnp
import numpy as np
from jax import lax
from jax.experimental import pallas as pl
from jax.experimental.pallas import tpu as pltpu
from jax.sharding import Mesh
from jax.sharding import PartitionSpec as P

H = 4
DK = 256
DV = 512
R = 16
CHUNK = 128
LEVELS = 7
SMALL = 128
RANK_AT = 32
HEAD_AT = 64
WAIT_FLOPS = 100_000_000
LANES = 128
TILE = 256
PIECES = 2
norm_eps = 1e-06
head_eps = 0.25
decay_norm = 16.0
BF = jnp.bfloat16
F32 = jnp.float32
REST = ("x", "c", "y")
OWN = ("x", "c", "z", "y")


def dot_plain(left, right):
    return jnp.dot(left, right, preferred_element_type=F32)


def dot_rows(left, right):
    return lax.dot_general(left, right, (((1,), (1,)), ((), ())), preferred_element_type=F32)


def dot_cols(left, right):
    return lax.dot_general(left, right, (((0,), (0,)), ((), ())), preferred_element_type=F32)


def split_two(value):
    high = value.astype(BF)
    return jnp.concatenate([high, (value - high.astype(F32)).astype(BF)], axis=1)


def sum_two(value):
    half = value.shape[1] // 2
    return value[:, :half] + value[:, half:]


def chunk_tables():
    t = np.arange(CHUNK)[:, None]
    j = np.arange(CHUNK)[None, :]
    parts = []
    level = np.full((CHUNK, CHUNK), -1, np.int32)
    for number in range(LEVELS):
        half = CHUNK >> (number + 1)
        middle = t // (2 * half) * (2 * half) + half - 1
        upper = t % (2 * half) >= half
        parts.append(np.where(upper, (j > middle) & (j <= t), (j > t) & (j <= middle)))
        pair = (t // (2 * half) == j // (2 * half)) & upper & (j % (2 * half) < half)
        level[pair] = number
    level[np.arange(CHUNK), np.arange(CHUNK)] = LEVELS
    parts.append(j <= t)
    parts.append(j > t)
    return np.concatenate(parts, axis=0).astype(np.float32), level


def upper_rows(number):
    half = CHUNK >> (number + 1)
    rows = lax.broadcasted_iota(jnp.int32, (CHUNK, 1), 0)
    return lax.rem(rows, 2 * half) >= half


def factors(ld_ref, sums_ref):
    exponents = sum_two(dot_plain(sums_ref[...], split_two(ld_ref[...])))
    return jnp.exp(exponents)


def rows_of(value, number):
    return value[number * CHUNK : (number + 1) * CHUNK]


def mix_forward_body(
    q_ref, k_ref, v_ref, ld_ref, aux_ref, seg_ref, sums_ref, level_ref,
    out_ref, enter_ref, score_ref, state,
):
    @pl.when(pl.program_id(0) == 0)
    def _():
        state[...] = jnp.zeros_like(state)

    factor = factors(ld_ref, sums_ref)
    query = q_ref[...].astype(F32) * DK ** (-0.5)
    key = k_ref[...].astype(F32)
    level = level_ref[...]
    aux = aux_ref[...]
    scores = jnp.where(level == LEVELS, dot_rows(query.astype(BF), k_ref[...]), 0.0)
    for number in range(LEVELS):
        part = rows_of(factor, number)
        pairs = dot_rows((query * part).astype(BF), (key * part).astype(BF))
        scores = jnp.where(level == number, pairs, scores)
    scores = jnp.where(aux[:, 2:3] == seg_ref[0], scores, 0.0).astype(BF)
    score_ref[0] = scores
    cumulative = rows_of(factor, LEVELS)
    enter = state[...].astype(BF)
    enter_ref[0] = enter
    lifted = (query * cumulative * aux[:, 0:1]).astype(BF)
    ending = (key * rows_of(factor, LEVELS + 1) * aux[:, 1:2]).astype(BF)
    out = dot_plain(scores, v_ref[...]) + dot_rows(lifted, enter)
    out_ref[...] = out.astype(out_ref.dtype)
    through = cumulative[CHUNK - 1 :] * aux[0:1, 3:4]
    state[...] = state[...] * through + dot_cols(v_ref[...], ending)


def mix_backward_body(
    q_ref, k_ref, v_ref, ld_ref, aux_ref, seg_ref, sums_ref, sums_t_ref, level_ref, level_t_ref,
    enter_ref, score_ref, do_ref,
    dq_ref, dk_ref, dv_ref, dld_ref, state,
):
    @pl.when(pl.program_id(0) == 0)
    def _():
        state[...] = jnp.zeros_like(state)

    factor = factors(ld_ref, sums_ref)
    scale = DK ** (-0.5)
    query = q_ref[...].astype(F32) * scale
    key = k_ref[...].astype(F32)
    value = v_ref[...]
    grad = do_ref[...]
    level = level_ref[...]
    level_t = level_t_ref[...]
    aux = aux_ref[...]
    same = aux[:, 2:3] == seg_ref[0]
    weight = jnp.where(same, dot_rows(grad, value), 0.0)
    weight_t = jnp.where(same, dot_rows(value, grad), 0.0)
    diagonal = jnp.sum(jnp.where(level == LEVELS, weight, 0.0), axis=1, keepdims=True)
    dq = diagonal * key
    dk = diagonal * query
    moved = []
    for number in range(LEVELS):
        part = rows_of(factor, number)
        left = jnp.concatenate(
            [
                jnp.where(level == number, weight, 0.0).astype(BF),
                jnp.where(level_t == number, weight_t, 0.0).astype(BF),
            ],
            axis=1,
        )
        right = jnp.concatenate([(key * part).astype(BF), (query * part).astype(BF)], axis=0)
        both = dot_plain(left, right) * part
        upper = upper_rows(number)
        dq = dq + jnp.where(upper, both, 0.0)
        dk = dk + jnp.where(upper, 0.0, both)
        moved.append(both * jnp.where(upper, query, key))
    cumulative = rows_of(factor, LEVELS)
    enter = enter_ref[0]
    after = state[...]
    after_low = after.astype(BF)
    lift = cumulative * aux[:, 0:1]
    finish = rows_of(factor, LEVELS + 1) * aux[:, 1:2]
    lifted = query * lift
    ending = key * finish
    from_enter = dot_plain(grad, enter)
    from_after = dot_plain(value, after_low)
    moved.append(lifted * from_enter)
    moved.append(ending * from_after)
    dq_ref[...] = ((dq + lift * from_enter) * scale).astype(dq_ref.dtype)
    dk_ref[...] = (dk + finish * from_after).astype(dk_ref.dtype)
    dv = dot_cols(score_ref[0], grad) + dot_rows(ending.astype(BF), after_low)
    dv_ref[...] = dv.astype(dv_ref.dtype)
    through = cumulative[CHUNK - 1 :] * aux[0:1, 3:4]
    passing = jnp.sum(after * enter.astype(F32), axis=0, keepdims=True) * through
    spread = sum_two(dot_plain(sums_t_ref[...], split_two(jnp.concatenate(moved, axis=0))))
    dld_ref[...] = spread + passing
    state[...] = after * through + dot_cols(grad, lifted.astype(BF))


def mix_specs(count, width, backward):
    def at(i):
        return count - 1 - i if backward else i

    def tokens(columns):
        return pl.BlockSpec((CHUNK, columns), lambda i: (at(i), 0))

    def chunks(rows, columns):
        return pl.BlockSpec((1, rows, columns), lambda i: (at(i), 0, 0))

    def whole(rows, columns):
        return pl.BlockSpec((rows, columns), lambda i: (0, 0))

    return tokens, chunks, whole


def mix_forward(query, key, value, log_decay, aux, seg_rows):
    total, width = value.shape
    count = total // CHUNK
    sums, level = chunk_tables()
    tokens, chunks, whole = mix_specs(count, width, False)
    return pl.pallas_call(
        mix_forward_body,
        grid=(count,),
        in_specs=[
            tokens(DK), tokens(DK), tokens(width), tokens(DK), tokens(aux.shape[1]),
            chunks(1, CHUNK), whole(*sums.shape), whole(CHUNK, CHUNK),
        ],
        out_specs=[tokens(width), chunks(width, DK), chunks(CHUNK, CHUNK)],
        out_shape=[
            jax.ShapeDtypeStruct((total, width), BF),
            jax.ShapeDtypeStruct((count, width, DK), BF),
            jax.ShapeDtypeStruct((count, CHUNK, CHUNK), BF),
        ],
        scratch_shapes=[pltpu.VMEM((width, DK), F32)],
        compiler_params=pltpu.CompilerParams(
            dimension_semantics=("arbitrary",), vmem_limit_bytes=32 * 1024 * 1024
        ),
        cost_estimate=pl.CostEstimate(
            flops=total * 2 * (8 * CHUNK * DK + 2 * width * DK + CHUNK * width + 18 * CHUNK * DK),
            bytes_accessed=total * 4096, transcendentals=total * 9 * DK,
        ),
        name="mix_forward",
    )(query, key, value, log_decay, aux, seg_rows, jnp.asarray(sums, BF), jnp.asarray(level))


def mix_backward(query, key, value, log_decay, aux, seg_rows, enter, scores, grad):
    total, width = value.shape
    count = total // CHUNK
    sums, level = chunk_tables()
    tokens, chunks, whole = mix_specs(count, width, True)
    return pl.pallas_call(
        mix_backward_body,
        grid=(count,),
        in_specs=[
            tokens(DK), tokens(DK), tokens(width), tokens(DK), tokens(aux.shape[1]),
            chunks(1, CHUNK), whole(*sums.shape), whole(*sums.shape[::-1]),
            whole(CHUNK, CHUNK), whole(CHUNK, CHUNK),
            chunks(width, DK), chunks(CHUNK, CHUNK), tokens(width),
        ],
        out_specs=[tokens(DK), tokens(DK), tokens(width), tokens(DK)],
        out_shape=[
            jax.ShapeDtypeStruct((total, DK), BF),
            jax.ShapeDtypeStruct((total, DK), BF),
            jax.ShapeDtypeStruct((total, width), BF),
            jax.ShapeDtypeStruct((total, DK), F32),
        ],
        scratch_shapes=[pltpu.VMEM((width, DK), F32)],
        compiler_params=pltpu.CompilerParams(
            dimension_semantics=("arbitrary",), vmem_limit_bytes=48 * 1024 * 1024
        ),
        cost_estimate=pl.CostEstimate(
            flops=total * 2 * (14 * CHUNK * DK + 4 * width * DK + CHUNK * width + 36 * CHUNK * DK),
            bytes_accessed=total * 6144, transcendentals=total * 9 * DK,
        ),
        name="mix_backward",
    )(
        query, key, value, log_decay, aux, seg_rows, jnp.asarray(sums, BF),
        jnp.asarray(np.ascontiguousarray(sums.T), BF), jnp.asarray(level),
        jnp.asarray(np.ascontiguousarray(level.T)), enter, scores, grad,
    )


def remote(source, target, send, arrive, axis, place):
    return pltpu.make_async_remote_copy(
        src_ref=source, dst_ref=target, send_sem=send, recv_sem=arrive,
        device_id={axis: place}, device_id_type=pl.DeviceIdType.MESH,
    )


def greet(peers):
    barrier = pltpu.get_barrier_semaphore()
    number = 0
    for present, peer in peers:
        if present is True:
            pl.semaphore_signal(
                barrier, inc=1, device_id=peer, device_id_type=pl.DeviceIdType.MESH
            )
            number = number + 1
        else:

            @pl.when(present)
            def _():
                pl.semaphore_signal(
                    barrier, inc=1, device_id=peer, device_id_type=pl.DeviceIdType.MESH
                )

            number = number + jnp.where(present, 1, 0)
    pl.semaphore_wait(barrier, number)


def line_peers(axis, count):
    me = lax.axis_index(axis)
    return [(me > 0, {axis: me - 1}), (me < count - 1, {axis: me + 1})]


def all_peers(axis, count):
    me = lax.axis_index(axis)
    return [(True, {axis: lax.rem(me + away, count)}) for away in range(1, count)]


class Gather:
    def __init__(self, axis, count, x_ref, out_ref, send, arrive, local_sem):
        self.axis, self.count, self.x_ref, self.out_ref = axis, count, x_ref, out_ref
        self.send, self.arrive = send, arrive
        self.me = lax.axis_index(axis)
        self.mine = pltpu.make_async_copy(x_ref, self.block(self.me), local_sem)

    def block(self, index):
        own = self.x_ref.shape[0]
        return self.out_ref.at[pl.ds(pl.multiple_of(index * own, own), own)]

    def copy(self, direction, step, index, source):
        return remote(
            source, self.block(index), self.send.at[direction, step],
            self.arrive.at[direction, step], self.axis,
            self.me + 1 if direction == 0 else self.me - 1,
        )

    def hop(self, direction, step):
        index = self.me - step if direction == 0 else self.me + step
        return self.copy(direction, step, index, self.x_ref if step == 0 else self.block(index))

    def landed(self, direction, step):
        index = self.me - 1 - step if direction == 0 else self.me + 1 + step
        return self.copy(direction, step, index, self.block(index))

    def holds(self, direction, step):
        return self.me - step >= 0 if direction == 0 else self.me + step <= self.count - 1

    def hands_on(self, direction, step):
        inner = self.me < self.count - 1 if direction == 0 else self.me > 0
        return self.holds(direction, step) & inner

    def start(self):
        self.mine.start()
        self.run(0)

    def run(self, first, last=None):
        for step in range(first, first + 1 if last is None else last):
            for direction in (0, 1):
                if step > 0:

                    @pl.when(self.holds(direction, step))
                    def _():
                        self.landed(direction, step - 1).wait_recv()

                if step < self.count - 1:

                    @pl.when(self.hands_on(direction, step))
                    def _():
                        self.hop(direction, step).start()

    def finish(self):
        self.finish_sends()
        self.mine.wait()

    def finish_sends(self):
        for step in range(self.count - 1):
            for direction in (0, 1):

                @pl.when(self.hands_on(direction, step))
                def _():
                    self.hop(direction, step).wait_send()

    @staticmethod
    def scratch(count):
        return [
            pltpu.SemaphoreType.DMA((2, count - 1)),
            pltpu.SemaphoreType.DMA((2, count - 1)),
            pltpu.SemaphoreType.DMA,
        ]


class Swap:
    def __init__(self, axis, count, x_ref, out_ref, send, arrive, local_sem):
        self.axis, self.count, self.x_ref, self.out_ref = axis, count, x_ref, out_ref
        self.send, self.arrive = send, arrive
        self.me = lax.axis_index(axis)
        self.mine = pltpu.make_async_copy(x_ref.at[self.me], out_ref.at[self.me], local_sem)

    def hop(self, away):
        peer = lax.rem(self.me + away, self.count)
        return remote(
            self.x_ref.at[peer], self.out_ref.at[self.me], self.send.at[away - 1],
            self.arrive.at[away - 1], self.axis, peer,
        )

    def landed(self, away):
        peer = lax.rem(self.me + self.count - away, self.count)
        return remote(
            self.x_ref.at[peer], self.out_ref.at[peer], self.send.at[away - 1],
            self.arrive.at[away - 1], self.axis, peer,
        )

    def start(self):
        self.mine.start()
        for away in range(1, self.count):
            self.hop(away).start()

    def finish(self):
        for away in range(1, self.count):
            self.landed(away).wait_recv()
        for away in range(1, self.count):
            self.hop(away).wait_send()
        self.mine.wait()

    @staticmethod
    def scratch(count):
        return [
            pltpu.SemaphoreType.DMA((count - 1,)),
            pltpu.SemaphoreType.DMA((count - 1,)),
            pltpu.SemaphoreType.DMA,
        ]


class Scatter:
    def __init__(self, axis, count, pieces, x_ref, out_ref, up, down, send, arrive):
        self.axis, self.count, self.pieces = axis, count, pieces
        self.x_ref, self.out_ref, self.held_refs = x_ref, out_ref, (up, down)
        self.send, self.arrive = send, arrive
        self.me = lax.axis_index(axis)
        self.own = out_ref.shape[0]
        self.size = self.own // pieces

    def part(self, index, piece):
        start = pl.multiple_of(index * self.own + piece * self.size, self.size)
        return self.x_ref.at[pl.ds(start, self.size)]

    def held(self, direction, number, piece):
        return self.held_refs[direction].at[number, pl.ds(piece * self.size, self.size)]

    def hop(self, direction, number, piece, source=None):
        held = self.held(direction, number, piece)
        return remote(
            held if source is None else source, held, self.send.at[direction, number, piece],
            self.arrive.at[direction, number, piece], self.axis,
            self.me + 1 if direction == 0 else self.me - 1,
        )

    def target(self, direction, number):
        return self.count - 1 - number if direction == 0 else number

    def start(self, numbers=None):
        for direction in (0, 1):

            @pl.when(self.me == (0 if direction == 0 else self.count - 1))
            def _():
                for number in range(self.count - 1) if numbers is None else numbers:
                    target = self.target(direction, number)
                    for piece in range(self.pieces):
                        self.hop(direction, number, piece, self.part(target, piece)).start()

    def stage(self, direction, number, piece):
        me, target = self.me, self.target(direction, number)
        inner = me > 0 if direction == 0 else me < self.count - 1
        passed = me < target if direction == 0 else me > target
        held = self.held(direction, number, piece)

        @pl.when(inner & (passed | (me == target)))
        def _():
            self.hop(direction, number, piece).wait_recv()

        @pl.when(inner & passed)
        def _():
            mine = self.part(target, piece)[...].astype(F32)
            held[...] = (held[...].astype(F32) + mine).astype(BF)
            self.hop(direction, number, piece).start()

    def run(self, number, far):
        for order in (0, 1):

            @pl.when((self.me >= self.count // 2) == (order == 1))
            def _():
                for piece in range(self.pieces):
                    self.stage(1 - order if far else order, number, piece)

    def finish(self):
        me, count, out_ref = self.me, self.count, self.out_ref
        for piece in range(self.pieces):
            rows = pl.ds(piece * self.size, self.size)
            out_ref[rows] = self.part(me, piece)[...].astype(F32)
            for direction in (0, 1):
                for number in range(count - 1):
                    inner = me > 0 if direction == 0 else me < count - 1

                    @pl.when((me == self.target(direction, number)) & inner)
                    def _():
                        out_ref[rows] += self.held(direction, number, piece)[...].astype(F32)

        for direction in (0, 1):
            for number in range(count - 1):
                target = self.target(direction, number)

                @pl.when(me < target if direction == 0 else me > target)
                def _():
                    for piece in range(self.pieces):
                        self.hop(direction, number, piece).wait_send()

    @staticmethod
    def scratch(count, own, columns, pieces):
        return [
            pltpu.VMEM((count - 1, own, columns), BF),
            pltpu.VMEM((count - 1, own, columns), BF),
            pltpu.SemaphoreType.DMA((2, count - 1, pieces)),
            pltpu.SemaphoreType.DMA((2, count - 1, pieces)),
        ]


class CutSwap:
    def __init__(self, axis, count, refs, out_ref, send, arrive, local_sem):
        self.axis, self.count, self.refs, self.out_ref = axis, count, refs, out_ref
        self.send, self.arrive = send, arrive
        self.me = lax.axis_index(axis)
        self.widths = [ref.shape[1] // count for ref in refs]
        self.mine = [
            pltpu.make_async_copy(self.cut(i, self.me), self.slot(i, self.me), local_sem.at[i])
            for i in range(len(refs))
        ]

    def cut(self, i, index):
        size = self.widths[i]
        return self.refs[i].at[:, pl.ds(pl.multiple_of(index * size, LANES), size)]

    def slot(self, i, index):
        return self.out_ref.at[index, :, pl.ds(sum(self.widths[:i]), self.widths[i])]

    def hop(self, away, i):
        peer = lax.rem(self.me + away, self.count)
        return remote(
            self.cut(i, peer), self.slot(i, self.me), self.send.at[away - 1, i],
            self.arrive.at[away - 1, i], self.axis, peer,
        )

    def landed(self, away, i):
        peer = lax.rem(self.me + self.count - away, self.count)
        return remote(
            self.cut(i, peer), self.slot(i, peer), self.send.at[away - 1, i],
            self.arrive.at[away - 1, i], self.axis, peer,
        )

    def each(self):
        return [(away, i) for away in range(1, self.count) for i in range(len(self.refs))]

    def start(self):
        for away, i in self.each():
            self.hop(away, i).start()
        for copy in self.mine:
            copy.start()

    def finish(self):
        for away, i in self.each():
            self.landed(away, i).wait_recv()
        for away, i in self.each():
            self.hop(away, i).wait_send()
        for copy in self.mine:
            copy.wait()

    @staticmethod
    def scratch(count, parts):
        sems = pltpu.SemaphoreType.DMA((count - 1, parts))
        return [sems, sems, pltpu.SemaphoreType.DMA((parts,))]


class Deal:
    def __init__(self, axis, count, forth, x_ref, out_ref, send, arrive, local_sem):
        self.axis, self.count, self.forth = axis, count, forth
        self.x_ref, self.out_ref, self.send, self.arrive = x_ref, out_ref, send, arrive
        self.me = lax.axis_index(axis)
        self.steps = x_ref.shape[1] if forth else x_ref.shape[0]
        self.mine = [
            pltpu.make_async_copy(self.given(self.me, k), self.got(self.me, k), local_sem.at[k])
            for k in range(self.steps)
        ]

    def given(self, device, k):
        return self.x_ref.at[device, k] if self.forth else self.x_ref.at[k, device]

    def got(self, device, k):
        return self.out_ref.at[k, device] if self.forth else self.out_ref.at[device, k]

    def hop(self, away, k):
        peer = lax.rem(self.me + away, self.count)
        return remote(
            self.given(peer, k), self.got(self.me, k), self.send.at[away - 1, k],
            self.arrive.at[away - 1, k], self.axis, peer,
        )

    def landed(self, away, k):
        peer = lax.rem(self.me + self.count - away, self.count)
        return remote(
            self.given(peer, k), self.got(peer, k), self.send.at[away - 1, k],
            self.arrive.at[away - 1, k], self.axis, peer,
        )

    def each(self):
        return [(away, k) for away in range(1, self.count) for k in range(self.steps)]

    def start(self):
        for away, k in self.each():
            self.hop(away, k).start()
        for copy in self.mine:
            copy.start()

    def finish(self):
        for away, k in self.each():
            self.landed(away, k).wait_recv()
        for away, k in self.each():
            self.hop(away, k).wait_send()
        for copy in self.mine:
            copy.wait()

    @staticmethod
    def scratch(count, steps):
        sems = pltpu.SemaphoreType.DMA((count - 1, steps))
        return [sems, sems, pltpu.SemaphoreType.DMA((steps,))]


class Spread:
    def __init__(self, sizes, cuts, out_ref, far_send, far_arrive, near_send, near_arrive):
        self.X, self.C, self.Z, self.Y = sizes
        self.cuts, self.out_ref = cuts, out_ref
        self.far_send, self.far_arrive = far_send, far_arrive
        self.near_send, self.near_arrive = near_send, near_arrive
        self.x, self.c, self.z, self.y = (lax.axis_index(name) for name in OWN)
        self.others = self.X * self.Y - 1

    def across(self, offset, sign):
        down, right = offset // self.Y, offset % self.Y
        if sign < 0:
            down, right = self.X - down, self.Y - right
        return lax.rem(self.x + down, self.X), lax.rem(self.y + right, self.Y)

    def place(self, offset, c, slot):
        x, y = self.across(offset, -1)
        z = lax.rem(self.z + self.Z - slot, self.Z)
        return self.out_ref.at[((x * self.C + c) * self.Y + y) * self.Z + z]

    def far(self, offset, slot, landed=False):
        x, y = self.across(offset, 1)
        held = self.place(offset if landed else 0, self.c, slot)
        return pltpu.make_async_remote_copy(
            src_ref=held, dst_ref=held, send_sem=self.far_send.at[offset - 1, slot],
            recv_sem=self.far_arrive.at[offset - 1, slot], device_id={"x": x, "y": y},
            device_id_type=pl.DeviceIdType.MESH,
        )

    def near(self, offset, slot, landed=False):
        held = self.place(offset, 1 - self.c if landed else self.c, slot)
        return remote(
            held, held, self.near_send.at[offset, slot],
            self.near_arrive.at[offset, slot], "c", 1 - self.c,
        )

    def peers(self):
        found = all_peers("z", self.Z) + [(True, {"c": 1 - self.c})]
        for offset in range(1, self.others + 1):
            x, y = self.across(offset, 1)
            found.append((True, {"x": x, "y": y}))
        return found

    def hand_on(self, slot):
        for i in range(len(self.cuts.refs)):
            if slot > 0:
                self.cuts.landed(slot, i).wait_recv()
            else:
                self.cuts.mine[i].wait()
        for offset in range(1, self.others + 1):
            self.far(offset, slot).start()
        self.near(0, slot).start()

    def collect(self, slot):
        for offset in range(1, self.others + 1):
            self.far(offset, slot, True).wait_recv()
            self.near(offset, slot).start()

    def finish(self):
        for slot in range(self.Z):
            for offset in range(self.others + 1):
                self.near(offset, slot, True).wait_recv()
        for slot in range(self.Z):
            for offset in range(self.others + 1):
                self.near(offset, slot).wait_send()
                if offset > 0:
                    self.far(offset, slot).wait_send()
        for away, i in self.cuts.each():
            self.cuts.hop(away, i).wait_send()

    @staticmethod
    def scratch(sizes):
        X, C, Z, Y = sizes
        far = pltpu.SemaphoreType.DMA((max(X * Y - 1, 1), Z))
        near = pltpu.SemaphoreType.DMA((X * Y, Z))
        return [far, far, near, near]


class FirstCuts(CutSwap):
    def __init__(self, spread_place, count, refs, out_ref, send, arrive, local_sem):
        self.place = spread_place
        super().__init__("z", count, refs, out_ref, send, arrive, local_sem)

    def cut(self, i, index):
        return self.refs[i] if i == len(self.refs) - 1 else super().cut(i, index)

    def slot(self, i, index):
        widths = [w for w in self.widths[:-1]] + [SMALL]
        return self.out_ref.at[self.place(index), :, pl.ds(sum(widths[:i]), widths[i])]


def spread_and_gather(weights, block, others, sizes, number):
    X, C, Z, Y = sizes
    parts = len(weights)
    rows = weights[0].shape[0]
    total = sum(w.shape[1] // Z for w in weights[:-1]) + weights[-1].shape[1]

    def body(*refs):
        extra = len(others)
        w_refs, x_ref, o_refs = refs[:parts], refs[parts], refs[parts + 1 : parts + 1 + extra]
        spread_ref, out_ref, swapped_ref = refs[parts + 1 + extra : parts + 4 + extra]
        sems = refs[parts + 4 + extra :]
        x, c, _, y = (lax.axis_index(name) for name in OWN)
        first = FirstCuts(
            lambda index: ((x * C + c) * Y + y) * Z + index, Z, w_refs, spread_ref, *sems[:3]
        )
        spread = Spread(sizes, first, spread_ref, *sems[3:7])
        gather = Gather("z", Z, x_ref, out_ref, *sems[7:10])
        swap = CutSwap("z", Z, o_refs, swapped_ref, *sems[10:])
        greet(spread.peers())
        first.start()
        gather.start()
        spread.hand_on(0)
        for slot in range(1, Z):
            spread.hand_on(slot)
        for step in range(1, Z):
            gather.run(step)
            if step == Z - 2:
                swap.start()
            spread.collect(step - 1)
        spread.collect(Z - 1)
        spread.finish()
        gather.finish()
        swap.finish()

    anywhere = pl.BlockSpec(memory_space=pl.ANY)
    return pl.pallas_call(
        body,
        in_specs=[anywhere] * (parts + 1 + len(others)),
        out_specs=[anywhere] * 3,
        out_shape=[
            jax.ShapeDtypeStruct((X * C * Y * Z, rows, total), BF),
            jax.ShapeDtypeStruct((Z * block.shape[0],) + block.shape[1:], block.dtype),
            jax.ShapeDtypeStruct((Z, rows, sum(w.shape[1] for w in others) // Z), BF),
        ],
        scratch_shapes=CutSwap.scratch(Z, parts)
        + Spread.scratch(sizes)
        + Gather.scratch(Z)
        + CutSwap.scratch(Z, len(others)),
        compiler_params=pltpu.CompilerParams(collective_id=number, has_side_effects=True),
        cost_estimate=pl.CostEstimate(
            flops=WAIT_FLOPS, bytes_accessed=rows * total * X * C * Y * Z * 2, transcendentals=0
        ),
        name="spread_and_gather",
    )(*weights, block, *others)


def move(
    number, scatter=None, swaps=(), gathers=(), cuts=(), deals=(), extras=(), post=None
):
    in_vmem, anywhere = pl.BlockSpec(memory_space=pltpu.VMEM), pl.BlockSpec(memory_space=pl.ANY)
    values, in_specs, shapes, out_specs, scratch = [], [], [], [], []
    flags = {}

    def scale(axis):
        return lax.axis_size(axis)

    if scatter is not None:
        partial, axis = scatter
        own = partial.shape[0] // scale(axis)
        values += [partial, *extras]
        in_specs += [in_vmem] * (1 + len(extras))
        shapes.append(jax.ShapeDtypeStruct((own, partial.shape[1]), F32))
        out_specs.append(in_vmem)
        scratch += Scatter.scratch(scale(axis), own, partial.shape[1], PIECES)
        flags = dict(vmem_limit_bytes=40 * 1024 * 1024)
    for value, axis in swaps:
        values.append(value)
        in_specs.append(anywhere)
        shapes.append(jax.ShapeDtypeStruct(value.shape, value.dtype))
        out_specs.append(anywhere)
        scratch += Swap.scratch(scale(axis))
    for block, axis in gathers:
        values.append(block)
        in_specs.append(anywhere)
        shapes.append(
            jax.ShapeDtypeStruct((scale(axis) * block.shape[0], block.shape[1]), block.dtype)
        )
        out_specs.append(anywhere)
        scratch += Gather.scratch(scale(axis))

    for weights, axis in cuts:
        values += weights
        in_specs += [anywhere] * len(weights)
        wide = sum(w.shape[1] for w in weights) // scale(axis)
        shapes.append(
            jax.ShapeDtypeStruct((scale(axis), weights[0].shape[0], wide), weights[0].dtype)
        )
        out_specs.append(anywhere)
        scratch += CutSwap.scratch(scale(axis), len(weights))
    for value, axis, forth in deals:
        first, second = value.shape[:2]
        values.append(value)
        in_specs.append(anywhere)
        shapes.append(jax.ShapeDtypeStruct((second, first) + value.shape[2:], value.dtype))
        out_specs.append(anywhere)
        scratch += Deal.scratch(scale(axis), second if forth else first)

    def body(*refs):
        ins = list(refs[: len(values)])
        outs = list(refs[len(values) : len(values) + len(shapes)])
        sems = list(refs[len(values) + len(shapes) :])
        peers = {}
        adding, extra_refs, swapping, gathering = None, (), [], []
        if scatter is not None:
            axis = scatter[1]
            adding = Scatter(axis, scale(axis), PIECES, ins.pop(0), outs.pop(0), *sems[:4])
            extra_refs, ins, sems = ins[: len(extras)], ins[len(extras) :], sems[4:]
            peers[axis] = line_peers(axis, scale(axis))
        for _, axis in gathers:
            peers[axis] = line_peers(axis, scale(axis))
        for _, axis in swaps:
            peers[axis] = all_peers(axis, scale(axis))
            swapping.append(Swap(axis, scale(axis), ins.pop(0), outs.pop(0), *sems[:3]))
            sems = sems[3:]
        for _, axis in gathers:
            gathering.append(Gather(axis, scale(axis), ins.pop(0), outs.pop(0), *sems[:3]))
            sems = sems[3:]
        for weights, axis in cuts:
            peers[axis] = all_peers(axis, scale(axis))
            taken, ins = ins[: len(weights)], ins[len(weights) :]
            swapping.append(CutSwap(axis, scale(axis), taken, outs.pop(0), *sems[:3]))
            sems = sems[3:]
        for _, axis, forth in deals:
            peers[axis] = all_peers(axis, scale(axis))
            swapping.append(
                Deal(axis, scale(axis), forth, ins.pop(0), outs.pop(0), *sems[:3])
            )
            sems = sems[3:]
        greet([peer for found in peers.values() for peer in found])
        for part in gathering + ([adding] if adding else []) + swapping:
            part.start()
        steps = max([part.count for part in gathering + ([adding] if adding else [])] + [0])
        for part in gathering:
            part.run(1)
        for step in range(1, steps):
            if adding:
                adding.run(step - 1, False)
            for part in gathering:
                if step + 1 < part.count:
                    part.run(step + 1)
            if adding:
                adding.run(step - 1, True)
        if adding:
            adding.finish()
            if post is not None:
                adding.out_ref[...] = post(adding.out_ref[...], *[r[...] for r in extra_refs])
        for part in swapping + gathering:
            part.finish()

    size = sum(v.size for v in values)
    return pl.pallas_call(
        body,
        in_specs=in_specs,
        out_specs=out_specs,
        out_shape=shapes,
        scratch_shapes=scratch,
        compiler_params=pltpu.CompilerParams(
            collective_id=number, has_side_effects=True, **flags
        ),
        cost_estimate=pl.CostEstimate(
            flops=WAIT_FLOPS, bytes_accessed=size * 4, transcendentals=0
        ),
        name="move",
    )(*values)


def feed_forward(normed_own, mlp_piece, out_down, cotangent, number):
    count = lax.axis_size("z")
    own, width = normed_own.shape
    group, ff = own * count, mlp_piece.shape[1] // 2
    half = group // 2
    block = width // (2 * lax.axis_size("x"))

    def body(x_ref, w_hbm, d_hbm, c_hbm, sum_ref, down_ref, grad_hbm,
             w_ref, d_ref, c_ref, normed, hidden_grad, hidden, grads, partial, stage, received,
             load_sem, store_sem, pair_send, pair_arrive, gather_send, gather_arrive, local_sem, up, down, send, arrive):
        me, core = lax.axis_index("z"), lax.axis_index("c")
        loads = [
            pltpu.make_async_copy(source, target, load_sem.at[i])
            for i, (source, target) in enumerate(
                [(c_hbm, c_ref), (d_hbm.at[:, pl.ds(DV, ff)], d_ref), (w_hbm, w_ref)]
            )
        ]
        for load in loads:
            load.start()
        gather = Gather("z", count, x_ref, normed, gather_send, gather_arrive, local_sem)
        scatter = Scatter("z", count, PIECES, partial, sum_ref, up, down, send, arrive)
        greet(line_peers("z", count) + [(True, {"c": 1 - core})])
        gather.start()
        loads[0].wait()
        loads[1].wait()

        def tile_of(index, size):
            return pl.ds(pl.multiple_of(index * size, size), size)

        def spans(total):
            return [pl.ds(at, min(TILE, total - at)) for at in range(0, total, TILE)]

        for at in spans(ff):
            hidden_grad[:, at] = dot_plain(c_ref[...], d_ref[:, at])
        loads[2].wait()
        lower = me < count // 2
        nearer = me // (count // 2)

        def forward(rows):
            for at in spans(ff):
                up_at = pl.ds(ff + at.start, at.size)
                gate = dot_plain(normed[rows], w_ref[:, at])
                upper = dot_plain(normed[rows], w_ref[:, up_at])
                grad = hidden_grad[rows, at]
                sig = jax.nn.sigmoid(gate)
                silu = gate * sig
                hidden[rows, at] = (silu * upper).astype(BF)
                grad_gate = grad * upper * sig * (1.0 + gate * (1.0 - sig))
                grads[rows, at] = grad_gate.astype(BF)
                grads[rows, up_at] = (grad * silu).astype(BF)

        def backward(rows):
            for at in spans(width):
                partial[rows, at] = dot_rows(grads[rows], w_ref[at]).astype(BF)

        kept = width // 2 // TILE
        rows_kept = functools.partial(rows_of_core, block)

        def store(number):
            return pltpu.make_async_copy(
                stage.at[number % 2], grad_hbm.at[pl.ds(number * TILE, TILE)],
                store_sem.at[number % 2],
            )

        def pass_over(number):
            return remote(
                stage.at[number % 2], received.at[number], pair_send.at[number % 2],
                pair_arrive.at[number], "c", 1 - core,
            )

        def weight_rows(i):
            ours, number = i >= kept, i % kept
            if i >= 2:
                if i - 2 >= kept:
                    store(i - 2 - kept).wait()
                else:
                    pass_over(i - 2).wait_send()
            at = rows_kept(number, core if ours else 1 - core)
            slot = i % 2
            top = dot_cols(normed[:, at], grads[...])
            low = dot_cols(c_ref[:, at], hidden[...])
            if ours:
                pass_over(number).wait_recv()
                top = top + received[number, :, : 2 * ff].astype(F32)
                low = low + received[number, :, 2 * ff :].astype(F32)
            stage[slot, :, : 2 * ff] = top.astype(BF)
            stage[slot, :, 2 * ff :] = low.astype(BF)
            if ours:
                store(number).start()
            else:
                pass_over(number).start()
            at = pl.ds(i * TILE, TILE)
            down_ref[:, at] = dot_rows(hidden[...], d_ref[at]).astype(BF)

        def away(near):
            block = jnp.where(lower, count // 2, count // 2 - 1)
            end = jnp.where(lower, count - 1, 0)
            return tile_of(block if near else end, own)

        gather.run(1)
        gather.mine.wait()
        forward(tile_of(nearer, half))
        gather.run(2)
        forward(away(True))
        gather.run(3)
        forward(away(False))
        backward(away(False))
        scatter.start([0])
        backward(away(True))
        scatter.start([1])
        backward(tile_of(nearer, half))
        scatter.start([2])
        units = list(range(width // TILE))
        stages = [(step, far) for step in range(count - 1) for far in (False, True)]
        spare = len(units) - len(stages) + 2
        for i in units[: max(spare, 0)]:
            weight_rows(i)
        rest = units[max(spare, 0) :]
        for step, far in stages:
            scatter.run(step, far)
            if rest:
                weight_rows(rest.pop(0))
        scatter.finish()
        gather.finish_sends()
        for number in range(kept - 2, kept):
            store(number).wait()

    in_vmem, anywhere = pl.BlockSpec(memory_space=pltpu.VMEM), pl.BlockSpec(memory_space=pl.ANY)
    return pl.pallas_call(
        body,
        in_specs=[in_vmem, anywhere, anywhere, anywhere],
        out_specs=[in_vmem, in_vmem, anywhere],
        out_shape=[
            jax.ShapeDtypeStruct((own, width), F32),
            jax.ShapeDtypeStruct((group, width), BF),
            jax.ShapeDtypeStruct((width // 2, 3 * ff), BF),
        ],
        scratch_shapes=[
            pltpu.VMEM((width, 2 * ff), BF),
            pltpu.VMEM((width, ff), BF),
            pltpu.VMEM((group, width), BF),
            pltpu.VMEM((group, width), BF),
            pltpu.VMEM((group, ff), F32),
            pltpu.VMEM((group, ff), BF),
            pltpu.VMEM((group, 2 * ff), BF),
            pltpu.VMEM((group, width), BF),
            pltpu.VMEM((2, TILE, 3 * ff), BF),
            pltpu.VMEM((width // 2 // TILE, TILE, 3 * ff), BF),
            pltpu.SemaphoreType.DMA((3,)),
            pltpu.SemaphoreType.DMA((2,)),
            pltpu.SemaphoreType.DMA((2,)),
            pltpu.SemaphoreType.DMA((width // 2 // TILE,)),
        ]
        + Gather.scratch(count)
        + Scatter.scratch(count, own, width, PIECES),
        compiler_params=pltpu.CompilerParams(
            collective_id=number, has_side_effects=True, vmem_limit_bytes=60 * 1024 * 1024
        ),
        cost_estimate=pl.CostEstimate(
            flops=WAIT_FLOPS, bytes_accessed=width * ff * 12, transcendentals=0
        ),
        name="feed_forward",
    )(normed_own, mlp_piece, out_down, cotangent)


def rows_of_core(block, number, by):
    per = block // TILE
    start = (number // per * 2 + by) * block + number % per * TILE
    return pl.ds(pl.multiple_of(start, TILE), TILE)


def attention_end(
    grad_heads, normed, small, weights, side, extras, post, sizes, number
):
    X, C, Z, Y = sizes
    group, total = grad_heads.shape
    width = normed.shape[1]
    own = group // Z
    near, skip = 2 * DK + DV, 2 * DK + 2 * DV
    wide = near + SMALL
    rows = width // (X * C * Y * Z)
    piece = Z * rows
    block = width // (C * X)
    kept = width // 2 // TILE
    others = X * Y - 1

    def body(*refs):
        gh_ref, normed_ref, small_ref = refs[:3]
        extra_refs = refs[3 : 3 + len(extras)]
        w_hbm, side_ref, out_ref, near_out, side_out = refs[3 + len(extras) : 8 + len(extras)]
        (w_ref, partial, given, received, sums, parts, final, load_sem, pair_send, pair_arrive,
         far_send, far_arrive) = refs[8 + len(extras) : 20 + len(extras)]
        sems = refs[20 + len(extras) :]
        x, core, me, y = (lax.axis_index(name) for name in OWN)
        scatter = Scatter("z", Z, PIECES, partial, out_ref, *sems[:4])
        near_swap = Swap("z", Z, final, near_out, *sems[4:7])
        side_swap = Swap("z", Z, side_ref, side_out, *sems[7:10])
        load = pltpu.make_async_copy(w_hbm, w_ref, load_sem)
        load.start()

        def across(offset, sign):
            down, right = offset // Y, offset % Y
            if sign < 0:
                down, right = X - down, Y - right
            return lax.rem(x + down, X), lax.rem(y + right, Y)

        peers = all_peers("z", Z) + [(True, {"c": 1 - core})]
        for offset in range(1, others + 1):
            to_x, to_y = across(offset, 1)
            peers.append((True, {"x": to_x, "y": to_y}))
        greet(peers)

        def backward(at_rows):
            for at in range(0, width, TILE):
                columns = pl.ds(at, TILE)
                partial[at_rows, columns] = dot_rows(gh_ref[at_rows], w_ref[columns]).astype(BF)

        def rows_at(index, size):
            return pl.ds(pl.multiple_of(index * size, size), size)

        lower = me < Z // 2
        load.wait()
        backward(rows_at(jnp.where(lower, Z - 1, 0), own))
        scatter.start([0])
        backward(rows_at(jnp.where(lower, Z // 2, Z // 2 - 1), own))
        scatter.start([1])
        backward(rows_at(me // (Z // 2), group // 2))
        scatter.start([2])

        def pass_over(i):
            return remote(
                given.at[i], received.at[i], pair_send.at[i], pair_arrive.at[i], "c", 1 - core
            )

        def products(i, by):
            at = rows_of_core(block, i, by)
            top = dot_cols(normed_ref[:, at], gh_ref[:, :near])
            low = dot_cols(normed_ref[:, at], gh_ref[:, skip:]) + small_ref[at]
            return top, low

        for i in range(kept):
            top, low = products(i, 1 - core)
            given[i, :, :near] = top.astype(BF)
            given[i, :, near:] = low.astype(BF)
            pass_over(i).start()
        for i in range(kept):
            top, low = products(i, core)
            pass_over(i).wait_recv()
            at = pl.ds(i * TILE, TILE)
            sums[at, :near] = (top + received[i, :, :near].astype(F32)).astype(BF)
            sums[at, near:] = (low + received[i, :, near:].astype(F32)).astype(BF)

        def far(offset, by=1):
            to_x, to_y = across(offset, by)
            return pltpu.make_async_remote_copy(
                src_ref=sums.at[rows_at(to_x * Y + to_y, piece)], dst_ref=parts.at[offset - 1],
                send_sem=far_send.at[offset - 1], recv_sem=far_arrive.at[offset - 1],
                device_id={"x": to_x, "y": to_y}, device_id_type=pl.DeviceIdType.MESH,
            )

        for offset in range(1, others + 1):
            far(offset).start()
        for step in range(Z - 2):
            scatter.run(step, False)
            scatter.run(step, True)
        side_swap.start()
        own_sum = sums[rows_at(x * Y + y, piece)].astype(F32)
        for offset in range(1, others + 1):
            far(offset).wait_recv()
            own_sum = own_sum + parts[offset - 1].astype(F32)
        for index in range(Z):
            final[index] = own_sum[index * rows : (index + 1) * rows].astype(BF)
        near_swap.start()
        scatter.run(Z - 2, False)
        scatter.run(Z - 2, True)
        scatter.finish()
        out_ref[...] = post(out_ref[...], *[r[...] for r in extra_refs])
        side_swap.finish()
        near_swap.finish()
        for offset in range(1, others + 1):
            far(offset).wait_send()
        for i in range(kept):
            pass_over(i).wait_send()

    in_vmem, anywhere = pl.BlockSpec(memory_space=pltpu.VMEM), pl.BlockSpec(memory_space=pl.ANY)
    return pl.pallas_call(
        body,
        in_specs=[in_vmem] * (3 + len(extras)) + [anywhere] * 2,
        out_specs=[in_vmem, anywhere, anywhere],
        out_shape=[
            jax.ShapeDtypeStruct((own, width), F32),
            jax.ShapeDtypeStruct((Z, rows, wide), BF),
            jax.ShapeDtypeStruct(side.shape, BF),
        ],
        scratch_shapes=[
            pltpu.VMEM((width, total), BF),
            pltpu.VMEM((group, width), BF),
            pltpu.VMEM((kept, TILE, wide), BF),
            pltpu.VMEM((kept, TILE, wide), BF),
            pltpu.VMEM((width // 2, wide), BF),
            pltpu.VMEM((max(others, 1), piece, wide), BF),
            pltpu.VMEM((Z, rows, wide), BF),
            pltpu.SemaphoreType.DMA,
            pltpu.SemaphoreType.DMA((kept,)),
            pltpu.SemaphoreType.DMA((kept,)),
            pltpu.SemaphoreType.DMA((max(others, 1),)),
            pltpu.SemaphoreType.DMA((max(others, 1),)),
        ]
        + Scatter.scratch(Z, own, width, PIECES)
        + Swap.scratch(Z)
        + Swap.scratch(Z),
        compiler_params=pltpu.CompilerParams(
            collective_id=number, has_side_effects=True, vmem_limit_bytes=56 * 1024 * 1024
        ),
        cost_estimate=pl.CostEstimate(
            flops=WAIT_FLOPS, bytes_accessed=width * total * 6, transcendentals=0
        ),
        name="attention_end",
    )(grad_heads, normed, small, *extras, weights, side)


def join(values, parts, weights=()):
    Z, rows = values[0].shape[:2]

    def body(*refs):
        ins, refs = refs[: len(values)], refs[len(values) :]
        w_refs, outs = refs[: len(weights)], refs[len(weights) :]
        moment = jnp.zeros((rows, 1), F32)
        for number, (out_ref, (index, start, size)) in enumerate(zip(outs, parts)):
            held = ins[index][0, :, start : start + size].astype(F32)
            out_ref[...] = held
            if number < len(weights):
                product = held * w_refs[number][...].astype(F32)
                moment = moment + jnp.sum(product, axis=1, keepdims=True)
        if weights:
            before = jnp.where(pl.program_id(0) == 0, 0.0, outs[-1][...])
            outs[-1][...] = before + moment

    return pl.pallas_call(
        body,
        grid=(Z,),
        in_specs=[pl.BlockSpec((1,) + v.shape[1:], lambda i: (i, 0, 0)) for v in values]
        + [pl.BlockSpec((rows, w.shape[1] // Z), lambda i: (0, i)) for w in weights],
        out_specs=[pl.BlockSpec((rows, part[2]), lambda i: (0, i)) for part in parts]
        + [pl.BlockSpec((rows, LANES), lambda i: (0, 0))] * (len(weights) > 0),
        out_shape=[jax.ShapeDtypeStruct((rows, Z * part[2]), F32) for part in parts]
        + [jax.ShapeDtypeStruct((rows, LANES), F32)] * (len(weights) > 0),
        compiler_params=pltpu.CompilerParams(dimension_semantics=("arbitrary",)),
        name="join",
    )(*values, *weights)


def local(
    tokens, doc_lengths, cotangent, attn_gain, query_weight, key_weight, value_weight, gate_weight,
    rank_in, rank_out, decay_bias, head_gain, out_weight, mlp_gain, mlp_gate_weight,
    mlp_up_weight, down_weight,
):
    own, width = tokens.shape
    rows = query_weight.shape[0]
    X, C, Z, Y = (lax.axis_size(name) for name in OWN)
    z = lax.axis_index("z")
    group = own * Z
    total = group * Y
    ff = down_weight.shape[1] // Z
    dvp = DV // Y

    def blocked(value):
        lead = value.shape[:-1]
        cut = value.reshape(lead + (X, C, Z, Y, rows))
        return jnp.swapaxes(cut, -3, -2).reshape(lead + (width,))

    def straight(value):
        found = []
        for start in range(0, width, Z * Y * rows):
            for at_z in range(Z):
                for at_y in range(Y):
                    first_lane = start + (at_y * Z + at_z) * rows
                    found.append(value[:, first_lane : first_lane + rows])
        return jnp.concatenate(found, axis=1)

    def pad_rows(value):
        flat = value.reshape(value.shape[0], -1)
        return jnp.pad(flat, ((0, rows - flat.shape[0]), (0, 0)))

    numbers = iter(range(32))

    def deal(value, forth):
        return move(next(numbers), deals=[(value, "y", forth)])[0]

    def after(value, *others):
        return lax.optimization_barrier((value,) + others)[0]

    def scatter_rest(value, axes=REST):
        sums = lax.psum_scatter(value, axes, scatter_dimension=0, tiled=True)
        return sums.reshape(Z, rows, -1)

    def gather_rest(value, axes=REST):
        return lax.all_gather(value.reshape(Z * rows, -1), axes, axis=0, tiled=True)

    small = jnp.concatenate(
        [
            rank_in, pad_rows(attn_gain), pad_rows(mlp_gain), pad_rows(rank_out),
            pad_rows(decay_bias), pad_rows(head_gain),
        ],
        axis=1,
    )
    small = jnp.pad(small, ((0, 0), (0, SMALL - small.shape[1])))
    own_tokens = blocked(tokens)
    input_weights, group_tokens, out_weights = spread_and_gather(
        [query_weight, key_weight, value_weight, gate_weight, small],
        own_tokens, [out_weight, down_weight], (X, C, Z, Y), next(numbers),
    )
    input_weights = input_weights.reshape(width, -1)

    projected = 2 * DK + 2 * DV
    near = 2 * DK + DV
    small_all = input_weights[:, projected:].astype(F32)

    def device_rows(value, count):
        cut = value.reshape(X, C, Y, Z, rows, -1)[:, :, :, :, : rows // count]
        return jnp.swapaxes(cut, 2, 3).reshape(width // count, -1)

    attn_gain_all = small_all[:, R]
    mlp_gain_all = small_all[:, R + 1]
    rank_out_all = device_rows(small_all[:, R + 2 : 2 * R + 2], width // (H * DK))
    bias_all = device_rows(small_all[:, 2 * R + 2 : 2 * R + 3], width // (H * DK))
    head_gain_all = device_rows(small_all[:, 2 * R + 3 : 2 * R + 4], width // DV)[:, 0]
    rank_out_z = lax.dynamic_slice_in_dim(rank_out_all, z * DK, DK).astype(BF)
    bias_z = lax.dynamic_slice_in_dim(bias_all, z * DK, DK)[:, 0]

    def to_device_rows(value, count):
        cut = value.reshape(X, C, Z, Y, rows // count, -1)
        cut = jnp.swapaxes(cut, 2, 3)
        cut = jnp.pad(cut, ((0, 0),) * 4 + ((0, rows - rows // count), (0, 0)))
        return cut.reshape(width, -1)

    def at_head(value):
        return lax.dynamic_update_slice_in_dim(
            jnp.zeros((H * DK, value.shape[1]), F32), value, z * DK, 0
        )

    rows_in = group_tokens.astype(F32)
    scale_in = lax.rsqrt(jnp.mean(rows_in * rows_in, axis=1, keepdims=True) + norm_eps)
    normed_in = (rows_in * scale_in * attn_gain_all).astype(BF)
    heads = dot_plain(normed_in, input_weights)
    out_gate = heads[:, 2 * DK + DV : projected]
    low = heads.astype(BF)
    rank_beside_one = jnp.concatenate(
        [
            jnp.zeros((group, RANK_AT), BF), low[:, projected : projected + R],
            jnp.ones((group, 1), BF), jnp.zeros((group, SMALL - RANK_AT - R - 1), BF),
        ],
        axis=1,
    )
    shared = jnp.concatenate([low[:, : 2 * DK], low[:, projected:]], axis=1)
    values = jnp.swapaxes(low[:, 2 * DK : 2 * DK + DV].reshape(group, Y, dvp), 0, 1)
    sent = jnp.concatenate([jnp.broadcast_to(shared[None], (Y,) + shared.shape), values], axis=2)
    mlp_weights, sequence = move(
        next(numbers), cuts=[([mlp_gate_weight, mlp_up_weight], "z")],
        deals=[(sent.reshape(Y, Z, own, -1), "y", True)],
    )
    out_down = gather_rest(out_weights)
    out_piece = out_down[:, :DV]
    mlp_piece = gather_rest(mlp_weights)
    sequence = sequence.reshape(total, -1)
    queries = sequence[:, :DK]
    keys = sequence[:, DK : 2 * DK]
    rank_low = sequence[:, 2 * DK : 2 * DK + R]
    value_part = sequence[:, 2 * DK + SMALL :]
    decay_logit = dot_rows(rank_low, rank_out_z) + bias_z
    log_decay = jax.nn.log_sigmoid(decay_logit) / decay_norm

    doc_ends = jnp.cumsum(doc_lengths[0])
    positions = lax.iota(jnp.int32, total)
    segments = jnp.sum((doc_ends[None, :] <= positions[:, None]).astype(jnp.int32), axis=1)
    cut = segments.reshape(-1, CHUNK)
    last = cut[:, CHUNK - 1 :]
    before = jnp.concatenate([jnp.full((1, 1), -1, jnp.int32), last[:-1]], axis=0)
    aux = jnp.stack(
        [cut == before, cut == last, cut, jnp.broadcast_to(last == before, cut.shape)], axis=-1
    )
    aux = aux.reshape(total, 4).astype(F32)
    seg_rows = cut.astype(F32)[:, None, :]

    mixed_part, enter, scores = mix_forward(queries, keys, value_part, log_decay, aux, seg_rows)
    mixed_part = deal(mixed_part.reshape(Z, Y, own, dvp), False).reshape(Y, group, dvp)
    mixed = jnp.swapaxes(mixed_part, 0, 1).reshape(group, DV).astype(F32)

    head_scale = lax.rsqrt(jnp.mean(mixed * mixed, axis=1, keepdims=True) + head_eps)
    head_hat = mixed * head_scale
    head_out = head_hat * head_gain_all
    sig_out = jax.nn.sigmoid(out_gate)
    silu_out = out_gate * sig_out
    gated = (head_out * silu_out).astype(BF)
    own_cotangent = blocked(cotangent)
    residual, group_cotangent = move(
        next(numbers), scatter=(dot_rows(gated, out_piece).astype(BF), "z"),
        gathers=[(own_cotangent, "z")], extras=[own_tokens],
        post=lambda total_sum, x: total_sum + x.astype(F32),
    )
    scale_mid = lax.rsqrt(jnp.mean(residual * residual, axis=1, keepdims=True) + norm_eps)
    hat_mid = residual * scale_mid
    normed_mlp = (hat_mid * mlp_gain_all).astype(BF)
    grad_normed_mlp, out_partial, mlp_partial = feed_forward(
        normed_mlp, mlp_piece, out_down, group_cotangent, next(numbers)
    )
    mlp_sums = scatter_rest(mlp_partial, ("x", "y"))

    scaled = grad_normed_mlp * mlp_gain_all
    grad_residual = own_cotangent.astype(F32) + scale_mid * (
        scaled - hat_mid * jnp.mean(scaled * hat_mid, axis=1, keepdims=True)
    )
    branch_own = grad_residual.astype(BF)
    layer_out, grad_branch = move(
        next(numbers), scatter=(out_partial, "z"), gathers=[(branch_own, "z")],
        extras=[residual], post=lambda total_sum, rest: straight(total_sum + rest),
    )
    grad_gated = dot_plain(grad_branch, out_piece)
    grad_head = grad_gated * silu_out
    head_gain_part = jnp.sum(grad_head * head_hat, axis=0)
    head_small = jnp.pad(
        to_device_rows(head_gain_part[:, None], width // DV), ((0, 0), (HEAD_AT, SMALL - HEAD_AT - 1))
    )
    from_head = grad_head * head_gain_all
    grad_mixed = head_scale * (
        from_head - head_hat * jnp.mean(from_head * head_hat, axis=1, keepdims=True)
    )
    grad_out_gate = (grad_gated * head_out * sig_out * (1.0 + out_gate * (1.0 - sig_out))).astype(BF)
    grad_cut = jnp.swapaxes(grad_mixed.astype(BF).reshape(group, Y, dvp), 0, 1)
    grad_part = deal(grad_cut.reshape(Y, Z, own, dvp), True).reshape(total, dvp)
    dq, dk, dv, dld = mix_backward(
        queries, keys, value_part, log_decay, aux, seg_rows, enter, scores, grad_part
    )
    dlogit = (dld * jax.nn.sigmoid(-decay_logit) / decay_norm).astype(BF)
    back = jnp.concatenate([dq, dk, dlogit, dv], axis=1).reshape(Z, Y, own, -1)
    side_partial = jnp.concatenate(
        [dot_cols(normed_in, grad_out_gate), dot_cols(grad_branch, gated)], axis=1
    ).astype(BF)
    back, side_partial = lax.optimization_barrier((back, side_partial))
    side_sums = scatter_rest(after(side_partial, mlp_sums))
    mlp_rows, back = move(
        next(numbers), swaps=[(mlp_sums, "z")], deals=[(back, "y", False)]
    )
    back = back.reshape(Y, group, -1)
    summed = jnp.sum(back[:, :, : 3 * DK].astype(F32), axis=0).astype(BF)
    grad_value = jnp.swapaxes(back[:, :, 3 * DK :], 0, 1).reshape(group, DV)
    grad_logit = summed[:, 2 * DK :]
    rank_out_part = dot_cols(grad_logit, rank_beside_one)
    grad_rank = dot_plain(grad_logit, rank_out_z).astype(BF)
    grad_heads = jnp.concatenate(
        [
            summed[:, : 2 * DK], grad_value, grad_out_gate,
            jnp.pad(grad_rank, ((0, 0), (0, SMALL - R))),
        ],
        axis=1,
    )
    small_part = to_device_rows(at_head(rank_out_part), width // (H * DK)) + head_small

    def finish_tokens(back_sum, x, grad_res, gain):
        held = x.astype(F32)
        scale = lax.rsqrt(jnp.mean(held * held, axis=1, keepdims=True) + norm_eps)
        hat = held * scale
        scaled = back_sum * gain
        mean = jnp.mean(scaled * hat, axis=1, keepdims=True)
        return straight(grad_res + scale * (scaled - hat * mean))

    tokens_grad, near_rows, side_rows = attention_end(
        grad_heads, normed_in, small_part, input_weights, side_sums,
        [own_tokens, grad_residual, attn_gain_all[None]], finish_tokens, (X, C, Z, Y),
        next(numbers),
    )
    *mlp_grads, mlp_moments = join(
        [mlp_rows], [(0, 0, ff), (0, ff, ff), (0, 2 * ff, ff)], [mlp_gate_weight, mlp_up_weight]
    )
    query_grad, key_grad, value_grad, gate_grad, out_grad, moments = join(
        [near_rows, side_rows],
        [
            (0, 0, DK), (0, DK, DK), (0, 2 * DK, DV), (1, 0, DV), (1, DV, DV),
        ],
        [query_weight, key_weight, value_weight, gate_weight],
    )
    small_rows = jnp.sum(near_rows[:, :, near : near + SMALL].astype(F32), axis=0)
    rank_in_grad = small_rows[:, :R]
    moment = moments[:, 0] + jnp.sum(rank_in_grad * rank_in.astype(F32), axis=1)
    return (
        layer_out,
        tokens_grad,
        moment / attn_gain.astype(F32),
        query_grad,
        key_grad,
        value_grad,
        gate_grad,
        rank_in_grad,
        small_rows[: rows * H * DK // width, RANK_AT : RANK_AT + R],
        small_rows[: rows * H * DK // width, RANK_AT + R],
        small_rows[: rows * DV // width, HEAD_AT],
        out_grad,
        mlp_moments[:, 0] / mlp_gain.astype(F32),
        *mlp_grads,
    )


def solution(mesh):
    groups, places = mesh.shape["grp"], mesh.shape["seq"]
    wide = Mesh(mesh.devices.reshape(groups // 2, 2, H, places // H), OWN)
    split = P(OWN, None)
    line = P(OWN)
    by_sequence = P(("x", "c"), None)
    placed = (
        split, by_sequence, split, line, split, split, split, split, split, split,
        line, line, split, line, split, split, split,
    )
    return jax.shard_map(
        local,
        mesh=wide,
        in_specs=placed,
        out_specs=(
            split, split, line, split, split, split, split, split, split, line, line, split,
            line, split, split, split,
        ),
        check_vma=False,
    )
```
